32 devices in a mesh: dp: 8 (over y, x, core), tp: 4 (over z).
Axes of the slice: x: 2, y: 2, z: 4, core: 2. Of those that a mesh axis runs over, the one named last changes fastest.
Arguments:
- tokens: bfloat16 [16384, 2048], P(('dp', 'tp')), may hold values from -6 to 6
- cotangent: bfloat16 [16384, 2048], P(('dp', 'tp')), may hold values from -6 to 6
- segments: int32 [16, 1024], P('dp'), may hold values from 0 to 3, never falling along the last dimension, each value on 1 to 512 neighbouring positions
- subsets: int32 [16, 4], P('dp'), may hold values from 0 to 21
- packs: int32 [8], P('dp'), may hold values from 1 to 2, as said below
- master_blocks: float32 [768, 256, 256], P(('dp', 'tp'))
- left_stats: float32 [768, 256, 256], P(('dp', 'tp'))
- right_stats: float32 [768, 256, 256], P(('dp', 'tp'))
- local_vecs: float32 [56, 256], P('tp', 'dp'), may hold values from -1.2 to 1.2
- local_vec_stats: float32 [56, 256], P('tp', 'dp')
- shared_vecs: float32 [6, 2048], P(None, ('dp', 'tp'))
- shared_vec_stats: float32 [6, 2048], P(None, ('dp', 'tp'))
Outputs:
- output: bfloat16 [16384, 2048], P(('dp', 'tp'))
- input_grad: float32 [16384, 2048], P(('dp', 'tp'))
- block_grads: float32 [768, 256, 256], P(('dp', 'tp'))
- left_new: float32 [768, 256, 256], P(('dp', 'tp'))
- right_new: float32 [768, 256, 256], P(('dp', 'tp'))
- new_blocks: float32 [768, 256, 256], P(('dp', 'tp'))
- local_vec_grads: float32 [56, 256], P('tp', 'dp')
- local_vec_stats_new: float32 [56, 256], P('tp', 'dp')
- local_vecs_new: float32 [56, 256], P('tp', 'dp')
- shared_vec_grads: float32 [6, 2048], P(None, ('dp', 'tp'))
- shared_vec_stats_new: float32 [6, 2048], P(None, ('dp', 'tp'))
- shared_vecs_new: float32 [6, 2048], P(None, ('dp', 'tp'))
The draws below stay inside these ranges and needn't reach their ends.
Inputs may be any that keep to these rules, and one draw needn't show every extreme that they name: Each data group holds 1 to 2 packs in its first slots; some group holds 2 and some holds 1. `segments`: document numbers never fall along a pack; each of the 4 documents has 1 to 512 tokens, one exactly 512.
All inputs are finite; a program needn't handle non-finite values.
Results may differ from the reference program's by a relative error of at most 0.011.
Values may be sent and summed in bfloat16 or wider, within the bound.
No kernel may reach another device: no remote copies, remote signals or barrier semaphores. Data moves between devices by JAX's collectives and lax.ppermute only.
A program may use at most 320 MiB of HBM per device.

```python
import math
import jax
import jax.numpy as jnp
import numpy as np
from jax import lax

D = 2048
HEADS = 8
HD = 256
ROT = 64
FF = 8192
PACK_LEN = 1024
PACKS = 2
SEGS = 4
SUBSETS = 22
BLK = 256
ROOT_ITERS = 8
GROUPS = 8
TOKENS = 16384
PACKS_ALL = 16
HPD = 2
FF_DEV = 2048
NBLK = 768
NB_DEV = 24
VEC_ROWS = 56
N_DP = 8
N_TP = 4


def block_kind(block_total):
    tp_ways = HEADS // HPD
    block_index = jnp.arange(block_total)
    within = block_index % NB_DEV
    owner_idx = block_index // (NB_DEV * tp_ways)
    local_idx = owner_idx * NB_DEV + within
    block_rows = D // BLK
    first_end = block_rows * (3 * HPD * HD // BLK)
    second_end = first_end + HPD * HD // BLK * block_rows
    third_end = second_end + block_rows * (FF_DEV // BLK)
    return (local_idx >= first_end).astype(jnp.int32) + (local_idx >= second_end).astype(jnp.int32) + (local_idx >= third_end).astype(jnp.int32)


def grad_square():
    return GROUPS * PACK_LEN * (PACKS + 1) / 2.0


def draw_packs(key, part):
    key_one = jax.random.fold_in(key, 101)
    key_two = jax.random.fold_in(key, 102)
    key_three = jax.random.fold_in(key, 103)
    counts = jax.random.randint(key_one, (GROUPS,), 1, PACKS + 1)
    full_idx = jax.random.randint(key_two, (), 0, GROUPS)
    single_idx = (full_idx + 1 + jax.random.randint(key_three, (), 0, GROUPS - 1)) % GROUPS
    positions = jnp.arange(GROUPS)
    counts = jnp.where(positions == full_idx, PACKS, jnp.where(positions == single_idx, 1, counts))
    return counts.astype(jnp.int32)


def draw_master_blocks(key, part):
    block_kinds = block_kind(NBLK)
    spreads = jnp.array([D ** (-0.5), 4.0 * D ** (-0.5), D ** (-0.5), FF ** (-0.5)], jnp.float32)
    normal_noise = jax.random.normal(jax.random.fold_in(key, 201), (NBLK, BLK, BLK), jnp.float32)
    return normal_noise * spreads[block_kinds][:, None, None]


def diagonal_stats(key):
    block_kinds = block_kind(NBLK)
    factors = jnp.array([2.0, 0.2, 0.3, 0.6], jnp.float32)
    stat_level = BLK * grad_square() * factors[block_kinds] ** 2
    diag_vals = jax.random.uniform(key, (NBLK, BLK), jnp.float32, 1.0, 4.0) * stat_level[:, None]
    identity = (jnp.arange(BLK)[:, None] == jnp.arange(BLK)[None, :]).astype(jnp.float32)
    return identity[None, :, :] * diag_vals[:, :, None]


def draw_left_stats(key, part):
    return diagonal_stats(jax.random.fold_in(key, 301))


def draw_right_stats(key, part):
    return diagonal_stats(jax.random.fold_in(key, 302))


def draw_local_vec_stats(key, part):
    rows_per_group = VEC_ROWS // (HEADS // HPD)
    feed_rows = jnp.arange(VEC_ROWS) % rows_per_group >= 3 * HPD
    factor = jnp.where(feed_rows, 0.3, 2.0)
    stat_level = grad_square() * factor * factor
    return jax.random.uniform(jax.random.fold_in(key, 401), (VEC_ROWS, HD), jnp.float32, 1.0, 4.0) * stat_level[:, None]


def draw_shared_vecs(key, part):
    normal_noise = jax.random.normal(jax.random.fold_in(key, 501), (6, D), jnp.float32)
    row_ids = jnp.arange(6)
    gain_rows = (row_ids == 0) | (row_ids == 2)
    return jnp.where(gain_rows[:, None], 1.0 + 0.1 * normal_noise, 0.2 * normal_noise)


def draw_shared_vec_stats(key, part):
    factors = jnp.array([3.5, 3.5, 0.6, 0.6, 1.0, 1.0], jnp.float32)
    stat_level = grad_square() * factors * factors
    return jax.random.uniform(jax.random.fold_in(key, 601), (6, D), jnp.float32, 1.0, 4.0) * stat_level[:, None]


def with_ends(values, own_key, least, largest):
    shape = values.shape
    index_at = [jax.random.randint(jax.random.fold_in(own_key, axis), (), 0, shape[axis]) for axis in range(len(shape))]
    values = values.at[tuple(index_at)].set(least)
    longest = shape.index(max(shape))
    index_at[longest] = (index_at[longest] + 1) % shape[longest]
    return values.at[tuple(index_at)].set(largest)


def shard_levels(key, extent, split, least, largest):
    level, own = 1.0, jax.random.fold_in(key, 6)
    for position, parts in split:
        steps = jnp.exp(jax.random.uniform(jax.random.fold_in(own, position), (parts,), jnp.float32, least / len(split), largest / len(split)))
        level = level * jnp.repeat(steps, extent[position] // parts).reshape([-1 if axis == position else 1 for axis in range(len(extent))])
    return level


def rank_bounds(amount, lean):
    weights = [(1 << 20) // math.isqrt(grade ** lean) + 1 for grade in range(1, amount + 1)]
    spread = 1 + sum(weights) // (1 << 30)
    return np.cumsum(np.array([max(1, weight // spread) for weight in weights]))


def ranked(stream_key, extent, number_of, slope):
    grid = rank_bounds(number_of, slope)
    lot = jax.random.randint(jax.random.fold_in(stream_key, 1), extent, 0, int(grid[number_of - 1]))
    grade = jnp.searchsorted(jnp.asarray(grid, jnp.int32), lot, side="right")
    return jax.random.permutation(jax.random.fold_in(stream_key, 2), number_of)[grade].astype(jnp.int32)


def profile(count, total, most, slope):
    weights = [(1 << 20) // math.isqrt(standing ** slope) + 1 for standing in range(2, count + 1)]
    rest, holding = total - most - (count - 1), [1] * (count - 1)
    while rest > 0:
        candidates = [i for i in range(count - 1) if holding[i] < most]
        whole, remaining = sum([weights[i] for i in candidates]), rest
        for i in candidates:
            addition = min(most - holding[i], max(1, remaining * weights[i] // whole), rest)
            holding[i] = holding[i] + addition
            rest = rest - addition
    return np.array([most] + holding)


def ragged(own_key, amount, total, reach, slope):
    if amount == 2:
        one = jax.random.randint(own_key, (), max(1, total - reach), min(reach, total - 1) + 1)
        return jnp.stack([one, total - one])
    tallies = jnp.asarray(profile(amount, total, reach, slope), jnp.int32)
    pairs = (amount - 1) // 2
    donor, taker = tallies[1:1 + 2 * pairs:2], tallies[2:2 + 2 * pairs:2]
    slack = jnp.minimum(donor - 1, reach - taker)
    moved = jax.random.randint(jax.random.fold_in(own_key, 1), (pairs,), 0, 1 << 20) % (slack + 1)
    tallies = tallies.at[1:1 + 2 * pairs:2].set(donor - moved).at[2:2 + 2 * pairs:2].set(taker + moved)
    return tallies[jax.random.permutation(jax.random.fold_in(own_key, 2), amount)]


def noise(stream_key, extent, deviation, reach, cuts=(), kind=jnp.bfloat16):
    entries = deviation * jax.random.normal(stream_key, extent, jnp.float32)
    if cuts:
        entries = entries * shard_levels(stream_key, extent, cuts, -0.22, 0.18)
    return jnp.clip(entries, -reach, reach).astype(kind)


def setup_inputs(seed: int = 0) -> dict:
    streams_of = jax.random.split(jax.random.key(seed), 13)
    tokens = noise(streams_of[0], (TOKENS, D), 1.0, 6.0, ((0, 32),))
    cotangent = noise(streams_of[1], (TOKENS, D), 1.0, 6.0, ((0, 32),))
    segments = jax.vmap(lambda own: jnp.searchsorted(jnp.cumsum(ragged(own, SEGS, PACK_LEN, PACK_LEN // 2, 2)), jnp.arange(PACK_LEN), side="right"))(jax.random.split(streams_of[2], PACKS_ALL)).reshape((PACKS_ALL, PACK_LEN)).astype(jnp.int32)
    subsets = with_ends(ranked(streams_of[3], (PACKS_ALL, SEGS), SUBSETS, 2), jax.random.fold_in(streams_of[3], 3), 0, SUBSETS - 1).astype(jnp.int32)
    packs = draw_packs(jax.random.fold_in(streams_of[12], 71), 0)
    master_blocks = draw_master_blocks(jax.random.fold_in(streams_of[12], 71), 0)
    left_stats = draw_left_stats(jax.random.fold_in(streams_of[12], 71), 0)
    right_stats = draw_right_stats(jax.random.fold_in(streams_of[12], 71), 0)
    local_vecs = noise(streams_of[8], (VEC_ROWS, HD), 0.2, 1.2, ((0, 4), (1, 8)), jnp.float32)
    local_vec_stats = draw_local_vec_stats(jax.random.fold_in(streams_of[12], 71), 0)
    shared_vecs = draw_shared_vecs(jax.random.fold_in(streams_of[12], 71), 0)
    shared_vec_stats = draw_shared_vec_stats(jax.random.fold_in(streams_of[12], 71), 0)
    return dict(tokens=tokens, cotangent=cotangent, segments=segments, subsets=subsets, packs=packs, master_blocks=master_blocks, left_stats=left_stats, right_stats=right_stats, local_vecs=local_vecs, local_vec_stats=local_vec_stats, shared_vecs=shared_vecs, shared_vec_stats=shared_vec_stats)


EPS_NORM = 1e-05
DECAY = 0.5
RATE_BLOCK = 0.6
RATE_VEC = 0.2
NEG_FILL = -1e+30
HIGHEST = lax.Precision.HIGHEST

@jax.custom_vjp
def reduced_precision(v):
    return lax.optimization_barrier(v.astype(jnp.bfloat16)).astype(jnp.float32)

@jax.custom_vjp
def low_back(v):
    return v

def low_keep(v):
    return (reduced_precision(v), None)

def low_pass(kept, grad):
    return (grad,)

def back_keep(v):
    return (v, None)

def back_low(kept, grad):
    return (reduced_precision(grad),)
reduced_precision.defvjp(low_keep, low_pass)
low_back.defvjp(back_keep, back_low)

def product(left_arg, right_arg):
    return jnp.dot(left_arg, right_arg, precision=HIGHEST, preferred_element_type=jnp.float32)

def apply_layer_norm(values):
    mean_val = lax.optimization_barrier(jnp.mean(values, axis=-1, keepdims=True))
    centred = values - mean_val
    variance = lax.optimization_barrier(jnp.mean(centred * centred, axis=-1, keepdims=True))
    inv_std = lax.rsqrt(variance + EPS_NORM)
    return (centred * inv_std, inv_std)

def rotary_tables(row_count, pack_len, rot_dims):
    positions = (jnp.arange(row_count) % pack_len).astype(jnp.float32)
    freqs = 10000.0 ** (-(jnp.arange(rot_dims // 2).astype(jnp.float32) * 2.0) / rot_dims)
    angles = positions[:, None] * freqs[None, :]
    cosines = jnp.cos(angles)
    sines = jnp.sin(angles)
    return (jnp.concatenate([cosines, cosines], -1), jnp.concatenate([sines, sines], -1))

def rotate(values, cosines, sines):
    rot_dims = cosines.shape[-1]
    half_dims = rot_dims // 2
    rotated = values[..., :rot_dims]
    turned = jnp.concatenate([-rotated[..., half_dims:], rotated[..., :half_dims]], -1)
    return jnp.concatenate([rotated * cosines[:, None, :] + turned * sines[:, None, :], values[..., rot_dims:]], -1)

def inverse_fourth_root(matrices):
    order_size = matrices.shape[-1]
    identity = jnp.eye(order_size, dtype=matrices.dtype)
    frob_norms = jnp.sqrt(lax.optimization_barrier(jnp.sum(matrices * matrices, axis=(1, 2))))
    scaled = matrices / frob_norms[:, None, None]
    root_now = jnp.broadcast_to(identity, matrices.shape)
    for repeat in range(ROOT_ITERS):
        factor = (5.0 * identity - scaled) * 0.25
        root_now = jnp.matmul(root_now, factor, precision=HIGHEST)
        square = jnp.matmul(factor, factor, precision=HIGHEST)
        scaled = jnp.matmul(jnp.matmul(square, square, precision=HIGHEST), scaled, precision=HIGHEST)
    return root_now * lax.rsqrt(jnp.sqrt(frob_norms))[:, None, None]

def order_table():
    per_group = NBLK // N_TP
    local_idx = np.arange(per_group)
    group_idx = np.arange(N_TP)
    return (((local_idx // NB_DEV)[None, :] * N_TP + group_idx[:, None]) * NB_DEV + (local_idx % NB_DEV)[None, :]).astype(np.int32)

def assemble(blocks_arg):
    local_blocks = blocks_arg[jnp.asarray(order_table())]
    block_rows = D // BLK
    qkv_cols = 3 * HPD * HD // BLK
    head_rows = HPD * HD // BLK
    ff_blocks = FF_DEV // BLK
    first_end = block_rows * qkv_cols
    second_end = first_end + head_rows * block_rows
    third_end = second_end + block_rows * ff_blocks
    w_qkv = local_blocks[:, :first_end].reshape(N_TP, block_rows, qkv_cols, BLK, BLK).transpose(1, 3, 0, 2, 4).reshape(D, 3 * D)
    w_out = local_blocks[:, first_end:second_end].reshape(N_TP, head_rows, block_rows, BLK, BLK).transpose(0, 1, 3, 2, 4).reshape(D, D)
    w_in = local_blocks[:, second_end:third_end].reshape(N_TP, block_rows, ff_blocks, BLK, BLK).transpose(1, 3, 0, 2, 4).reshape(D, FF)
    w_down = local_blocks[:, third_end:].reshape(N_TP, ff_blocks, block_rows, BLK, BLK).transpose(0, 1, 3, 2, 4).reshape(FF, D)
    return (w_qkv, w_out, w_in, w_down)

def attend(query_all, key_all, value_all, seg_group):
    query_rows = min(512, PACK_LEN)
    block_count = PACK_LEN // query_rows
    score_scale = 1.0 / math.sqrt(HD)

    @jax.checkpoint
    def one_block(block_num):
        pack_start = block_num // block_count * PACK_LEN
        row_start = block_num % block_count * query_rows
        query_block = lax.dynamic_slice_in_dim(query_all, pack_start + row_start, query_rows, 0)
        key_pack = lax.dynamic_slice_in_dim(key_all, pack_start, PACK_LEN, 0)
        value_pack = lax.dynamic_slice_in_dim(value_all, pack_start, PACK_LEN, 0)
        seg_keys = lax.dynamic_slice_in_dim(seg_group, pack_start, PACK_LEN, 0)
        seg_query = lax.dynamic_slice_in_dim(seg_keys, row_start, query_rows, 0)
        query_pos = row_start + jnp.arange(query_rows)
        key_pos = jnp.arange(PACK_LEN)
        allowed = (key_pos[None, :] <= query_pos[:, None]) & (seg_query[:, None] == seg_keys[None, :])
        scores = low_back(jnp.einsum('qhd,khd->hqk', query_block, key_pack, precision=HIGHEST) * score_scale)
        masked = jnp.where(allowed[None], scores, NEG_FILL)
        row_max = lax.optimization_barrier(jnp.max(masked, axis=-1, keepdims=True))
        exp_terms = jnp.exp(masked - row_max)
        attn_probs = exp_terms / lax.optimization_barrier(jnp.sum(exp_terms, axis=-1, keepdims=True))
        return jnp.einsum('hqk,khd->qhd', reduced_precision(attn_probs), value_pack, precision=HIGHEST)
    blocks_out = lax.map(one_block, jnp.arange(PACKS * block_count, dtype=jnp.int32))
    return blocks_out.reshape(PACKS * PACK_LEN, HEADS, HD)

def forward(blocks_arg, local_arg, shared_arg, input_argument, seg_group, valid_mask):
    group_tok = PACKS * PACK_LEN
    w_qkv, w_out, w_in, w_down = assemble(reduced_precision(blocks_arg))
    local_rows = reduced_precision(local_arg).reshape(N_TP, VEC_ROWS // N_TP, HD)
    bias_qkv = local_rows[:, :3 * HPD].reshape(3 * D)
    bias_in = local_rows[:, 3 * HPD:].reshape(FF)
    shared_reduced_precision = reduced_precision(shared_arg)
    centred_scaled_input, ignored_deviation = apply_layer_norm(input_argument)
    first_normed_input = reduced_precision(centred_scaled_input * shared_reduced_precision[0] + shared_reduced_precision[1])
    second_normed_input = reduced_precision(centred_scaled_input * shared_reduced_precision[2] + shared_reduced_precision[3])
    qkv_vals = low_back(product(first_normed_input, w_qkv) + bias_qkv).reshape(group_tok, HEADS, 3, HD)
    cosines, sines = rotary_tables(group_tok, PACK_LEN, ROT)
    query_all = reduced_precision(rotate(qkv_vals[:, :, 0], cosines, sines))
    key_all = reduced_precision(rotate(qkv_vals[:, :, 1], cosines, sines))
    value_all = reduced_precision(qkv_vals[:, :, 2])
    attended = reduced_precision(low_back(attend(query_all, key_all, value_all, seg_group)))
    hidden = low_back(product(second_normed_input, w_in) + bias_in)
    activated = reduced_precision(jax.nn.gelu(hidden, approximate=False))
    summed = input_argument + product(attended.reshape(group_tok, D), w_out) + product(activated, w_down) + shared_reduced_precision[4] + shared_reduced_precision[5]
    return summed * valid_mask[:, None]

def reference(tokens, cotangent, segments, subsets, packs, master_blocks, left_stats, right_stats, local_vecs, local_vec_stats, shared_vecs, shared_vec_stats):
    group_tok = PACKS * PACK_LEN
    tok_groups = tokens.astype(jnp.float32).reshape(N_DP, group_tok, D)
    cot_groups = cotangent.astype(jnp.float32).reshape(N_DP, group_tok, D)
    seg_groups = segments.reshape(N_DP, group_tok)
    sub_groups = subsets.reshape(N_DP, PACKS, SEGS)
    tok_pack = (jnp.arange(group_tok) // PACK_LEN).astype(jnp.int32)

    def one_group(carry, inputs):
        input_group, cot_group, seg_group, sub_group, pack_total = inputs
        valid_mask = (tok_pack < pack_total).astype(jnp.float32)
        subset_tok = sub_group[tok_pack, seg_group]
        weight = 0.5 + subset_tok.astype(jnp.float32) / (SUBSETS - 1)
        seed_grad = reduced_precision(cot_group * weight[:, None] * valid_mask[:, None])

        def forward_group(blocks_arg, local_arg, shared_arg, input_argument):
            return forward(blocks_arg, local_arg, shared_arg, input_argument, seg_group, valid_mask)
        result, pullback = jax.vjp(forward_group, master_blocks, local_vecs, shared_vecs, input_group)
        grad_blocks, grad_local, grad_shared, grad_input = pullback(seed_grad)
        carry = (carry[0] + grad_blocks, carry[1] + grad_local, carry[2] + grad_shared)
        return (carry, (result.astype(jnp.bfloat16), grad_input))
    init = (jnp.zeros(master_blocks.shape, jnp.float32), jnp.zeros(local_vecs.shape, jnp.float32), jnp.zeros(shared_vecs.shape, jnp.float32))
    (block_grads, local_grads, shared_grads), (outs, input_grads) = lax.scan(one_group, init, (tok_groups, cot_groups, seg_groups, sub_groups, packs))
    left_new = DECAY * left_stats + jnp.einsum('nij,nkj->nik', block_grads, block_grads, precision=HIGHEST)
    right_new = DECAY * right_stats + jnp.einsum('nji,njk->nik', block_grads, block_grads, precision=HIGHEST)
    root_left = inverse_fourth_root(left_new)
    root_right = inverse_fourth_root(right_new)
    precond = jnp.matmul(jnp.matmul(root_left, block_grads, precision=HIGHEST), root_right, precision=HIGHEST)
    new_blocks = master_blocks - RATE_BLOCK * precond
    local_stat_new = DECAY * local_vec_stats + local_grads * local_grads
    local_new = local_vecs - RATE_VEC * local_grads * lax.rsqrt(local_stat_new)
    shared_stat_new = DECAY * shared_vec_stats + shared_grads * shared_grads
    shared_new = shared_vecs - RATE_VEC * shared_grads * lax.rsqrt(shared_stat_new)
    return (outs.reshape(N_DP * group_tok, D), input_grads.reshape(N_DP * group_tok, D), block_grads, left_new, right_new, new_blocks, local_grads, local_stat_new, local_new, shared_grads, shared_stat_new, shared_new)
```

```python
import functools
import math

import jax
import jax.numpy as jnp
from jax import lax
from jax.experimental import pallas as pl
from jax.experimental.pallas import tpu as pltpu
from jax.sharding import PartitionSpec as P

HEADS = 8
HD = 256
ROT = 64
FF = 8192
SUBSETS = 22
ROOT_ITERS = 8


EPS_NORM = 1e-05
DECAY = 0.5
RATE_BLOCK = 0.6
RATE_VEC = 0.2
NEG_FILL = -1e30
HIGHEST = lax.Precision.HIGHEST
HALF_ROOT = 0.7071067811865476
DENSITY_SCALE = 0.3989422804014327


def apply_layer_norm(values):
    mean_val = jnp.mean(values, axis=-1, keepdims=True)
    centred = values - mean_val
    variance = jnp.mean(centred * centred, axis=-1, keepdims=True)
    inv_std = lax.rsqrt(variance + EPS_NORM)
    return (centred * inv_std, inv_std)


def rotary_tables(row_count, pack_len, rot_dims):
    positions = (jnp.arange(row_count) % pack_len).astype(jnp.float32)
    freqs = 10000.0 ** (-(jnp.arange(rot_dims // 2).astype(jnp.float32) * 2.0) / rot_dims)
    angles = positions[:, None] * freqs[None, :]
    cosines = jnp.cos(angles)
    sines = jnp.sin(angles)
    return (jnp.concatenate([cosines, cosines], -1), jnp.concatenate([sines, sines], -1))


def rotate(values, cosines, sines):
    rot_dims = cosines.shape[-1]
    half_dims = rot_dims // 2
    rotated = values[..., :rot_dims]
    turned = jnp.concatenate([-rotated[..., half_dims:], rotated[..., :half_dims]], -1)
    return jnp.concatenate(
        [rotated * cosines[:, None, :] + turned * sines[:, None, :], values[..., rot_dims:]], -1
    )


def rotate_back(grads, cosines, sines):
    rot_dims = cosines.shape[-1]
    half_dims = rot_dims // 2
    rotated = grads[..., :rot_dims]
    sined = rotated * sines[:, None, :]
    back_turn = jnp.concatenate([sined[..., half_dims:], -sined[..., :half_dims]], -1)
    return jnp.concatenate([rotated * cosines[:, None, :] + back_turn, grads[..., rot_dims:]], -1)


def gelu_slope(values):
    return (
        0.5 * (1.0 + lax.erf(values * HALF_ROOT))
        + values * jnp.exp(-0.5 * values * values) * DENSITY_SCALE
    )


def dot32(left_arg, right_arg):
    return jnp.dot(left_arg, right_arg, preferred_element_type=jnp.float32)


def two_terms(values):
    high = values.astype(jnp.bfloat16)
    return high, (values - high.astype(jnp.float32)).astype(jnp.bfloat16)


def product_three(left_arg, right_arg):
    left_high, left_low = two_terms(left_arg)
    right_high, right_low = two_terms(right_arg)
    return (
        dot32(left_high, right_high) + dot32(left_high, right_low) + dot32(left_low, right_high)
    )


def next_scaled(quarter, quarter16, scaled):
    square_rest = 2.0 * quarter + dot32(quarter16, quarter16)
    square16 = square_rest.astype(jnp.bfloat16)
    fourth_rest = 2.0 * square_rest + dot32(square16, square16)
    return scaled + product_three(fourth_rest, scaled)


def shampoo_kernel(
    grad_ref, left_ref, right_ref, master_ref, grad_out, left_out, right_out, new_out, scaled, roots
):
    count, size, _ = grad_ref.shape
    identity = (
        lax.broadcasted_iota(jnp.int32, (size, size), 0)
        == lax.broadcasted_iota(jnp.int32, (size, size), 1)
    ).astype(jnp.float32)
    factors = []
    for block in range(count):
        grad = grad_ref[block]
        grad_out[block] = grad.astype(jnp.float32)
        for side, stat_ref, stat_out in ((0, left_ref, left_out), (1, right_ref, right_out)):
            dims = (((1 - side,), (1 - side,)), ((), ()))
            stat = DECAY * stat_ref[block] + lax.dot_general(
                grad, grad, dims, preferred_element_type=jnp.float32
            )
            stat_out[block] = stat
            total = jnp.sum(stat * stat, axis=0, keepdims=True)
            norm = jnp.sqrt(jnp.sum(total, axis=1, keepdims=True))
            factors.append(lax.rsqrt(jnp.sqrt(norm)))
            start = stat / norm
            quarter = (identity - start) * 0.25
            roots[2 * block + side] = identity + quarter
            scaled[2 * block + side] = next_scaled(quarter, quarter.astype(jnp.bfloat16), start)

    def iterate(step, carry):
        for item in range(2 * count):
            now = scaled[item]
            quarter = (identity - now) * 0.25
            quarter16 = quarter.astype(jnp.bfloat16)
            root = roots[item]
            roots[item] = root + dot32(root.astype(jnp.bfloat16), quarter16)
            scaled[item] = next_scaled(quarter, quarter16, now)
        return carry

    lax.fori_loop(0, ROOT_ITERS - 2, iterate, 0)
    for block in range(count):
        ends = []
        for side in range(2):
            item = 2 * block + side
            quarter16 = ((identity - scaled[item]) * 0.25).astype(jnp.bfloat16)
            root = roots[item]
            ends.append(root + dot32(root.astype(jnp.bfloat16), quarter16))
        grad = grad_ref[block]
        left_high, left_low = two_terms(ends[0])
        half = dot32(left_high, grad) + dot32(left_low, grad)
        rate = RATE_BLOCK * factors[2 * block] * factors[2 * block + 1]
        new_out[block] = master_ref[block] - rate * product_three(half, ends[1])


def shampoo(grads, left_stats, right_stats, master_blocks):
    owned, size, _ = grads.shape
    count = next(each for each in (4, 3, 2, 1) if owned % each == 0)
    spec = pl.BlockSpec((count, size, size), lambda step: (step, 0, 0))
    result = jax.ShapeDtypeStruct(grads.shape, jnp.float32)
    return pl.pallas_call(
        shampoo_kernel,
        grid=(owned // count,),
        in_specs=[spec] * 4,
        out_specs=[spec] * 4,
        out_shape=[result] * 4,
        scratch_shapes=[pltpu.VMEM((2 * count, size, size), jnp.float32)] * 2,
        compiler_params=pltpu.CompilerParams(vmem_limit_bytes=48 << 20),
        cost_estimate=pl.CostEstimate(
            flops=owned * 88 * 2 * size**3, bytes_accessed=owned * size * size * 30, transcendentals=0
        ),
    )(grads, left_stats, right_stats, master_blocks)


def to_matrix(blocks, block_rows, block_cols):
    block_size = blocks.shape[-1]
    return (
        blocks.reshape(block_rows, block_cols, block_size, block_size)
        .transpose(0, 2, 1, 3)
        .reshape(block_rows * block_size, block_cols * block_size)
    )


def to_blocks(matrix, block_size):
    block_rows = matrix.shape[0] // block_size
    block_cols = matrix.shape[1] // block_size
    return (
        matrix.reshape(block_rows, block_size, block_cols, block_size)
        .transpose(0, 2, 1, 3)
        .reshape(block_rows * block_cols, block_size, block_size)
    )


def allow_mask(row_start, seg_keys, query_rows):
    key_pos = jnp.arange(seg_keys.shape[0])
    query_pos = row_start + jnp.arange(query_rows)
    seg_query = lax.dynamic_slice_in_dim(seg_keys, row_start, query_rows, 0)
    return (key_pos[None, :] <= query_pos[:, None]) & (seg_query[:, None] == seg_keys[None, :])


def block_scores(queries, keys, allowed, score_scale):
    scores = (
        jnp.einsum("qhd,khd->hqk", queries, keys, preferred_element_type=jnp.float32) * score_scale
    )
    return jnp.where(allowed[None], scores, NEG_FILL)


def shards(
    tokens,
    cotangent,
    segments,
    subsets,
    packs,
    master_blocks,
    left_stats,
    right_stats,
    local_vecs,
    local_vec_stats,
    shared_vecs,
    shared_vec_stats,
):
    tp_ways = lax.axis_size("tp")
    tp_rank = lax.axis_index("tp")
    tok_dev, model_width = tokens.shape
    group_tok = tok_dev * tp_ways
    pack_count, pack_len = segments.shape
    seg_width = subsets.shape[1]
    heads_dev = HEADS // tp_ways
    ff_dev = FF // tp_ways
    block_size = master_blocks.shape[-1]
    block_rows = model_width // block_size
    qkv_cols = 3 * heads_dev * HD // block_size
    head_rows = heads_dev * HD // block_size
    ff_blocks = ff_dev // block_size
    first_end = block_rows * qkv_cols
    second_end = first_end + head_rows * block_rows
    third_end = second_end + block_rows * ff_blocks
    group_tokens = lax.all_gather(tokens, "tp", axis=0, tiled=True)
    all_blocks, all_vecs = (
        lax.all_gather(master_blocks.astype(jnp.bfloat16), "dp", axis=0, tiled=True),
        lax.all_gather(local_vecs.astype(jnp.bfloat16), "dp", axis=1, tiled=True),
    )
    norm_params = lax.all_gather(
        shared_vecs.astype(jnp.bfloat16), ("dp", "tp"), axis=1, tiled=True
    ).astype(jnp.float32)
    w_qkv = to_matrix(all_blocks[:first_end], block_rows, qkv_cols)
    w_out = to_matrix(all_blocks[first_end:second_end], head_rows, block_rows)
    w_in = to_matrix(all_blocks[second_end:third_end], block_rows, ff_blocks)
    w_down = to_matrix(all_blocks[third_end:], ff_blocks, block_rows)
    vec_values = all_vecs.astype(jnp.float32)
    bias_qkv = vec_values[: 3 * heads_dev].reshape(-1)
    bias_in = vec_values[3 * heads_dev :].reshape(-1)
    first_gain = norm_params[0]
    first_shift = norm_params[1]
    second_gain = norm_params[2]
    second_shift = norm_params[3]
    own_pos = tp_rank * tok_dev + jnp.arange(tok_dev)
    own_pack = own_pos // pack_len
    valid_own = (own_pack < packs[0]).astype(jnp.float32)
    owned_input_rows = tokens.astype(jnp.float32)
    owned_centred_scaled, owned_inverse_deviation = apply_layer_norm(owned_input_rows)
    group_scaled, _ = apply_layer_norm(group_tokens.astype(jnp.float32))
    first_normed_input = (group_scaled * first_gain + first_shift).astype(jnp.bfloat16)
    second_normed_input = (group_scaled * second_gain + second_shift).astype(jnp.bfloat16)
    seg_flat = segments.reshape(-1)
    cosines, sines = rotary_tables(group_tok, pack_len, ROT)
    qkv_vals = (
        jnp.dot(first_normed_input, w_qkv, preferred_element_type=jnp.float32) + bias_qkv
    ).reshape(group_tok, heads_dev, 3, HD)
    query16 = rotate(qkv_vals[:, :, 0], cosines, sines).astype(jnp.bfloat16)
    key16 = rotate(qkv_vals[:, :, 1], cosines, sines).astype(jnp.bfloat16)
    value16 = qkv_vals[:, :, 2].astype(jnp.bfloat16)
    score_scale = 1.0 / math.sqrt(HD)
    query_rows = min(512, pack_len)
    block_count = pack_len // query_rows

    def forward_pack(pack_idx):
        pack_start = pack_idx * pack_len
        keys = lax.dynamic_slice_in_dim(key16, pack_start, pack_len, 0)
        values = lax.dynamic_slice_in_dim(value16, pack_start, pack_len, 0)
        seg_keys = lax.dynamic_slice_in_dim(seg_flat, pack_start, pack_len, 0)

        def forward_block(block_idx):
            row_start = block_idx * query_rows
            queries = lax.dynamic_slice_in_dim(query16, pack_start + row_start, query_rows, 0)
            masked = block_scores(
                queries, keys, allow_mask(row_start, seg_keys, query_rows), score_scale
            )
            row_max = jnp.max(masked, axis=-1, keepdims=True)
            exp_terms = jnp.exp(masked - row_max)
            row_total = jnp.sum(exp_terms, axis=-1, keepdims=True)
            attn_probs = (exp_terms / row_total).astype(jnp.bfloat16)
            attended = jnp.einsum(
                "hqk,khd->qhd", attn_probs, values, preferred_element_type=jnp.float32
            )
            return (attended.astype(jnp.bfloat16), (row_max + jnp.log(row_total))[..., 0])

        attended, sums_pack = lax.map(forward_block, jnp.arange(block_count))
        return (attended.reshape(pack_len, heads_dev, HD), sums_pack)

    attn_heads, log_sums = lax.map(forward_pack, jnp.arange(pack_count))
    attn16 = attn_heads.reshape(group_tok, heads_dev * HD)
    hidden = jnp.dot(second_normed_input, w_in, preferred_element_type=jnp.float32) + bias_in
    activated = jax.nn.gelu(hidden, approximate=False).astype(jnp.bfloat16)
    partial_value = jnp.dot(attn16, w_out, preferred_element_type=jnp.float32) + jnp.dot(
        activated, w_down, preferred_element_type=jnp.float32
    )
    branch = lax.psum_scatter(
        partial_value.astype(jnp.bfloat16), "tp", scatter_dimension=0, tiled=True
    ).astype(jnp.float32)
    output = (
        valid_own[:, None] * (owned_input_rows + branch + norm_params[4] + norm_params[5])
    ).astype(jnp.bfloat16)
    seg_own = lax.dynamic_slice_in_dim(seg_flat, tp_rank * tok_dev, tok_dev, 0)
    lookup_key = own_pack * seg_width + seg_own
    subset_flat = subsets.reshape(-1)
    onehot = lookup_key[:, None] == jnp.arange(pack_count * seg_width)[None, :]
    subset_own = jnp.sum(jnp.where(onehot, subset_flat[None, :], 0), axis=1)
    weight = 0.5 + subset_own.astype(jnp.float32) / (SUBSETS - 1)
    seed16 = (cotangent.astype(jnp.float32) * weight[:, None] * valid_own[:, None]).astype(
        jnp.bfloat16
    )
    seed_all = lax.all_gather(seed16, "tp", axis=0, tiled=True)
    out_bias_grad = jnp.sum(seed16, axis=0, dtype=jnp.float32)
    d_attn16 = jnp.einsum("td,cd->tc", seed_all, w_out, preferred_element_type=jnp.float32).astype(
        jnp.bfloat16
    )
    grad_wout = jnp.einsum("tc,td->cd", attn16, seed_all, preferred_element_type=jnp.float32)
    d_act = jnp.einsum("td,fd->tf", seed_all, w_down, preferred_element_type=jnp.float32)
    grad_wdown = jnp.einsum("tf,td->fd", activated, seed_all, preferred_element_type=jnp.float32)
    d_hidden16 = (d_act * gelu_slope(hidden)).astype(jnp.bfloat16)
    grad_win = jnp.einsum(
        "td,tf->df", second_normed_input, d_hidden16, preferred_element_type=jnp.float32
    )
    grad_bin = jnp.sum(d_hidden16, axis=0, dtype=jnp.float32)
    d_normed_two = jnp.einsum("tf,df->td", d_hidden16, w_in, preferred_element_type=jnp.float32)
    d_attn_heads = d_attn16.reshape(group_tok, heads_dev, HD)

    def backward_pack(pack_idx):
        pack_start = pack_idx * pack_len
        keys = lax.dynamic_slice_in_dim(key16, pack_start, pack_len, 0)
        values = lax.dynamic_slice_in_dim(value16, pack_start, pack_len, 0)
        seg_keys = lax.dynamic_slice_in_dim(seg_flat, pack_start, pack_len, 0)
        query_pack = lax.dynamic_slice_in_dim(query16, pack_start, pack_len, 0)
        d_out_pack = lax.dynamic_slice_in_dim(d_attn_heads, pack_start, pack_len, 0)
        sums_pack = log_sums[pack_idx]

        def backward_block(carry, block_idx):
            key_acc, value_acc = carry
            row_start = block_idx * query_rows
            queries = lax.dynamic_slice_in_dim(query_pack, row_start, query_rows, 0)
            d_out = lax.dynamic_slice_in_dim(d_out_pack, row_start, query_rows, 0)
            masked = block_scores(
                queries, keys, allow_mask(row_start, seg_keys, query_rows), score_scale
            )
            attn_probs = jnp.exp(masked - sums_pack[block_idx][:, :, None])
            d_probs = jnp.einsum("qhd,khd->hqk", d_out, values, preferred_element_type=jnp.float32)
            row_dot = jnp.sum(attn_probs * d_probs, axis=-1, keepdims=True)
            d_scores = (attn_probs * (d_probs - row_dot)).astype(jnp.bfloat16)
            d_query = (
                jnp.einsum("hqk,khd->qhd", d_scores, keys, preferred_element_type=jnp.float32)
                * score_scale
            )
            key_acc = (
                key_acc
                + jnp.einsum("hqk,qhd->khd", d_scores, queries, preferred_element_type=jnp.float32)
                * score_scale
            )
            value_acc = value_acc + jnp.einsum(
                "hqk,qhd->khd",
                attn_probs.astype(jnp.bfloat16),
                d_out,
                preferred_element_type=jnp.float32,
            )
            return ((key_acc, value_acc), d_query)

        zero_acc = jnp.zeros((pack_len, heads_dev, HD), jnp.float32)
        (d_keys, d_values), d_queries = lax.scan(
            backward_block, (zero_acc, zero_acc), jnp.arange(block_count)
        )
        return (d_queries.reshape(pack_len, heads_dev, HD), d_keys, d_values)

    d_queries, d_keys, d_values = lax.map(backward_pack, jnp.arange(pack_count))
    d_queries = rotate_back(d_queries.reshape(group_tok, heads_dev, HD), cosines, sines)
    d_keys = rotate_back(d_keys.reshape(group_tok, heads_dev, HD), cosines, sines)
    d_values = d_values.reshape(group_tok, heads_dev, HD)
    d_qkv16 = (
        jnp.stack([d_queries, d_keys, d_values], 2)
        .reshape(group_tok, 3 * heads_dev * HD)
        .astype(jnp.bfloat16)
    )
    grad_wqkv = jnp.einsum(
        "td,tc->dc", first_normed_input, d_qkv16, preferred_element_type=jnp.float32
    )
    grad_bqkv = jnp.sum(d_qkv16, axis=0, dtype=jnp.float32)
    d_normed_one = jnp.einsum("tc,dc->td", d_qkv16, w_qkv, preferred_element_type=jnp.float32)
    first_gain_gradient = jnp.sum(d_normed_one * group_scaled, axis=0)
    grad_shift_one = jnp.sum(d_normed_one, axis=0)
    second_gain_gradient = jnp.sum(d_normed_two * group_scaled, axis=0)
    grad_shift_two = jnp.sum(d_normed_two, axis=0)
    norm_input_gradient = lax.psum_scatter(
        (d_normed_one * first_gain + d_normed_two * second_gain).astype(jnp.bfloat16),
        "tp",
        scatter_dimension=0,
        tiled=True,
    ).astype(jnp.float32)
    average_gradient = jnp.mean(norm_input_gradient, axis=-1, keepdims=True)
    average_projection = jnp.mean(
        norm_input_gradient * owned_centred_scaled, axis=-1, keepdims=True
    )
    input_grad = seed16.astype(jnp.float32) + owned_inverse_deviation * (
        norm_input_gradient - average_gradient - owned_centred_scaled * average_projection
    )
    dp_ways = lax.axis_size("dp")
    vec_rows = 3 * heads_dev + ff_dev // HD
    shared_local = jnp.stack(
        [first_gain_gradient, grad_shift_one, second_gain_gradient, grad_shift_two, out_bias_grad], 0
    )
    vecs_local = jnp.concatenate(
        [grad_bqkv.reshape(3 * heads_dev, HD), grad_bin.reshape(ff_dev // HD, HD)], 0
    )
    small = jnp.concatenate(
        [
            shared_local.reshape(5, dp_ways, -1).transpose(1, 0, 2).reshape(dp_ways, -1),
            vecs_local.reshape(vec_rows, dp_ways, -1).transpose(1, 0, 2).reshape(dp_ways, -1),
        ],
        1,
    )
    used = small.shape[1]
    small = jnp.pad(small, ((0, 0), (0, -used % 1024))).reshape(-1, 128)
    small_own = lax.psum_scatter(small, "dp", scatter_dimension=0, tiled=True).reshape(-1)
    shared_used = 5 * model_width // dp_ways
    own_vec_grads = small_own[shared_used:used].reshape(vec_rows, HD // dp_ways)
    shared_part = small_own[:shared_used].reshape(5, tp_ways, -1).transpose(1, 0, 2)
    shared_part = jnp.pad(
        shared_part.reshape(tp_ways, -1), ((0, 0), (0, -(shared_used // tp_ways) % 1024))
    ).reshape(-1, 128)
    shared_own = lax.psum_scatter(shared_part, "tp", scatter_dimension=0, tiled=True).reshape(-1)
    shared_own = shared_own[: shared_used // tp_ways].reshape(5, -1)
    shared_grads = jnp.concatenate([shared_own, shared_own[4:]], 0)
    blocks_local = jnp.concatenate(
        [
            to_blocks(grad_wqkv.astype(jnp.bfloat16), block_size),
            to_blocks(grad_wout.astype(jnp.bfloat16), block_size),
            to_blocks(grad_win.astype(jnp.bfloat16), block_size),
            to_blocks(grad_wdown.astype(jnp.bfloat16), block_size),
        ],
        0,
    )
    grads16 = lax.psum_scatter(blocks_local, "dp", scatter_dimension=0, tiled=True)
    own_grads, left_new, right_new, new_blocks = shampoo(
        grads16, left_stats, right_stats, master_blocks
    )
    local_stat_new = DECAY * local_vec_stats + own_vec_grads * own_vec_grads
    local_new = local_vecs - RATE_VEC * own_vec_grads * lax.rsqrt(local_stat_new)
    shared_stat_new = DECAY * shared_vec_stats + shared_grads * shared_grads
    shared_new = shared_vecs - RATE_VEC * shared_grads * lax.rsqrt(shared_stat_new)
    return (
        output,
        input_grad,
        own_grads,
        left_new,
        right_new,
        new_blocks,
        own_vec_grads,
        local_stat_new,
        local_new,
        shared_grads,
        shared_stat_new,
        shared_new,
    )


def solution(mesh):
    placed = (
        P(("dp", "tp"), None),
        P(("dp", "tp"), None),
        P("dp", None),
        P("dp", None),
        P("dp"),
        P(("dp", "tp"), None, None),
        P(("dp", "tp"), None, None),
        P(("dp", "tp"), None, None),
        P("tp", "dp"),
        P("tp", "dp"),
        P(None, ("dp", "tp")),
        P(None, ("dp", "tp")),
    )
    return jax.shard_map(
        shards,
        mesh=mesh,
        in_specs=placed,
        out_specs=(
            P(("dp", "tp"), None),
            P(("dp", "tp"), None),
            P(("dp", "tp"), None, None),
            P(("dp", "tp"), None, None),
            P(("dp", "tp"), None, None),
            P(("dp", "tp"), None, None),
            P("tp", "dp"),
            P("tp", "dp"),
            P("tp", "dp"),
            P(None, ("dp", "tp")),
            P(None, ("dp", "tp")),
            P(None, ("dp", "tp")),
        ),
        check_vma=False,
    )
```

```python
import functools
import math

import jax
import jax.numpy as jnp
from jax import lax
from jax.experimental import pallas as pl
from jax.experimental.pallas import tpu as pltpu
from jax.sharding import PartitionSpec as P

HEADS = 8
HD = 256
ROT = 64
FF = 8192
SUBSETS = 22
ROOT_ITERS = 8


EPS_NORM = 1e-05
DECAY = 0.5
RATE_BLOCK = 0.6
RATE_VEC = 0.2
NEG_FILL = -1e30
DOC_MAX = 512
HALF_ROOT = 0.7071067811865476
DENSITY_SCALE = 0.3989422804014327


def apply_layer_norm(values):
    mean_val = jnp.mean(values, axis=-1, keepdims=True)
    centred = values - mean_val
    variance = jnp.mean(centred * centred, axis=-1, keepdims=True)
    inv_std = lax.rsqrt(variance + EPS_NORM)
    return (centred * inv_std, inv_std)


EXTRA_ROWS = 16
VMEM_LIMIT = 60 << 20
NN = (((1,), (0,)), ((), ()))
NT = (((1,), (1,)), ((), ()))
TN = (((0,), (0,)), ((), ()))


def contract(left_arg, right_arg, dims):
    return lax.dot_general(left_arg, right_arg, dims, preferred_element_type=jnp.float32)


def kernel_params():
    return pltpu.CompilerParams(vmem_limit_bytes=VMEM_LIMIT)


def block_row(index, owned, size):
    return index // owned * (owned * size + EXTRA_ROWS) + index % owned * size


def block_copies(blocks_ref, owned, first, rows, cols, target, sems):
    size = blocks_ref.shape[-1]
    return [
        pltpu.make_async_copy(
            blocks_ref.at[pl.ds(block_row(first + row * cols + col, owned, size), size), :],
            target.at[pl.ds(row * size, size), pl.ds(col * size, size)],
            sems.at[row * cols + col],
        )
        for row in range(rows)
        for col in range(cols)
    ]


def begin_copies(copies):
    @pl.when(pl.program_id(0) == 0)
    def _():
        for copy in copies:
            copy.start()


def end_copies(copies):
    @pl.when(pl.program_id(0) == 0)
    def _():
        for copy in copies:
            copy.wait()


def turn(values, cosines, sines):
    lane = lax.broadcasted_iota(jnp.int32, values.shape, 1)
    half = ROT // 2
    wide = values.shape[1]
    swapped = jnp.where(
        lane < half, pltpu.roll(values, wide - half, 1), pltpu.roll(values, half, 1)
    )
    return values * cosines + swapped * sines


def turn_tables(pack_len, lanes):
    half = ROT // 2
    positions = jnp.arange(pack_len).astype(jnp.float32)
    freqs = 10000.0 ** (-(jnp.arange(half).astype(jnp.float32) * 2.0) / ROT)
    angles = positions[:, None] * freqs[None, :]
    cosines = jnp.cos(angles)
    sines = jnp.sin(angles)
    rest = jnp.zeros((pack_len, lanes - ROT), jnp.float32)
    return (
        jnp.concatenate([cosines, cosines, rest + 1.0], -1),
        jnp.concatenate([-sines, sines, rest], -1),
    )


def normed_rows(rows):
    mean = jnp.mean(rows, axis=1, keepdims=True)
    centred = rows - mean
    variance = jnp.mean(centred * centred, axis=1, keepdims=True)
    return mean, lax.rsqrt(variance + EPS_NORM)


def part_copies(part_refs, held, sems):
    return [
        pltpu.make_async_copy(part, held.at[index], sems.at[index])
        for index, part in enumerate(part_refs)
    ]


def await_part(copies, per_part):
    step = pl.program_id(0)
    for index, copy in enumerate(copies):

        @pl.when(step == index * per_part)
        def _():
            copy.wait()


def qkv_kernel(heads, owned, parts, rank_ref, *refs):
    part_refs = refs[:parts]
    blocks_ref, norm_ref, bias_ref, cos_ref, sin_ref = refs[parts : parts + 5]
    qkv_ref, first_ref, second_ref, tokens_ref, weight, held, sems, part_sems = refs[parts + 5 :]
    size = blocks_ref.shape[-1]
    copies = block_copies(blocks_ref, owned, 0, weight.shape[0] // size, weight.shape[1] // size, weight, sems)
    moves = part_copies(part_refs, held, part_sems)
    begin_copies(moves + copies)
    await_part(moves, 1)
    own = held[pl.program_id(0)]
    tokens_ref[...] = own
    rows = own.astype(jnp.float32)
    mean, inverse = normed_rows(rows)
    scaled = (rows - mean) * inverse
    second_ref[...] = (scaled * norm_ref[2:3, :] + norm_ref[3:4, :]).astype(jnp.bfloat16)
    values = (scaled * norm_ref[0:1, :] + norm_ref[1:2, :]).astype(jnp.bfloat16)
    first_ref[...] = values
    end_copies(copies)
    lanes = cos_ref.shape[1]
    for head in range(heads):
        for part in range(3):
            cols = pl.ds((head * 3 + part) * HD, HD)
            result = contract(first_ref[...], weight[:, cols], NN) + bias_ref[:, cols]
            if part < 2:
                first = turn(result[:, :lanes], cos_ref[...], sin_ref[...])
                result = jnp.concatenate([first, result[:, lanes:]], 1)
            if part == 0:
                result = result * (1.0 / math.sqrt(HD))
            qkv_ref[:, cols] = result.astype(jnp.bfloat16)


def project_qkv(parts, rank, blocks, owned, norm_params, bias, cosines, sines, heads):
    ways = len(parts)
    tile, width = parts[0].shape
    tokens = ways * tile
    size = blocks.shape[-1]
    pack_len, lanes = cosines.shape
    cols = 3 * heads * HD
    per_pack = pack_len // tile
    place = lambda i, rank: (rank[0] - i + ways) % ways
    row = lambda n: pl.BlockSpec((tile, n), lambda i, rank: (place(i, rank), 0))
    table = pl.BlockSpec((tile, lanes), lambda i, rank: (place(i, rank) % per_pack, 0))
    anywhere = pl.BlockSpec(memory_space=pl.ANY)
    wide = jax.ShapeDtypeStruct((tokens, width), jnp.bfloat16)
    return pl.pallas_call(
        functools.partial(qkv_kernel, heads, owned, ways),
        grid_spec=pltpu.PrefetchScalarGridSpec(
            num_scalar_prefetch=1,
            grid=(ways,),
            in_specs=[anywhere] * (ways + 1)
            + [
                pl.BlockSpec(norm_params.shape, lambda i, rank: (0, 0)),
                pl.BlockSpec((1, cols), lambda i, rank: (0, 0)),
                table,
                table,
            ],
            out_specs=[row(cols), row(width), row(width), row(width)],
            scratch_shapes=[
                pltpu.VMEM((width, cols), jnp.bfloat16),
                pltpu.VMEM((ways, tile, width), jnp.bfloat16),
                pltpu.SemaphoreType.DMA((width // size * (cols // size),)),
                pltpu.SemaphoreType.DMA((ways,)),
            ],
        ),
        out_shape=[jax.ShapeDtypeStruct((tokens, cols), jnp.bfloat16), wide, wide, wide],
        compiler_params=kernel_params(),
        cost_estimate=pl.CostEstimate(
            flops=2 * tokens * width * cols, bytes_accessed=tokens * (4 * width + cols) * 2 + width * cols * 2, transcendentals=0
        ),
        name="qkv",
    )(rank, *parts, blocks, norm_params, bias, cosines, sines)


def attend_kernel(query_ref, key_ref, value_ref, seg_row, seg_col, out_ref):
    length = key_ref.shape[0]
    step = 256
    for start in range(0, length, step):
        first = max(0, start - DOC_MAX)
        stop = start + step
        scores = contract(query_ref[start:stop, :], key_ref[first:stop, :], NT)
        row = lax.broadcasted_iota(jnp.int32, scores.shape, 0) + start
        col = lax.broadcasted_iota(jnp.int32, scores.shape, 1) + first
        allowed = (col <= row) & (seg_col[0, start:stop, :] == seg_row[0, :, first:stop])
        masked = jnp.where(allowed, scores, NEG_FILL)
        exp_terms = jnp.exp(masked - jnp.max(masked, axis=1, keepdims=True))
        probs = exp_terms * (1.0 / jnp.sum(exp_terms, axis=1, keepdims=True))
        out_ref[start:stop, :] = contract(
            probs.astype(jnp.bfloat16), value_ref[first:stop, :], NN
        ).astype(jnp.bfloat16)


def attend(qkv, segments, heads):
    packs, length = segments.shape
    part = lambda which: pl.BlockSpec((length, HD), lambda p, h: (p, h * 3 + which))
    return pl.pallas_call(
        attend_kernel,
        grid=(packs, heads),
        in_specs=[
            part(0),
            part(1),
            part(2),
            pl.BlockSpec((1, 1, length), lambda p, h: (p, 0, 0)),
            pl.BlockSpec((1, length, 1), lambda p, h: (p, 0, 0)),
        ],
        out_specs=pl.BlockSpec((length, HD), lambda p, h: (p, h)),
        out_shape=jax.ShapeDtypeStruct((packs * length, heads * HD), jnp.bfloat16),
        compiler_params=kernel_params(),
        cost_estimate=pl.CostEstimate(
            flops=packs * heads * length * length * HD * 3, bytes_accessed=packs * length * heads * HD * 8, transcendentals=0
        ),
        name="attend",
    )(qkv, qkv, qkv, segments[:, None, :], segments[:, :, None])


def attend_back_kernel(
    query_ref, key_ref, value_ref, d_out_ref, seg_row, seg_col, cos_ref, sin_ref, grad_ref, d_key, d_value
):
    length = key_ref.shape[0]
    step = 256
    lanes = cos_ref.shape[1]
    d_key[...] = jnp.zeros_like(d_key)
    d_value[...] = jnp.zeros_like(d_value)
    for start in range(0, length, step):
        first = max(0, start - DOC_MAX)
        stop = start + step
        query = query_ref[start:stop, :]
        d_out = d_out_ref[start:stop, :]
        keys = key_ref[first:stop, :]
        scores = contract(keys, query, NT)
        key_pos = lax.broadcasted_iota(jnp.int32, scores.shape, 0) + first
        query_pos = lax.broadcasted_iota(jnp.int32, scores.shape, 1) + start
        allowed = (key_pos <= query_pos) & (seg_col[0, first:stop, :] == seg_row[0, :, start:stop])
        masked = jnp.where(allowed, scores, NEG_FILL)
        exp_terms = jnp.exp(masked - jnp.max(masked, axis=0, keepdims=True))
        probs = exp_terms * (1.0 / jnp.sum(exp_terms, axis=0, keepdims=True))
        d_probs = contract(value_ref[first:stop, :], d_out, NT)
        row_dot = jnp.sum(probs * d_probs, axis=0, keepdims=True)
        d_scores = (probs * (d_probs - row_dot)).astype(jnp.bfloat16)
        d_value[first:stop, :] += contract(probs.astype(jnp.bfloat16), d_out, NN)
        d_key[first:stop, :] += contract(d_scores, query, NN)
        d_query = contract(d_scores, keys, TN) * (1.0 / math.sqrt(HD))
        back = turn(d_query[:, :lanes], cos_ref[start:stop, :], -sin_ref[start:stop, :])
        grad_ref[start:stop, :lanes] = back.astype(jnp.bfloat16)
        grad_ref[start:stop, lanes:HD] = d_query[:, lanes:].astype(jnp.bfloat16)
    back = turn(d_key[:, :lanes], cos_ref[...], -sin_ref[...])
    grad_ref[:, HD : HD + lanes] = back.astype(jnp.bfloat16)
    grad_ref[:, HD + lanes : 2 * HD] = d_key[:, lanes:].astype(jnp.bfloat16)
    grad_ref[:, 2 * HD :] = d_value[...].astype(jnp.bfloat16)


def attend_back(qkv, d_attended, segments, cosines, sines, heads):
    packs, length = segments.shape
    lanes = cosines.shape[1]
    part = lambda which: pl.BlockSpec((length, HD), lambda p, h: (p, h * 3 + which))
    table = pl.BlockSpec((length, lanes), lambda p, h: (0, 0))
    return pl.pallas_call(
        attend_back_kernel,
        grid=(packs, heads),
        in_specs=[
            part(0),
            part(1),
            part(2),
            pl.BlockSpec((length, HD), lambda p, h: (p, h)),
            pl.BlockSpec((1, 1, length), lambda p, h: (p, 0, 0)),
            pl.BlockSpec((1, length, 1), lambda p, h: (p, 0, 0)),
            table,
            table,
        ],
        out_specs=pl.BlockSpec((length, 3 * HD), lambda p, h: (p, h)),
        out_shape=jax.ShapeDtypeStruct((packs * length, 3 * heads * HD), jnp.bfloat16),
        scratch_shapes=[pltpu.VMEM((length, HD), jnp.float32)] * 2,
        compiler_params=kernel_params(),
        cost_estimate=pl.CostEstimate(
            flops=packs * heads * length * length * HD * 7, bytes_accessed=packs * length * heads * HD * 16, transcendentals=0
        ),
        name="attend_back",
    )(qkv, qkv, qkv, d_attended, segments[:, None, :], segments[:, :, None], cosines, sines)


def feed_kernel(
    offsets, owned, x_ref, attended_ref, blocks_ref, bias_ref, act_ref, slope_ref, out_ref, w_in, w_down, sems_in, sems_down
):
    size = blocks_ref.shape[-1]
    width, hidden_units = w_in.shape
    inner = hidden_units // size
    first_out, first_in, first_down = offsets
    head_rows = attended_ref.shape[1] // size
    outer = width // size
    copies_in = block_copies(blocks_ref, owned, first_in, outer, inner, w_in, sems_in)
    copies_down = block_copies(blocks_ref, owned, first_down, inner, outer, w_down.at[pl.ds(0, hidden_units)], sems_down)
    copies_down += block_copies(
        blocks_ref,
        owned,
        first_out,
        head_rows,
        outer,
        w_down.at[pl.ds(hidden_units, head_rows * size)],
        sems_down.at[pl.ds(inner * outer, head_rows * outer)],
    )
    begin_copies(copies_in + copies_down)
    end_copies(copies_in)
    values = x_ref[...]
    for col in range(inner):
        cols = pl.ds(col * size, size)
        hidden = contract(values, w_in[:, cols], NN) + bias_ref[:, cols]
        cdf = 0.5 + 0.5 * lax.erf(hidden * HALF_ROOT)
        density = jnp.exp(-0.5 * hidden * hidden) * DENSITY_SCALE
        act_ref[:, cols] = (hidden * cdf).astype(jnp.bfloat16)
        slope_ref[:, cols] = (cdf + hidden * density).astype(jnp.bfloat16)
    end_copies(copies_down)
    for col in range(outer):
        cols = pl.ds(col * size, size)
        out_ref[:, cols] = (
            contract(act_ref[...], w_down[:hidden_units, cols], NN)
            + contract(attended_ref[...], w_down[hidden_units:, cols], NN)
        ).astype(jnp.bfloat16)


def feed_forward(normed, attended, blocks, owned, bias, offsets):
    tokens, width = normed.shape
    size = blocks.shape[-1]
    hidden_units = bias.shape[1]
    head_cols = attended.shape[1]
    tile = 512
    row = lambda cols: pl.BlockSpec((tile, cols), lambda i: (i, 0))
    inner, outer = hidden_units // size, width // size
    return pl.pallas_call(
        functools.partial(feed_kernel, offsets, owned),
        grid=(tokens // tile,),
        in_specs=[
            row(width),
            row(head_cols),
            pl.BlockSpec(memory_space=pl.ANY),
            pl.BlockSpec((1, hidden_units), lambda i: (0, 0)),
        ],
        out_specs=[row(hidden_units), row(hidden_units), row(width)],
        out_shape=[
            jax.ShapeDtypeStruct((tokens, hidden_units), jnp.bfloat16),
            jax.ShapeDtypeStruct((tokens, hidden_units), jnp.bfloat16),
            jax.ShapeDtypeStruct((tokens, width), jnp.bfloat16),
        ],
        scratch_shapes=[
            pltpu.VMEM((width, hidden_units), jnp.bfloat16),
            pltpu.VMEM((hidden_units + head_cols, width), jnp.bfloat16),
            pltpu.SemaphoreType.DMA((inner * outer,)),
            pltpu.SemaphoreType.DMA((inner * outer + head_cols // size * outer,)),
        ],
        compiler_params=kernel_params(),
        cost_estimate=pl.CostEstimate(
            flops=2 * tokens * width * (2 * hidden_units + head_cols), bytes_accessed=tokens * width * 10 + width * hidden_units * 4, transcendentals=0
        ),
        name="feed",
    )(normed, attended, blocks, bias)


def column_sum(values):
    rows, cols = values.shape
    return jnp.sum(values.reshape(rows // 8, 8, cols), axis=0)


def feed_back_kernel(offsets, owned, parts, held_count, rank_ref, *refs):
    part_refs = refs[:parts]
    factor_ref, slope_ref, tokens_ref, blocks_ref, norm_ref = refs[parts : parts + 5]
    (
        seed_ref, d_attended_ref, d_hidden_ref, dz_ref, norm_sums, hidden_sums,
        w_in, w_down, w_out, held, sems_in, sems_down, sems_out, part_sems,
    ) = refs[parts + 5 + held_count :]
    size = blocks_ref.shape[-1]
    width, hidden_units = w_in.shape
    inner, outer = hidden_units // size, width // size
    first_out, first_in, first_down = offsets
    tile = seed_ref.shape[0]
    per_part = held.shape[1] // tile
    moves = part_copies(part_refs, held, part_sems)
    copies_out = block_copies(blocks_ref, owned, first_out, w_out.shape[0] // size, outer, w_out, sems_out)
    copies_down = block_copies(blocks_ref, owned, first_down, inner, outer, w_down, sems_down)
    copies_in = block_copies(blocks_ref, owned, first_in, outer, inner, w_in, sems_in)
    begin_copies(moves + copies_out + copies_down + copies_in)

    @pl.when(pl.program_id(0) == 0)
    def _():
        norm_sums[...] = jnp.zeros_like(norm_sums)
        hidden_sums[...] = jnp.zeros_like(hidden_sums)

    await_part(moves, per_part)
    step = pl.program_id(0)
    cotangent = held[step // per_part, pl.ds(pl.multiple_of(step % per_part * tile, tile), tile), :]
    seed_ref[...] = (cotangent.astype(jnp.float32) * factor_ref[...]).astype(jnp.bfloat16)
    seed = seed_ref[...]
    end_copies(copies_out)
    d_attended_ref[...] = contract(seed, w_out[...], NT).astype(jnp.bfloat16)
    end_copies(copies_down)
    for col in range(inner):
        cols = pl.ds(col * size, size)
        d_act = contract(seed_ref[...], w_down[cols, :], NT)
        d_hidden = (d_act * slope_ref[:, cols].astype(jnp.float32)).astype(jnp.bfloat16)
        d_hidden_ref[:, cols] = d_hidden
        hidden_sums[:, cols] += column_sum(d_hidden.astype(jnp.float32))
    end_copies(copies_in)
    mean, inverse = normed_rows(tokens_ref[...].astype(jnp.float32))
    for col in range(outer):
        cols = pl.ds(col * size, size)
        scaled = (tokens_ref[:, cols].astype(jnp.float32) - mean) * inverse
        second = contract(d_hidden_ref[...], w_in[cols, :], NT)
        dz_ref[:, cols] = second * norm_ref[2:3, cols]
        norm_sums[0:8, cols] += column_sum(second * scaled)
        norm_sums[8:16, cols] += column_sum(second)


def feed_back(parts, first_part, ways, rank, factor, slope, group_tokens, blocks, owned, norm_params, offsets, head_cols, priors):
    chunk, width = parts[0].shape
    tokens = ways * chunk
    size = blocks.shape[-1]
    hidden_units = slope.shape[1]
    tile = min(256, chunk)
    per_part = chunk // tile
    inner, outer = hidden_units // size, width // size
    place = lambda i, rank: (rank[0] - first_part - i // per_part + ways) % ways * per_part + i % per_part
    row = lambda n: pl.BlockSpec((tile, n), lambda i, rank: (place(i, rank), 0))
    whole = lambda rows, cols: pl.BlockSpec((rows, cols), lambda i, rank: (0, 0))
    anywhere = pl.BlockSpec(memory_space=pl.ANY)
    count = len(parts)
    rows = count * chunk
    return pl.pallas_call(
        functools.partial(feed_back_kernel, offsets, owned, count, len(priors)),
        grid_spec=pltpu.PrefetchScalarGridSpec(
            num_scalar_prefetch=1,
            grid=(count * per_part,),
            in_specs=[anywhere] * count
            + [row(1), row(hidden_units), row(width), anywhere, whole(norm_params.shape[0], width)]
            + [anywhere] * len(priors),
            out_specs=[
                row(width), row(head_cols), row(hidden_units), row(width), whole(16, width), whole(8, hidden_units),
            ],
            scratch_shapes=[
                pltpu.VMEM((width, hidden_units), jnp.bfloat16),
                pltpu.VMEM((hidden_units, width), jnp.bfloat16),
                pltpu.VMEM((head_cols, width), jnp.bfloat16),
                pltpu.VMEM((count, chunk, width), jnp.bfloat16),
                pltpu.SemaphoreType.DMA((inner * outer,)),
                pltpu.SemaphoreType.DMA((inner * outer,)),
                pltpu.SemaphoreType.DMA((head_cols // size * outer,)),
                pltpu.SemaphoreType.DMA((count,)),
            ],
        ),
        out_shape=[
            jax.ShapeDtypeStruct((tokens, width), jnp.bfloat16),
            jax.ShapeDtypeStruct((tokens, head_cols), jnp.bfloat16),
            jax.ShapeDtypeStruct((tokens, hidden_units), jnp.bfloat16),
            jax.ShapeDtypeStruct((tokens, width), jnp.float32),
            jax.ShapeDtypeStruct((16, width), jnp.float32),
            jax.ShapeDtypeStruct((8, hidden_units), jnp.float32),
        ],
        input_output_aliases={1 + count + 5 + index: index for index in range(len(priors))},
        compiler_params=kernel_params(),
        cost_estimate=pl.CostEstimate(
            flops=2 * rows * width * (2 * hidden_units + head_cols), bytes_accessed=rows * width * 14 + width * hidden_units * 4, transcendentals=0
        ),
        name="feed_back",
    )(rank, *parts, factor, slope, group_tokens, blocks, norm_params, *priors)


def qkv_back_kernel(owned, d_qkv_ref, part_ref, tokens_ref, blocks_ref, norm_ref, dz_ref, norm_sums, qkv_sums, w_qkv, sems):
    size = blocks_ref.shape[-1]
    outer = w_qkv.shape[0] // size
    copies = block_copies(blocks_ref, owned, 0, outer, w_qkv.shape[1] // size, w_qkv, sems)
    begin_copies(copies)

    @pl.when(pl.program_id(0) == 0)
    def _():
        norm_sums[...] = jnp.zeros_like(norm_sums)
        qkv_sums[...] = jnp.zeros_like(qkv_sums)

    qkv_sums[...] += column_sum(d_qkv_ref[...].astype(jnp.float32))
    mean, inverse = normed_rows(tokens_ref[...].astype(jnp.float32))
    end_copies(copies)
    for col in range(outer):
        cols = pl.ds(col * size, size)
        scaled = (tokens_ref[:, cols].astype(jnp.float32) - mean) * inverse
        first = contract(d_qkv_ref[...], w_qkv[cols, :], NT)
        dz_ref[:, cols] = (part_ref[:, cols] + first * norm_ref[0:1, cols]).astype(jnp.bfloat16)
        norm_sums[0:8, cols] += column_sum(first * scaled)
        norm_sums[8:16, cols] += column_sum(first)


def qkv_back(d_qkv, dz_part, group_tokens, blocks, owned, norm_params):
    tokens, qkv_cols = d_qkv.shape
    width = dz_part.shape[1]
    size = blocks.shape[-1]
    tile = 512
    row = lambda cols: pl.BlockSpec((tile, cols), lambda i: (i, 0))
    whole = lambda rows, cols: pl.BlockSpec((rows, cols), lambda i: (0, 0))
    outer = width // size
    return pl.pallas_call(
        functools.partial(qkv_back_kernel, owned),
        grid=(tokens // tile,),
        in_specs=[
            row(qkv_cols), row(width), row(width), pl.BlockSpec(memory_space=pl.ANY), whole(norm_params.shape[0], width),
        ],
        out_specs=[row(width), whole(16, width), whole(8, qkv_cols)],
        out_shape=[
            jax.ShapeDtypeStruct((tokens, width), jnp.bfloat16),
            jax.ShapeDtypeStruct((16, width), jnp.float32),
            jax.ShapeDtypeStruct((8, qkv_cols), jnp.float32),
        ],
        scratch_shapes=[
            pltpu.VMEM((width, qkv_cols), jnp.bfloat16),
            pltpu.SemaphoreType.DMA((outer * (qkv_cols // size),)),
        ],
        compiler_params=kernel_params(),
        cost_estimate=pl.CostEstimate(
            flops=2 * tokens * width * qkv_cols, bytes_accessed=tokens * width * 11, transcendentals=0
        ),
        name="qkv_back",
    )(d_qkv, dz_part, group_tokens, blocks, norm_params)


def weight_grad_kernel(table, owned, part_size, core_ref, *refs):
    products = len(table)
    parts = owned // part_size
    left_refs, refs = refs[:products], refs[products:]
    rights, refs = refs[:3], refs[3:]
    outs, refs = refs[: 2 * parts], refs[2 * parts :]
    held, (results, sems, right_sems) = refs[:3], refs[3:]
    size = results.shape[-1]
    step = pl.program_id(0)
    slot = lax.rem(step, 2)
    core = core_ref[0]
    loads = [pltpu.make_async_copy(rights[i], held[i], right_sems.at[i]) for i in range(3)]

    @pl.when(step == 0)
    def _():
        for load in loads:
            load.start()

    def finish(of_slot, amount):
        for index in range(amount):
            pltpu.make_async_copy(
                results.at[of_slot, index], outs[0].at[0], sems.at[of_slot, index]
            ).wait()

    def amount_of(product):
        left, right = left_refs[product], held[table[product][3]]
        return left.shape[1] // size * (right.shape[1] // size)

    made = [product for product in range(products) for _ in range(table[product][1])]
    total = len(made)
    for product, (begin, times, first, which, fresh) in enumerate(table):

        @pl.when((step >= begin) & (step < begin + times))
        def _():
            left_ref, right = left_refs[product], held[which]
            rows, cols = left_ref.shape[1] // size, right.shape[1] // size
            if fresh:

                @pl.when(step == begin)
                def _():
                    loads[which].wait()

            for back in range(begin, begin + times):
                if back >= 2:

                    @pl.when(step == back)
                    def _():
                        finish(back % 2, amount_of(made[back - 2]))

            turned = left_ref[...].T
            for col in range(cols):
                result = contract(turned, right[:, pl.ds(col * size, size)], NN)
                for row in range(rows):
                    results[slot, row * cols + col] = result[
                        row * size : (row + 1) * size
                    ].astype(jnp.bfloat16)
            for row in range(rows):
                for col in range(cols):
                    block = first + ((step - begin) * rows + row) * cols + col
                    owner, within = block // owned, block % owned
                    place = owner // 2 * part_size + within % part_size
                    for part in range(parts):
                        for away in range(2):

                            @pl.when((within // part_size == part) & ((owner % 2 == core) == (away == 0)))
                            def _():
                                pltpu.make_async_copy(
                                    results.at[slot, row * cols + col],
                                    outs[2 * part + away].at[place],
                                    sems.at[slot, row * cols + col],
                                ).start()

    @pl.when(step == total - 1)
    def _():
        if total >= 2:
            finish((total - 2) % 2, amount_of(made[total - 2]))
        finish((total - 1) % 2, amount_of(made[total - 1]))


def weight_grads(lefts, rights, chosen, firsts, core, owned, part_size, dp_ways, size):
    tokens = lefts[0].shape[0]
    groups = [min(512, left.shape[1]) for left in lefts]
    times = [left.shape[1] // group for left, group in zip(lefts, groups)]
    begins = [sum(times[:index]) for index in range(len(times))]
    table = tuple(
        (begins[i], times[i], firsts[i], chosen[i], chosen[i] not in chosen[:i]) for i in range(len(lefts))
    )
    most = max(group // size * (rights[which].shape[1] // size) for group, which in zip(groups, chosen))
    parts = owned // part_size

    def left_spec(index):
        begin, last, group = begins[index], times[index] - 1, groups[index]
        return pl.BlockSpec((tokens, group), lambda i, core: (0, jnp.clip(i - begin, 0, last)))

    anywhere = pl.BlockSpec(memory_space=pl.ANY)
    half = jax.ShapeDtypeStruct((dp_ways // 2 * part_size, size, size), jnp.bfloat16)
    flops = sum(2 * tokens * left.shape[1] * rights[which].shape[1] for left, which in zip(lefts, chosen))
    return pl.pallas_call(
        functools.partial(weight_grad_kernel, table, owned, part_size),
        grid_spec=pltpu.PrefetchScalarGridSpec(
            num_scalar_prefetch=1,
            grid=(sum(times),),
            in_specs=[left_spec(index) for index in range(len(lefts))] + [anywhere] * 3,
            out_specs=[anywhere] * (2 * parts),
            scratch_shapes=[pltpu.VMEM(right.shape, jnp.bfloat16) for right in rights]
            + [
                pltpu.VMEM((2, most, size, size), jnp.bfloat16),
                pltpu.SemaphoreType.DMA((2, most)),
                pltpu.SemaphoreType.DMA((3,)),
            ],
        ),
        out_shape=[half] * (2 * parts),
        compiler_params=kernel_params(),
        cost_estimate=pl.CostEstimate(flops=flops, bytes_accessed=flops // 1000, transcendentals=0),
        name="weight_grads",
    )(core, *lefts, *rights)


def pair_sum_kernel(chip_ref, *refs):
    chips = len(refs) // 3
    for index in range(chips):
        total = refs[index][...].astype(jnp.float32) + refs[chips + index][...].astype(jnp.float32)
        refs[2 * chips + index][...] = total.astype(refs[2 * chips + index].dtype)


def pair_sum(kept, received, chip, chips):
    rows, size, _ = kept.shape
    part = rows // chips
    spec = lambda away: pl.BlockSpec(
        (part, size, size), lambda i, chip: (jnp.bitwise_xor(chip[0], away), 0, 0)
    )
    plain = pl.BlockSpec((part, size, size), lambda i, chip: (0, 0, 0))
    dtypes = [jnp.float32] + [jnp.bfloat16] * (chips - 1)
    return pl.pallas_call(
        pair_sum_kernel,
        grid_spec=pltpu.PrefetchScalarGridSpec(
            num_scalar_prefetch=1,
            grid=(1,),
            in_specs=[spec(away) for away in range(chips)] * 2,
            out_specs=[plain] * chips,
        ),
        out_shape=[jax.ShapeDtypeStruct((part, size, size), dtype) for dtype in dtypes],
        compiler_params=kernel_params(),
        cost_estimate=pl.CostEstimate(flops=rows * size * size, bytes_accessed=rows * size * size * 6, transcendentals=0),
        name="pair_sum",
    )(chip, *([kept] * chips), *([received] * chips))


def dot32(left_arg, right_arg):
    return jnp.dot(left_arg, right_arg, preferred_element_type=jnp.float32)


def two_terms(values):
    high = values.astype(jnp.bfloat16)
    return high, (values - high.astype(jnp.float32)).astype(jnp.bfloat16)


def product_three(left_arg, right_arg):
    left_high, left_low = two_terms(left_arg)
    right_high, right_low = two_terms(right_arg)
    return (
        dot32(left_high, right_high) + dot32(left_high, right_low) + dot32(left_low, right_high)
    )


def next_scaled(quarter, quarter16, scaled):
    square_rest = 2.0 * quarter + dot32(quarter16, quarter16)
    square16 = square_rest.astype(jnp.bfloat16)
    fourth_rest = 2.0 * square_rest + dot32(square16, square16)
    return scaled + product_three(fourth_rest, scaled)


def shampoo_kernel(
    grad_refs, left_ref, right_ref, master_ref, grad_out, left_out, right_out, new_out, scaled, roots
):
    count, size, _ = left_ref.shape
    identity = (
        lax.broadcasted_iota(jnp.int32, (size, size), 0)
        == lax.broadcasted_iota(jnp.int32, (size, size), 1)
    ).astype(jnp.float32)
    factors = []
    for block in range(count):
        total = grad_refs[0][block].astype(jnp.float32)
        for grad_ref in grad_refs[1:]:
            total = total + grad_ref[block].astype(jnp.float32)
        grad_out[block] = total
        grad = total.astype(jnp.bfloat16)
        for side, stat_ref, stat_out in ((0, left_ref, left_out), (1, right_ref, right_out)):
            dims = (((1 - side,), (1 - side,)), ((), ()))
            stat = DECAY * stat_ref[block] + lax.dot_general(
                grad, grad, dims, preferred_element_type=jnp.float32
            )
            stat_out[block] = stat
            squares = jnp.sum(stat * stat, axis=0, keepdims=True)
            norm = jnp.sqrt(jnp.sum(squares, axis=1, keepdims=True))
            factors.append(lax.rsqrt(jnp.sqrt(norm)))
            start = stat / norm
            quarter = (identity - start) * 0.25
            roots[2 * block + side] = identity + quarter
            scaled[2 * block + side] = next_scaled(quarter, quarter.astype(jnp.bfloat16), start)

    def iterate(step, carry):
        for item in range(2 * count):
            now = scaled[item]
            quarter = (identity - now) * 0.25
            quarter16 = quarter.astype(jnp.bfloat16)
            root = roots[item]
            roots[item] = root + dot32(root.astype(jnp.bfloat16), quarter16)
            scaled[item] = next_scaled(quarter, quarter16, now)
        return carry

    lax.fori_loop(0, ROOT_ITERS - 2, iterate, 0)
    for block in range(count):
        ends = []
        for side in range(2):
            item = 2 * block + side
            quarter16 = ((identity - scaled[item]) * 0.25).astype(jnp.bfloat16)
            root = roots[item]
            ends.append(root + dot32(root.astype(jnp.bfloat16), quarter16))
        grad = grad_out[block].astype(jnp.bfloat16)
        left_high, left_low = two_terms(ends[0])
        half = dot32(left_high, grad) + dot32(left_low, grad)
        rate = RATE_BLOCK * factors[2 * block] * factors[2 * block + 1]
        new_out[block] = master_ref[block] - rate * product_three(half, ends[1])


def shampoo(grads, left_stats, right_stats, master_blocks, first, priors):
    part, size, _ = grads[0].shape
    terms = len(grads)
    count = next(each for each in (3, 2, 1) if part % each == 0)
    start = first // count
    spec = pl.BlockSpec((count, size, size), lambda step: (step + start, 0, 0))
    own = pl.BlockSpec((count, size, size), lambda step: (step, 0, 0))
    result = jax.ShapeDtypeStruct(left_stats.shape, jnp.float32)
    held = [] if priors is None else list(priors)

    def kernel(*refs):
        shampoo_kernel(refs[:terms], *refs[terms : terms + 3], *refs[terms + 3 + len(held) :])

    return pl.pallas_call(
        kernel,
        grid=(part // count,),
        in_specs=[own] * terms + [spec] * 3 + [pl.BlockSpec(memory_space=pl.ANY)] * len(held),
        out_specs=[spec] * 4,
        out_shape=[result] * 4,
        input_output_aliases={terms + 3 + index: index for index in range(len(held))},
        scratch_shapes=[pltpu.VMEM((2 * count, size, size), jnp.float32)] * 2,
        compiler_params=kernel_params(),
        cost_estimate=pl.CostEstimate(
            flops=part * 180 * 2 * size**3, bytes_accessed=part * size * size * 30, transcendentals=0
        ),
        name="shampoo",
    )(*grads, left_stats, right_stats, master_blocks, *held)


def after(value, *earlier):
    return lax.optimization_barrier((value,) + earlier)[0]


def onward(part, axis):
    ways = lax.axis_size(axis)
    return lax.ppermute(part, axis, [(each, (each + 1) % ways) for each in range(ways)])


def swap(part, bits):
    ways = lax.axis_size("dp")
    return lax.ppermute(part, "dp", [(each, each ^ bits) for each in range(ways)])


def small_rows(values, ways):
    return jnp.pad(values, ((0, 0), (0, -values.shape[1] % 2048))).reshape(-1, 128)


def shards(
    tokens,
    cotangent,
    segments,
    subsets,
    packs,
    master_blocks,
    left_stats,
    right_stats,
    local_vecs,
    local_vec_stats,
    shared_vecs,
    shared_vec_stats,
):
    tp_ways = lax.axis_size("tp")
    dp_ways = lax.axis_size("dp")
    tp_rank = lax.axis_index("tp")
    tok_dev, model_width = tokens.shape
    group_tok = tok_dev * tp_ways
    pack_count, pack_len = segments.shape
    seg_width = subsets.shape[1]
    heads_dev = HEADS // tp_ways
    ff_dev = FF // tp_ways
    head_cols = heads_dev * HD
    owned, block_size, _ = master_blocks.shape
    block_rows = model_width // block_size
    first_out = block_rows * (3 * head_cols // block_size)
    first_in = first_out + head_cols // block_size * block_rows
    first_down = first_in + block_rows * (ff_dev // block_size)
    all_count = owned * dp_ways
    vec_rows = 3 * heads_dev + ff_dev // HD

    shared16 = shared_vecs.astype(jnp.bfloat16)
    shared_here = [(tp_rank, shared16)] + [
        (
            (tp_rank - step) % tp_ways,
            lax.ppermute(shared16, "tp", [(each, (each + step) % tp_ways) for each in range(tp_ways)]),
        )
        for step in range(1, tp_ways)
    ]
    shared_group = jnp.zeros((tp_ways,) + shared16.shape, jnp.bfloat16)
    for place, part in shared_here:
        shared_group = lax.dynamic_update_slice(shared_group, part[None], (place, 0, 0))
    vec_flat = jnp.concatenate([local_vecs.astype(jnp.bfloat16).reshape(-1), shared_group.reshape(-1)])
    vec_used = local_vecs.size
    shared_used = shared_group.size
    extra = jnp.pad(vec_flat, (0, EXTRA_ROWS * block_size - vec_flat.size)).reshape(EXTRA_ROWS, block_size)
    rows16 = jnp.concatenate([master_blocks.astype(jnp.bfloat16).reshape(-1, block_size), extra], 0)
    blocks = lax.all_gather(rows16, "dp", axis=0, tiled=True)

    token_parts = [tokens]
    for step in range(1, tp_ways):
        token_parts.append(onward(token_parts[-1], "tp"))

    gathered = blocks.reshape(dp_ways, -1, block_size)[:, owned * block_size :].reshape(dp_ways, -1)
    vec_values = (
        gathered[:, :vec_used].reshape(dp_ways, vec_rows, -1).transpose(1, 0, 2).reshape(vec_rows, HD)
    ).astype(jnp.float32)
    norm_params = (
        gathered[:, vec_used : vec_used + shared_used]
        .reshape(dp_ways, tp_ways, 6, -1)
        .transpose(2, 0, 1, 3)
        .reshape(6, model_width)
    ).astype(jnp.float32)
    bias_qkv = vec_values[: 3 * heads_dev].reshape(1, -1)
    bias_in = vec_values[3 * heads_dev :].reshape(1, -1)

    own_pos = tp_rank * tok_dev + jnp.arange(tok_dev)
    own_pack = own_pos // pack_len
    valid_own = (own_pack < packs[0]).astype(jnp.float32)
    owned_input_rows = tokens.astype(jnp.float32)
    owned_centred_scaled, owned_inverse_deviation = apply_layer_norm(owned_input_rows)

    group_pack = jnp.arange(group_tok) // pack_len
    lookup_key = group_pack * seg_width + segments.reshape(-1)
    onehot = lookup_key[:, None] == jnp.arange(pack_count * seg_width)[None, :]
    subset_tok = jnp.sum(jnp.where(onehot, subsets.reshape(-1)[None, :], 0), axis=1)
    weight = 0.5 + subset_tok.astype(jnp.float32) / (SUBSETS - 1)
    factor = (weight * (group_pack < packs[0]).astype(jnp.float32))[:, None]
    own_factor = lax.dynamic_slice_in_dim(factor, tp_rank * tok_dev, tok_dev, 0)
    seed16 = (cotangent.astype(jnp.float32) * own_factor).astype(jnp.bfloat16)
    out_bias_grad = jnp.sum(seed16, axis=0, dtype=jnp.float32)

    rank = tp_rank.astype(jnp.int32)[None]
    cosines, sines = turn_tables(pack_len, 128)
    cotangent_parts = [cotangent, onward(after(cotangent, token_parts[-1]), "tp")]
    qkv16, first_normed, second_normed, group_tokens = project_qkv(
        token_parts, rank, blocks, owned, norm_params, bias_qkv, cosines, sines, heads_dev
    )
    attended = attend(qkv16, segments, heads_dev)
    cotangent_parts.append(onward(after(cotangent_parts[-1], attended), "tp"))
    activated, slope, partial_value = feed_forward(
        second_normed, attended, blocks, owned, bias_in, (first_out, first_in, first_down)
    )
    while len(cotangent_parts) < tp_ways:
        cotangent_parts.append(onward(after(cotangent_parts[-1], slope), "tp"))

    back_args = (
        tp_ways, rank, factor, slope, group_tokens, blocks, owned, norm_params, (first_out, first_in, first_down), head_cols,
    )
    early = feed_back(cotangent_parts[:-1], 0, *back_args, ())
    late = feed_back(cotangent_parts[-1:], tp_ways - 1, *back_args, early[:4])
    seed_all, d_attended, d_hidden16, dz_part = late[:4]
    branch = lax.psum_scatter(
        after(partial_value, cotangent_parts[-1]), "tp", scatter_dimension=0, tiled=True
    )
    output = (
        valid_own[:, None]
        * (owned_input_rows + branch.astype(jnp.float32) + norm_params[4] + norm_params[5])
    ).astype(jnp.bfloat16)
    d_qkv16 = attend_back(qkv16, d_attended, segments, cosines, sines, heads_dev)
    dz16, first_sums, qkv_sums = qkv_back(d_qkv16, dz_part, group_tokens, blocks, owned, norm_params)

    dz_rows = lambda back: lax.dynamic_slice_in_dim(dz16, (tp_rank - back) % tp_ways * tok_dev, tok_dev, 0)
    moving = onward(dz_rows(1), "tp")

    parts = next(each for each in (4, 3, 2, 1) if owned % each == 0)
    part_size = owned // parts
    dp_rank = lax.axis_index("dp").astype(jnp.int32)
    halves = weight_grads(
        (first_normed, attended, second_normed, activated),
        (d_qkv16, seed_all, d_hidden16),
        (0, 1, 2, 1),
        (0, first_out, first_in, first_down),
        (dp_rank % 2)[None],
        owned,
        part_size,
        dp_ways,
        block_size,
    )
    results = None
    last = None
    back = 2

    def pass_on(moving, back):
        total = moving.astype(jnp.float32) + dz_rows(back).astype(jnp.float32)
        return total if back == tp_ways else onward(total.astype(jnp.bfloat16), "tp")

    moving = pass_on(after(moving, halves[0]), back)
    terms = []
    for part in range(parts):
        kept, away = halves[2 * part : 2 * part + 2]
        received = swap(away, 1)
        if dp_ways == 8:
            sums = pair_sum(kept, received, (dp_rank // 2)[None], dp_ways // 2)
            if last is not None:
                sums = [sums[0]] + [after(each, last) for each in sums[1:]]
            terms.append([sums[0]] + [swap(sums[bits], 2 * bits) for bits in range(1, 4)])
            last = terms[-1][3]
        else:
            total = (kept.astype(jnp.float32) + received.astype(jnp.float32)).astype(jnp.bfloat16)
            cores = [[each for each in range(dp_ways) if each % 2 == core] for core in range(2)]
            terms.append(
                [lax.psum_scatter(total, "dp", scatter_dimension=0, tiled=True, axis_index_groups=cores)]
            )
    for part in range(parts):
        results = shampoo(
            terms[part], left_stats, right_stats, master_blocks, part * part_size, results
        )
        while back < tp_ways and (back < part + 3 or part == parts - 1):
            back += 1
            moving, first_result = lax.optimization_barrier((moving, results[0]))
            results = [first_result] + list(results[1:])
            moving = pass_on(moving, back)
    norm_input_gradient = moving
    own_grads, left_new, right_new, new_blocks = results

    average_gradient = jnp.mean(norm_input_gradient, axis=-1, keepdims=True)
    average_projection = jnp.mean(
        norm_input_gradient * owned_centred_scaled, axis=-1, keepdims=True
    )
    input_grad = seed16.astype(jnp.float32) + owned_inverse_deviation * (
        norm_input_gradient - average_gradient - owned_centred_scaled * average_projection
    )

    shared_local = jnp.concatenate(
        [
            jnp.sum(first_sums.reshape(2, 8, model_width), axis=1),
            jnp.sum((early[4] + late[4]).reshape(2, 8, model_width), axis=1),
            out_bias_grad[None],
        ],
        0,
    )
    vecs_local = jnp.concatenate(
        [
            jnp.sum(qkv_sums, axis=0).reshape(3 * heads_dev, HD),
            jnp.sum(early[5] + late[5], axis=0).reshape(ff_dev // HD, HD),
        ],
        0,
    )
    small = jnp.concatenate(
        [
            shared_local.reshape(5, dp_ways, -1).transpose(1, 0, 2).reshape(dp_ways, -1),
            vecs_local.reshape(vec_rows, dp_ways, -1).transpose(1, 0, 2).reshape(dp_ways, -1),
        ],
        1,
    )
    small_own = lax.psum_scatter(
        small_rows(small, dp_ways), "dp", scatter_dimension=0, tiled=True
    ).reshape(-1)
    shared_size = 5 * model_width // dp_ways
    own_vec_grads = small_own[shared_size : small.shape[1]].reshape(vec_rows, HD // dp_ways)
    shared_part = small_own[:shared_size].reshape(5, tp_ways, -1).transpose(1, 0, 2)
    shared_own = lax.psum_scatter(
        small_rows(shared_part.reshape(tp_ways, -1), tp_ways), "tp", scatter_dimension=0, tiled=True
    ).reshape(-1)
    shared_own = shared_own[: shared_size // tp_ways].reshape(5, -1)
    shared_grads = jnp.concatenate([shared_own, shared_own[4:]], 0)
    local_stat_new = DECAY * local_vec_stats + own_vec_grads * own_vec_grads
    local_new = local_vecs - RATE_VEC * own_vec_grads * lax.rsqrt(local_stat_new)
    shared_stat_new = DECAY * shared_vec_stats + shared_grads * shared_grads
    shared_new = shared_vecs - RATE_VEC * shared_grads * lax.rsqrt(shared_stat_new)
    return (
        output,
        input_grad,
        own_grads,
        left_new,
        right_new,
        new_blocks,
        own_vec_grads,
        local_stat_new,
        local_new,
        shared_grads,
        shared_stat_new,
        shared_new,
    )


def solution(mesh):
    placed = (
        P(("dp", "tp"), None),
        P(("dp", "tp"), None),
        P("dp", None),
        P("dp", None),
        P("dp"),
        P(("dp", "tp"), None, None),
        P(("dp", "tp"), None, None),
        P(("dp", "tp"), None, None),
        P("tp", "dp"),
        P("tp", "dp"),
        P(None, ("dp", "tp")),
        P(None, ("dp", "tp")),
    )
    return jax.shard_map(
        shards,
        mesh=mesh,
        in_specs=placed,
        out_specs=(
            P(("dp", "tp"), None),
            P(("dp", "tp"), None),
            P(("dp", "tp"), None, None),
            P(("dp", "tp"), None, None),
            P(("dp", "tp"), None, None),
            P(("dp", "tp"), None, None),
            P("tp", "dp"),
            P("tp", "dp"),
            P("tp", "dp"),
            P(None, ("dp", "tp")),
            P(None, ("dp", "tp")),
            P(None, ("dp", "tp")),
        ),
        check_vma=False,
    )
```

```python
import functools
import math

import jax
import jax.numpy as jnp
from jax import lax
from jax.experimental import pallas as pl
from jax.experimental.pallas import tpu as pltpu
from jax.sharding import PartitionSpec as P

HEADS = 8
HD = 256
ROT = 64
FF = 8192
SUBSETS = 22
ROOT_ITERS = 8


EPS_NORM = 1e-05
DECAY = 0.5
RATE_BLOCK = 0.6
RATE_VEC = 0.2
NEG_FILL = -1e30
DOC_MAX = 512
HALF_ROOT = 0.7071067811865476
DENSITY_SCALE = 0.3989422804014327


def apply_layer_norm(values):
    mean_val = jnp.mean(values, axis=-1, keepdims=True)
    centred = values - mean_val
    variance = jnp.mean(centred * centred, axis=-1, keepdims=True)
    inv_std = lax.rsqrt(variance + EPS_NORM)
    return (centred * inv_std, inv_std)


def to_blocks(matrix, block_size):
    block_rows = matrix.shape[0] // block_size
    block_cols = matrix.shape[1] // block_size
    return (
        matrix.reshape(block_rows, block_size, block_cols, block_size)
        .transpose(0, 2, 1, 3)
        .reshape(block_rows * block_cols, block_size, block_size)
    )


EXTRA_ROWS = 16
COST_PART = 16
FEED_BACK_TILE = 512
VMEM_LIMIT = 60 << 20
NN = (((1,), (0,)), ((), ()))
NT = (((1,), (1,)), ((), ()))
TN = (((0,), (0,)), ((), ()))


def contract(left_arg, right_arg, dims):
    return lax.dot_general(left_arg, right_arg, dims, preferred_element_type=jnp.float32)


def kernel_params():
    return pltpu.CompilerParams(vmem_limit_bytes=VMEM_LIMIT)


def kernel_cost(flops, bytes_accessed, transcendentals):
    return pl.CostEstimate(
        flops=flops // COST_PART, bytes_accessed=bytes_accessed // COST_PART, transcendentals=transcendentals
    )


def block_row(index, owned, size):
    return index // owned * (owned * size + EXTRA_ROWS) + index % owned * size


def block_copies(blocks_ref, owned, first, rows, cols, target, sems):
    size = blocks_ref.shape[-1]
    return [
        pltpu.make_async_copy(
            blocks_ref.at[pl.ds(block_row(first + row * cols + col, owned, size), size), :],
            target.at[pl.ds(row * size, size), pl.ds(col * size, size)],
            sems.at[row * cols + col],
        )
        for row in range(rows)
        for col in range(cols)
    ]


def begin_copies(copies):
    @pl.when(pl.program_id(0) == 0)
    def _():
        for copy in copies:
            copy.start()


def end_copies(copies):
    @pl.when(pl.program_id(0) == 0)
    def _():
        for copy in copies:
            copy.wait()


def turn(values, cosines, sines):
    lane = lax.broadcasted_iota(jnp.int32, values.shape, 1)
    half = ROT // 2
    wide = values.shape[1]
    swapped = jnp.where(
        lane < half, pltpu.roll(values, wide - half, 1), pltpu.roll(values, half, 1)
    )
    return values * cosines + swapped * sines


def turn_tables(pack_len, lanes):
    half = ROT // 2
    positions = jnp.arange(pack_len).astype(jnp.float32)
    freqs = 10000.0 ** (-(jnp.arange(half).astype(jnp.float32) * 2.0) / ROT)
    angles = positions[:, None] * freqs[None, :]
    cosines = jnp.cos(angles)
    sines = jnp.sin(angles)
    rest = jnp.zeros((pack_len, lanes - ROT), jnp.float32)
    return (
        jnp.concatenate([cosines, cosines, rest + 1.0], -1),
        jnp.concatenate([-sines, sines, rest], -1),
    )


def normed_rows(rows):
    mean = jnp.mean(rows, axis=1, keepdims=True)
    centred = rows - mean
    variance = jnp.mean(centred * centred, axis=1, keepdims=True)
    return mean, lax.rsqrt(variance + EPS_NORM)


def part_copies(part_refs, held, sems):
    return [
        pltpu.make_async_copy(part, held.at[index], sems.at[index])
        for index, part in enumerate(part_refs)
    ]


def await_part(copies, per_part):
    step = pl.program_id(0)
    for index, copy in enumerate(copies):

        @pl.when(step == index * per_part)
        def _():
            copy.wait()


def qkv_kernel(heads, owned, parts, rank_ref, *refs):
    part_refs = refs[:parts]
    blocks_ref, norm_ref, bias_ref, cos_ref, sin_ref = refs[parts : parts + 5]
    outs, (normed, weight, held, sems, part_sems) = refs[parts + 5 : parts + 12], refs[parts + 12 :]
    qkv_ref, first_turned, second_ref, second_turned, tokens_ref, mean_ref, inverse_ref = outs
    size = blocks_ref.shape[-1]
    copies = block_copies(blocks_ref, owned, 0, weight.shape[0] // size, weight.shape[1] // size, weight, sems)
    moves = part_copies(part_refs, held, part_sems)
    begin_copies(moves + copies)
    await_part(moves, 1)
    own = held[pl.program_id(0)]
    tokens_ref[...] = own
    rows = own.astype(jnp.float32)
    mean, inverse = normed_rows(rows)
    mean_ref[...] = mean
    inverse_ref[...] = inverse
    for col in range(rows.shape[1] // size):
        cols = pl.ds(col * size, size)
        scaled = (own[:, col * size : (col + 1) * size].astype(jnp.float32) - mean) * inverse
        second = (scaled * norm_ref[2:3, cols] + norm_ref[3:4, cols]).astype(jnp.bfloat16)
        second_ref[:, cols] = second
        second_turned[cols, :] = second.T
        first = (scaled * norm_ref[0:1, cols] + norm_ref[1:2, cols]).astype(jnp.bfloat16)
        normed[:, cols] = first
        first_turned[cols, :] = first.T
    end_copies(copies)
    lanes = cos_ref.shape[1]
    for head in range(heads):
        for part in range(3):
            cols = pl.ds((head * 3 + part) * HD, HD)
            result = contract(normed[...], weight[:, cols], NN) + bias_ref[:, cols]
            if part < 2:
                first = turn(result[:, :lanes], cos_ref[...], sin_ref[...])
                result = jnp.concatenate([first, result[:, lanes:]], 1)
            if part == 0:
                result = result * (1.0 / math.sqrt(HD))
            qkv_ref[:, cols] = result.astype(jnp.bfloat16)


def project_qkv(parts, rank, blocks, owned, norm_params, bias, cosines, sines, heads):
    ways = len(parts)
    tile, width = parts[0].shape
    tokens = ways * tile
    size = blocks.shape[-1]
    pack_len, lanes = cosines.shape
    cols = 3 * heads * HD
    per_pack = pack_len // tile
    place = lambda i, rank: (rank[0] - i + ways) % ways
    row = lambda n: pl.BlockSpec((tile, n), lambda i, rank: (place(i, rank), 0))
    table = pl.BlockSpec((tile, lanes), lambda i, rank: (place(i, rank) % per_pack, 0))
    anywhere = pl.BlockSpec(memory_space=pl.ANY)
    wide = jax.ShapeDtypeStruct((tokens, width), jnp.bfloat16)
    tall = jax.ShapeDtypeStruct((width, tokens), jnp.bfloat16)
    single = jax.ShapeDtypeStruct((tokens, 1), jnp.float32)
    turned = pl.BlockSpec((width, tile), lambda i, rank: (0, place(i, rank)))
    return pl.pallas_call(
        functools.partial(qkv_kernel, heads, owned, ways),
        grid_spec=pltpu.PrefetchScalarGridSpec(
            num_scalar_prefetch=1,
            grid=(ways,),
            in_specs=[anywhere] * (ways + 1)
            + [
                pl.BlockSpec(norm_params.shape, lambda i, rank: (0, 0)),
                pl.BlockSpec((1, cols), lambda i, rank: (0, 0)),
                table,
                table,
            ],
            out_specs=[row(cols), turned, row(width), turned, row(width), row(1), row(1)],
            scratch_shapes=[
                pltpu.VMEM((tile, width), jnp.bfloat16),
                pltpu.VMEM((width, cols), jnp.bfloat16),
                pltpu.VMEM((ways, tile, width), jnp.bfloat16),
                pltpu.SemaphoreType.DMA((width // size * (cols // size),)),
                pltpu.SemaphoreType.DMA((ways,)),
            ],
        ),
        out_shape=[jax.ShapeDtypeStruct((tokens, cols), jnp.bfloat16), tall, wide, tall, wide, single, single],
        compiler_params=kernel_params(),
        cost_estimate=kernel_cost(
            flops=2 * tokens * width * cols, bytes_accessed=tokens * (4 * width + cols) * 2 + width * cols * 2, transcendentals=0
        ),
        name="qkv",
    )(rank, *parts, blocks, norm_params, bias, cosines, sines)


def attend_kernel(query_ref, key_ref, value_ref, seg_row, seg_col, out_ref, turned_ref):
    length = key_ref.shape[0]
    step = 256
    for start in range(0, length, step):
        first = max(0, start - DOC_MAX)
        stop = start + step
        scores = contract(query_ref[start:stop, :], key_ref[first:stop, :], NT)
        row = lax.broadcasted_iota(jnp.int32, scores.shape, 0) + start
        col = lax.broadcasted_iota(jnp.int32, scores.shape, 1) + first
        allowed = (col <= row) & (seg_col[0, start:stop, :] == seg_row[0, :, first:stop])
        masked = jnp.where(allowed, scores, NEG_FILL)
        exp_terms = jnp.exp(masked - jnp.max(masked, axis=1, keepdims=True))
        probs = exp_terms * (1.0 / jnp.sum(exp_terms, axis=1, keepdims=True))
        result = contract(probs.astype(jnp.bfloat16), value_ref[first:stop, :], NN).astype(jnp.bfloat16)
        out_ref[start:stop, :] = result
        turned_ref[:, start:stop] = result.T


def attend(qkv, segments, heads):
    packs, length = segments.shape
    part = lambda which: pl.BlockSpec((length, HD), lambda p, h: (p, h * 3 + which))
    return pl.pallas_call(
        attend_kernel,
        grid=(packs, heads),
        in_specs=[
            part(0),
            part(1),
            part(2),
            pl.BlockSpec((1, 1, length), lambda p, h: (p, 0, 0)),
            pl.BlockSpec((1, length, 1), lambda p, h: (p, 0, 0)),
        ],
        out_specs=[
            pl.BlockSpec((length, HD), lambda p, h: (p, h)),
            pl.BlockSpec((HD, length), lambda p, h: (h, p)),
        ],
        out_shape=[
            jax.ShapeDtypeStruct((packs * length, heads * HD), jnp.bfloat16),
            jax.ShapeDtypeStruct((heads * HD, packs * length), jnp.bfloat16),
        ],
        compiler_params=kernel_params(),
        cost_estimate=kernel_cost(
            flops=packs * heads * length * length * HD * 3, bytes_accessed=packs * length * heads * HD * 8, transcendentals=0
        ),
        name="attend",
    )(qkv, qkv, qkv, segments[:, None, :], segments[:, :, None])


def attend_back_kernel(
    query_ref, key_ref, value_ref, d_out_ref, seg_row, seg_col, cos_ref, sin_ref, grad_ref, d_key, d_value
):
    length = key_ref.shape[0]
    step = 256
    lanes = cos_ref.shape[1]
    d_key[...] = jnp.zeros_like(d_key)
    d_value[...] = jnp.zeros_like(d_value)
    for start in range(0, length, step):
        first = max(0, start - DOC_MAX)
        stop = start + step
        query = query_ref[start:stop, :]
        d_out = d_out_ref[start:stop, :]
        keys = key_ref[first:stop, :]
        scores = contract(keys, query, NT)
        key_pos = lax.broadcasted_iota(jnp.int32, scores.shape, 0) + first
        query_pos = lax.broadcasted_iota(jnp.int32, scores.shape, 1) + start
        allowed = (key_pos <= query_pos) & (seg_col[0, first:stop, :] == seg_row[0, :, start:stop])
        masked = jnp.where(allowed, scores, NEG_FILL)
        exp_terms = jnp.exp(masked - jnp.max(masked, axis=0, keepdims=True))
        probs = exp_terms * (1.0 / jnp.sum(exp_terms, axis=0, keepdims=True))
        d_probs = contract(value_ref[first:stop, :], d_out, NT)
        row_dot = jnp.sum(probs * d_probs, axis=0, keepdims=True)
        d_scores = (probs * (d_probs - row_dot)).astype(jnp.bfloat16)
        d_value[first:stop, :] += contract(probs.astype(jnp.bfloat16), d_out, NN)
        d_key[first:stop, :] += contract(d_scores, query, NN)
        d_query = contract(d_scores, keys, TN) * (1.0 / math.sqrt(HD))
        back = turn(d_query[:, :lanes], cos_ref[start:stop, :], -sin_ref[start:stop, :])
        grad_ref[start:stop, :lanes] = back.astype(jnp.bfloat16)
        grad_ref[start:stop, lanes:HD] = d_query[:, lanes:].astype(jnp.bfloat16)
    back = turn(d_key[:, :lanes], cos_ref[...], -sin_ref[...])
    grad_ref[:, HD : HD + lanes] = back.astype(jnp.bfloat16)
    grad_ref[:, HD + lanes : 2 * HD] = d_key[:, lanes:].astype(jnp.bfloat16)
    grad_ref[:, 2 * HD :] = d_value[...].astype(jnp.bfloat16)


def attend_back(qkv, d_attended, segments, cosines, sines, heads):
    packs, length = segments.shape
    lanes = cosines.shape[1]
    part = lambda which: pl.BlockSpec((length, HD), lambda p, h: (p, h * 3 + which))
    table = pl.BlockSpec((length, lanes), lambda p, h: (0, 0))
    return pl.pallas_call(
        attend_back_kernel,
        grid=(packs, heads),
        in_specs=[
            part(0),
            part(1),
            part(2),
            pl.BlockSpec((length, HD), lambda p, h: (p, h)),
            pl.BlockSpec((1, 1, length), lambda p, h: (p, 0, 0)),
            pl.BlockSpec((1, length, 1), lambda p, h: (p, 0, 0)),
            table,
            table,
        ],
        out_specs=pl.BlockSpec((length, 3 * HD), lambda p, h: (p, h)),
        out_shape=jax.ShapeDtypeStruct((packs * length, 3 * heads * HD), jnp.bfloat16),
        scratch_shapes=[pltpu.VMEM((length, HD), jnp.float32)] * 2,
        compiler_params=kernel_params(),
        cost_estimate=kernel_cost(
            flops=packs * heads * length * length * HD * 7, bytes_accessed=packs * length * heads * HD * 16, transcendentals=0
        ),
        name="attend_back",
    )(qkv, qkv, qkv, d_attended, segments[:, None, :], segments[:, :, None], cosines, sines)


def feed_kernel(
    offsets, owned, x_ref, attended_ref, blocks_ref, bias_ref, turned_ref, slope_ref, out_ref, act_ref, w_in, w_down, sems_in, sems_down
):
    size = blocks_ref.shape[-1]
    width, hidden_units = w_in.shape
    inner = hidden_units // size
    first_out, first_in, first_down = offsets
    head_rows = attended_ref.shape[1] // size
    outer = width // size
    copies_in = block_copies(blocks_ref, owned, first_in, outer, inner, w_in, sems_in)
    copies_down = block_copies(blocks_ref, owned, first_down, inner, outer, w_down.at[pl.ds(0, hidden_units)], sems_down)
    copies_down += block_copies(
        blocks_ref,
        owned,
        first_out,
        head_rows,
        outer,
        w_down.at[pl.ds(hidden_units, head_rows * size)],
        sems_down.at[pl.ds(inner * outer, head_rows * outer)],
    )
    begin_copies(copies_in + copies_down)
    end_copies(copies_in)
    values = x_ref[...]
    for col in range(inner):
        cols = pl.ds(col * size, size)
        hidden = contract(values, w_in[:, cols], NN) + bias_ref[:, cols]
        cdf = 0.5 + 0.5 * lax.erf(hidden * HALF_ROOT)
        density = jnp.exp(-0.5 * hidden * hidden) * DENSITY_SCALE
        activated = (hidden * cdf).astype(jnp.bfloat16)
        act_ref[:, cols] = activated
        turned_ref[cols, :] = activated.T
        slope_ref[:, cols] = (cdf + hidden * density).astype(jnp.bfloat16)
    end_copies(copies_down)
    for col in range(outer):
        cols = pl.ds(col * size, size)
        out_ref[:, cols] = (
            contract(act_ref[...], w_down[:hidden_units, cols], NN)
            + contract(attended_ref[...], w_down[hidden_units:, cols], NN)
        ).astype(jnp.bfloat16)


def feed_forward(normed, attended, blocks, owned, bias, offsets):
    tokens, width = normed.shape
    size = blocks.shape[-1]
    hidden_units = bias.shape[1]
    head_cols = attended.shape[1]
    tile = 512
    row = lambda cols: pl.BlockSpec((tile, cols), lambda i: (i, 0))
    inner, outer = hidden_units // size, width // size
    return pl.pallas_call(
        functools.partial(feed_kernel, offsets, owned),
        grid=(tokens // tile,),
        in_specs=[
            row(width),
            row(head_cols),
            pl.BlockSpec(memory_space=pl.ANY),
            pl.BlockSpec((1, hidden_units), lambda i: (0, 0)),
        ],
        out_specs=[
            pl.BlockSpec((hidden_units, tile), lambda i: (0, i)), row(hidden_units), row(width),
        ],
        out_shape=[
            jax.ShapeDtypeStruct((hidden_units, tokens), jnp.bfloat16),
            jax.ShapeDtypeStruct((tokens, hidden_units), jnp.bfloat16),
            jax.ShapeDtypeStruct((tokens, width), jnp.bfloat16),
        ],
        scratch_shapes=[
            pltpu.VMEM((tile, hidden_units), jnp.bfloat16),
            pltpu.VMEM((width, hidden_units), jnp.bfloat16),
            pltpu.VMEM((hidden_units + head_cols, width), jnp.bfloat16),
            pltpu.SemaphoreType.DMA((inner * outer,)),
            pltpu.SemaphoreType.DMA((inner * outer + head_cols // size * outer,)),
        ],
        compiler_params=kernel_params(),
        cost_estimate=kernel_cost(
            flops=2 * tokens * width * (2 * hidden_units + head_cols), bytes_accessed=tokens * width * 10 + width * hidden_units * 4, transcendentals=0
        ),
        name="feed",
    )(normed, attended, blocks, bias)


def column_sum(values):
    rows, cols = values.shape
    return jnp.sum(values.reshape(rows // 8, 8, cols), axis=0)


def feed_back_kernel(offsets, owned, first_part, parts, held_count, rank_ref, *refs):
    part_refs = refs[:parts]
    factor_ref, slope_ref, tokens_ref, mean_ref, inverse_ref, blocks_ref, norm_ref = refs[parts : parts + 7]
    (
        seed_ref, d_attended_ref, d_hidden_ref, dz_ref, norm_sums, hidden_sums,
        w_in, w_down, w_out, held, sems_in, sems_down, sems_out, part_sems,
    ) = refs[parts + 7 + held_count :]
    size = blocks_ref.shape[-1]
    width, hidden_units = w_in.shape
    inner, outer = hidden_units // size, width // size
    first_out, first_in, first_down = offsets
    tile = seed_ref.shape[0]
    per_part = held.shape[1] // tile
    moves = part_copies(part_refs, held, part_sems)
    copies_out = block_copies(blocks_ref, owned, first_out, w_out.shape[0] // size, outer, w_out, sems_out)
    copies_down = block_copies(blocks_ref, owned, first_down, inner, outer, w_down, sems_down)
    copies_in = block_copies(blocks_ref, owned, first_in, outer, inner, w_in, sems_in)
    begin_copies(moves + copies_out + copies_down + copies_in)

    @pl.when(pl.program_id(0) == 0)
    def _():
        norm_sums[...] = jnp.zeros_like(norm_sums)
        hidden_sums[...] = jnp.zeros_like(hidden_sums)

    await_part(moves, per_part)
    step = pl.program_id(0)
    cotangent = held[step // per_part, pl.ds(pl.multiple_of(step % per_part * tile, tile), tile), :]
    seed_ref[...] = (cotangent.astype(jnp.float32) * factor_ref[...]).astype(jnp.bfloat16)
    seed = seed_ref[...]
    if first_part == 0:

        @pl.when(step < per_part)
        def _():
            norm_sums[16:24, :] += column_sum(seed_ref[...].astype(jnp.float32))

    end_copies(copies_out)
    d_attended_ref[...] = contract(seed, w_out[...], NT).astype(jnp.bfloat16)
    end_copies(copies_down)
    for col in range(inner):
        cols = pl.ds(col * size, size)
        d_act = contract(seed_ref[...], w_down[cols, :], NT)
        d_hidden = (d_act * slope_ref[:, cols].astype(jnp.float32)).astype(jnp.bfloat16)
        d_hidden_ref[:, cols] = d_hidden
        hidden_sums[:, cols] += column_sum(d_hidden.astype(jnp.float32))
    end_copies(copies_in)
    mean, inverse = mean_ref[...], inverse_ref[...]
    for col in range(outer):
        cols = pl.ds(col * size, size)
        scaled = (tokens_ref[:, cols].astype(jnp.float32) - mean) * inverse
        second = contract(d_hidden_ref[...], w_in[cols, :], NT)
        dz_ref[:, cols] = second * norm_ref[2:3, cols]
        norm_sums[0:8, cols] += column_sum(second * scaled)
        norm_sums[8:16, cols] += column_sum(second)


def feed_back(parts, first_part, ways, rank, factor, slope, group_tokens, mean, inverse, blocks, owned, norm_params, offsets, head_cols, priors):
    chunk, width = parts[0].shape
    tokens = ways * chunk
    size = blocks.shape[-1]
    hidden_units = slope.shape[1]
    tile = min(FEED_BACK_TILE, chunk)
    per_part = chunk // tile
    inner, outer = hidden_units // size, width // size
    place = lambda i, rank: (rank[0] - first_part - i // per_part + ways) % ways * per_part + i % per_part
    row = lambda n: pl.BlockSpec((tile, n), lambda i, rank: (place(i, rank), 0))
    whole = lambda rows, cols: pl.BlockSpec((rows, cols), lambda i, rank: (0, 0))
    anywhere = pl.BlockSpec(memory_space=pl.ANY)
    count = len(parts)
    rows = count * chunk
    return pl.pallas_call(
        functools.partial(feed_back_kernel, offsets, owned, first_part, count, len(priors)),
        grid_spec=pltpu.PrefetchScalarGridSpec(
            num_scalar_prefetch=1,
            grid=(count * per_part,),
            in_specs=[anywhere] * count
            + [row(1), row(hidden_units), row(width), row(1), row(1), anywhere]
            + [whole(norm_params.shape[0], width)]
            + [anywhere] * len(priors),
            out_specs=[
                row(width), row(head_cols), row(hidden_units), row(width), whole(24, width), whole(8, hidden_units),
            ],
            scratch_shapes=[
                pltpu.VMEM((width, hidden_units), jnp.bfloat16),
                pltpu.VMEM((hidden_units, width), jnp.bfloat16),
                pltpu.VMEM((head_cols, width), jnp.bfloat16),
                pltpu.VMEM((count, chunk, width), jnp.bfloat16),
                pltpu.SemaphoreType.DMA((inner * outer,)),
                pltpu.SemaphoreType.DMA((inner * outer,)),
                pltpu.SemaphoreType.DMA((head_cols // size * outer,)),
                pltpu.SemaphoreType.DMA((count,)),
            ],
        ),
        out_shape=[
            jax.ShapeDtypeStruct((tokens, width), jnp.bfloat16),
            jax.ShapeDtypeStruct((tokens, head_cols), jnp.bfloat16),
            jax.ShapeDtypeStruct((tokens, hidden_units), jnp.bfloat16),
            jax.ShapeDtypeStruct((tokens, width), jnp.float32),
            jax.ShapeDtypeStruct((24, width), jnp.float32),
            jax.ShapeDtypeStruct((8, hidden_units), jnp.float32),
        ],
        input_output_aliases={1 + count + 7 + index: index for index in range(len(priors))},
        compiler_params=kernel_params(),
        cost_estimate=kernel_cost(
            flops=2 * rows * width * (2 * hidden_units + head_cols), bytes_accessed=rows * width * 14 + width * hidden_units * 4, transcendentals=0
        ),
        name="feed_back",
    )(rank, *parts, factor, slope, group_tokens, mean, inverse, blocks, norm_params, *priors)


def qkv_back_kernel(owned, d_qkv_ref, part_ref, tokens_ref, mean_ref, inverse_ref, blocks_ref, norm_ref, dz_ref, norm_sums, qkv_sums, w_qkv, sems):
    size = blocks_ref.shape[-1]
    outer = w_qkv.shape[0] // size
    copies = block_copies(blocks_ref, owned, 0, outer, w_qkv.shape[1] // size, w_qkv, sems)
    begin_copies(copies)

    @pl.when(pl.program_id(0) == 0)
    def _():
        norm_sums[...] = jnp.zeros_like(norm_sums)
        qkv_sums[...] = jnp.zeros_like(qkv_sums)

    qkv_sums[...] += column_sum(d_qkv_ref[...].astype(jnp.float32))
    mean, inverse = mean_ref[...], inverse_ref[...]
    end_copies(copies)
    for col in range(outer):
        cols = pl.ds(col * size, size)
        scaled = (tokens_ref[:, cols].astype(jnp.float32) - mean) * inverse
        first = contract(d_qkv_ref[...], w_qkv[cols, :], NT)
        dz_ref[:, cols] = (part_ref[:, cols] + first * norm_ref[0:1, cols]).astype(jnp.bfloat16)
        norm_sums[0:8, cols] += column_sum(first * scaled)
        norm_sums[8:16, cols] += column_sum(first)


def qkv_back(d_qkv, dz_part, group_tokens, mean, inverse, blocks, owned, norm_params):
    tokens, qkv_cols = d_qkv.shape
    width = dz_part.shape[1]
    size = blocks.shape[-1]
    tile = 512
    row = lambda cols: pl.BlockSpec((tile, cols), lambda i: (i, 0))
    whole = lambda rows, cols: pl.BlockSpec((rows, cols), lambda i: (0, 0))
    outer = width // size
    return pl.pallas_call(
        functools.partial(qkv_back_kernel, owned),
        grid=(tokens // tile,),
        in_specs=[
            row(qkv_cols), row(width), row(width), row(1), row(1), pl.BlockSpec(memory_space=pl.ANY), whole(norm_params.shape[0], width),
        ],
        out_specs=[row(width), whole(16, width), whole(8, qkv_cols)],
        out_shape=[
            jax.ShapeDtypeStruct((tokens, width), jnp.bfloat16),
            jax.ShapeDtypeStruct((16, width), jnp.float32),
            jax.ShapeDtypeStruct((8, qkv_cols), jnp.float32),
        ],
        scratch_shapes=[
            pltpu.VMEM((width, qkv_cols), jnp.bfloat16),
            pltpu.SemaphoreType.DMA((outer * (qkv_cols // size),)),
        ],
        compiler_params=kernel_params(),
        cost_estimate=kernel_cost(
            flops=2 * tokens * width * qkv_cols, bytes_accessed=tokens * width * 11, transcendentals=0
        ),
        name="qkv_back",
    )(d_qkv, dz_part, group_tokens, mean, inverse, blocks, norm_params)


def weight_grad_kernel(steps, core_ref, *refs):
    lefts, rights, outs = refs[:4], refs[4:7], refs[7:9]
    rows_held, rights_held, (results, left_sems, right_sems, sems) = refs[9], refs[10:13], refs[13:]
    size = results.shape[-1]
    core = core_ref[0]

    def left_copy(index):
        left, first, rows, _, _, _ = steps[index]
        return pltpu.make_async_copy(
            lefts[left].at[pl.ds(first, rows), :],
            rows_held.at[index % 2, pl.ds(0, rows), :],
            left_sems.at[index % 2],
        )

    def right_copy(right, first):
        held = rights_held[right]
        return pltpu.make_async_copy(
            rights[right].at[:, pl.ds(first, held.shape[1])], held, right_sems.at[right]
        )

    def finish(index):
        for place in range(len(steps[index][5])):
            pltpu.make_async_copy(
                results.at[index % 2, place], outs[0].at[0], sems.at[index % 2, place]
            ).wait()

    order = []
    for step in steps:
        if step[3:5] not in order:
            order.append(step[3:5])
    left_copy(0).start()
    for right in order:
        right_copy(*right).start()
    for index, (left, first, rows, right, right_first, places) in enumerate(steps):
        left_copy(index).wait()
        if index + 1 < len(steps):
            left_copy(index + 1).start()
        if all(step[3:5] != (right, right_first) for step in steps[:index]):
            right_copy(right, right_first).wait()
        if index >= 2:
            finish(index - 2)
        held = rights_held[right]
        cols = held.shape[1] // size
        for col in range(cols):
            result = contract(rows_held[index % 2, :rows, :], held[:, col * size : (col + 1) * size], NN)
            for row in range(rows // size):
                results[index % 2, row * cols + col] = result[row * size : (row + 1) * size].astype(jnp.bfloat16)
        for number, (owner, place) in enumerate(places):
            for away in range(2):

                @pl.when((core == owner % 2) == (away == 0))
                def _():
                    pltpu.make_async_copy(
                        results.at[index % 2, number], outs[away].at[place], sems.at[index % 2, number]
                    ).start()

    for index in range(max(0, len(steps) - 2), len(steps)):
        finish(index)


def weight_grads(part, parts, lefts, rights, firsts, core, owned, dp_ways, size):
    first_normed, second_normed, activated, attended = lefts
    d_hidden, seed, d_qkv = rights
    tokens = d_qkv.shape[0]
    width = seed.shape[1]
    part_size = owned // parts
    qkv_blocks = d_qkv.shape[1] // size
    per_row = width // size
    span = per_row // parts
    steps = []
    for left, right, first, rows_all in (
        (1, 0, firsts[2], second_normed.shape[0]),
        (2, 1, firsts[3], activated.shape[0]),
        (3, 1, firsts[1], attended.shape[0]),
    ):
        rows = min(512, rows_all)
        for begin in range(0, rows_all, rows):
            places = []
            for row in range(begin // size, (begin + rows) // size):
                for col in range(span):
                    block = first + row * per_row + part * span + col
                    owner, within = block // owned, block % owned
                    places.append((owner, owner // 2 * part_size + within // per_row * span + col))
            steps.append((left, begin, rows, right, part * span * size, tuple(places)))
    for owner in range(per_row // parts):
        row = owner * parts + part
        places = [(owner, owner // 2 * part_size + col) for col in range(qkv_blocks)]
        steps.append((0, row * size, size, 2, 0, tuple(places)))
    most = max(len(step[5]) for step in steps)
    anywhere = pl.BlockSpec(memory_space=pl.ANY)
    half = jax.ShapeDtypeStruct((dp_ways // 2 * part_size, size, size), jnp.bfloat16)
    flops = 2 * tokens * size * size * dp_ways * part_size
    return pl.pallas_call(
        functools.partial(weight_grad_kernel, tuple(steps)),
        in_specs=[pl.BlockSpec(memory_space=pltpu.SMEM)] + [anywhere] * 7,
        out_specs=[anywhere] * 2,
        out_shape=[half] * 2,
        scratch_shapes=[
            pltpu.VMEM((2, max(step[2] for step in steps), tokens), jnp.bfloat16),
            pltpu.VMEM((tokens, span * size), jnp.bfloat16),
            pltpu.VMEM((tokens, span * size), jnp.bfloat16),
            pltpu.VMEM((tokens, d_qkv.shape[1]), jnp.bfloat16),
            pltpu.VMEM((2, most, size, size), jnp.bfloat16),
            pltpu.SemaphoreType.DMA((2,)),
            pltpu.SemaphoreType.DMA((3,)),
            pltpu.SemaphoreType.DMA((2, most)),
        ],
        compiler_params=kernel_params(),
        cost_estimate=kernel_cost(flops=flops, bytes_accessed=flops // 500, transcendentals=0),
        name="weight_grads",
    )(core, *lefts, *rights)


def pair_sum_kernel(chip_ref, *refs):
    chips = len(refs) // 3
    for index in range(chips):
        total = refs[index][...].astype(jnp.float32) + refs[chips + index][...].astype(jnp.float32)
        refs[2 * chips + index][...] = total.astype(refs[2 * chips + index].dtype)


def pair_sum(kept, received, chip, chips):
    rows, size, _ = kept.shape
    part = rows // chips
    spec = lambda away: pl.BlockSpec(
        (part, size, size), lambda i, chip: (jnp.bitwise_xor(chip[0], away), 0, 0)
    )
    plain = pl.BlockSpec((part, size, size), lambda i, chip: (0, 0, 0))
    dtypes = [jnp.float32] + [jnp.bfloat16] * (chips - 1)
    return pl.pallas_call(
        pair_sum_kernel,
        grid_spec=pltpu.PrefetchScalarGridSpec(
            num_scalar_prefetch=1,
            grid=(1,),
            in_specs=[spec(away) for away in range(chips)] * 2,
            out_specs=[plain] * chips,
        ),
        out_shape=[jax.ShapeDtypeStruct((part, size, size), dtype) for dtype in dtypes],
        compiler_params=kernel_params(),
        cost_estimate=kernel_cost(flops=rows * size * size, bytes_accessed=rows * size * size * 6, transcendentals=0),
        name="pair_sum",
    )(chip, *([kept] * chips), *([received] * chips))


def dot32(left_arg, right_arg):
    return jnp.dot(left_arg, right_arg, preferred_element_type=jnp.float32)


def two_terms(values):
    high = values.astype(jnp.bfloat16)
    return high, (values - high.astype(jnp.float32)).astype(jnp.bfloat16)


def shampoo_kernel(count, terms, held, places_ref, *refs):
    grads, refs = refs[:terms], refs[terms:]
    left_refs, right_refs, master_refs = (refs[side * count : (side + 1) * count] for side in range(3))
    outs, refs = refs[3 * count + held : 3 * count + held + 4], refs[3 * count + held + 4 :]
    results, scaled, roots, pairs, powers, high, low, sems = refs
    size = results.shape[-1]
    step, steps = pl.program_id(0), pl.num_programs(0)
    slot = lax.rem(step, 2)
    chains = range(2 * count)
    stat_refs = (left_refs, right_refs)
    identity = (
        lax.broadcasted_iota(jnp.int32, (size, size), 0)
        == lax.broadcasted_iota(jnp.int32, (size, size), 1)
    ).astype(jnp.float32)

    def copies(of_step, of_slot):
        return [
            pltpu.make_async_copy(
                results.at[of_slot, kind, block],
                outs[kind].at[places_ref[of_step * count + block]],
                sems.at[of_slot, kind, block],
            )
            for kind in range(4)
            for block in range(count)
        ]

    @pl.when(step >= 2)
    def _():
        for copy in copies(step - 2, slot):
            copy.wait()

    grad16 = []
    for block in range(count):
        total = grads[0][block].astype(jnp.float32)
        for grad in grads[1:]:
            total = total + grad[block].astype(jnp.float32)
        results[slot, 0, block] = total
        grad16.append(total.astype(jnp.bfloat16))
    for item in chains:
        block, side = item // 2, item % 2
        dims = (((1 - side,), (1 - side,)), ((), ()))
        results[slot, 1 + side, block] = DECAY * stat_refs[side][block][0] + lax.dot_general(
            grad16[block], grad16[block], dims, preferred_element_type=jnp.float32
        )
    sums = []
    for item in chains:
        stat = results[slot, 1 + item % 2, item // 2]
        sums.append(jnp.sum(stat * stat, axis=0, keepdims=True))
    norms = [jnp.sqrt(jnp.sum(each, axis=1, keepdims=True)) for each in sums]
    for item in chains:
        scaled[item] = results[slot, 1 + item % 2, item // 2] * (1.0 / norms[item])
    factors = [lax.rsqrt(jnp.sqrt(norm)) for norm in norms]

    for repeat in range(ROOT_ITERS - 1):
        for item in chains:
            quarter = (identity - scaled[item]) * 0.25
            pairs[item, size:] = quarter.astype(jnp.bfloat16)
            if repeat == 0:
                roots[item] = identity + quarter
            else:
                pairs[item, :size] = roots[item].astype(jnp.bfloat16)
        if repeat == 0:
            squares = [dot32(pairs[item, size:], pairs[item, size:]) for item in chains]
        else:
            both = [dot32(pairs[item], pairs[item, size:]) for item in chains]
            for item in chains:
                roots[item] = roots[item] + both[item][:size]
            squares = [each[size:] for each in both]
        seconds = [(identity - scaled[item]) * 0.5 + squares[item] for item in chains]
        seconds16 = [second.astype(jnp.bfloat16) for second in seconds]
        fourths = [2.0 * seconds[item] + dot32(seconds16[item], seconds16[item]) for item in chains]
        for item in chains:
            high[item], low[item] = two_terms(scaled[item])
            powers[item, :size], powers[item, size:] = two_terms(fourths[item])
        for item in chains:
            both_terms = dot32(powers[item], high[item])
            scaled[item] = scaled[item] + (
                both_terms[:size] + both_terms[size:] + dot32(powers[item, :size], low[item])
            )
    for item in chains:
        pairs[item, size:] = ((identity - scaled[item]) * 0.25).astype(jnp.bfloat16)
        pairs[item, :size] = roots[item].astype(jnp.bfloat16)
    for item in chains:
        ends = two_terms(roots[item] + dot32(pairs[item, :size], pairs[item, size:]))
        if item % 2 == 0:
            powers[item, :size], powers[item, size:] = ends
        else:
            high[item], low[item] = ends
    halves = []
    for block in range(count):
        both_terms = dot32(powers[2 * block], grad16[block])
        halves.append(both_terms[:size] + both_terms[size:])
    for block in range(count):
        pairs[block, :size], pairs[block, size:] = two_terms(halves[block])
    for block in range(count):
        item = 2 * block + 1
        both_terms = dot32(pairs[block], high[item])
        product = both_terms[:size] + both_terms[size:] + dot32(pairs[block, :size], low[item])
        rate = RATE_BLOCK * factors[2 * block] * factors[item]
        results[slot, 3, block] = master_refs[block][0] - rate * product
    for copy in copies(step, slot):
        copy.start()

    @pl.when(step == steps - 1)
    def _():
        @pl.when(steps >= 2)
        def _():
            for copy in copies(step - 1, 1 - slot):
                copy.wait()

        for copy in copies(step, slot):
            copy.wait()


def shampoo(grads, left_stats, right_stats, master_blocks, places, priors):
    part, size, _ = grads[0].shape
    count = next(each for each in (3, 2, 1) if part % each == 0)
    own = pl.BlockSpec((count, size, size), lambda step, places: (step, 0, 0))
    anywhere = pl.BlockSpec(memory_space=pl.ANY)

    def single(block):
        return pl.BlockSpec((1, size, size), lambda step, places: (places[step * count + block], 0, 0))

    result = jax.ShapeDtypeStruct(left_stats.shape, jnp.float32)
    held = len(priors)
    first_prior = 1 + len(grads) + 3 * count
    wide = pltpu.VMEM((2 * count, 2 * size, size), jnp.bfloat16)
    plain = pltpu.VMEM((2 * count, size, size), jnp.bfloat16)
    return pl.pallas_call(
        functools.partial(shampoo_kernel, count, len(grads), held),
        grid_spec=pltpu.PrefetchScalarGridSpec(
            num_scalar_prefetch=1,
            grid=(part // count,),
            in_specs=[own] * len(grads)
            + [single(block) for block in range(count)] * 3
            + [anywhere] * held,
            out_specs=[anywhere] * 4,
            scratch_shapes=[
                pltpu.VMEM((2, 4, count, size, size), jnp.float32),
                pltpu.VMEM((2 * count, size, size), jnp.float32),
                pltpu.VMEM((2 * count, size, size), jnp.float32),
                wide,
                wide,
                plain,
                plain,
                pltpu.SemaphoreType.DMA((2, 4, count)),
            ],
        ),
        out_shape=[result] * 4,
        input_output_aliases={first_prior + index: index for index in range(held)},
        compiler_params=kernel_params(),
        cost_estimate=kernel_cost(
            flops=part * 130 * 2 * size**3, bytes_accessed=part * size * size * 30, transcendentals=0
        ),
        name="shampoo",
    )(
        places,
        *grads,
        *([left_stats] * count),
        *([right_stats] * count),
        *([master_blocks] * count),
        *priors,
    )


def after(value, *earlier):
    return lax.optimization_barrier((value,) + earlier)[0]


def onward(part, axis):
    ways = lax.axis_size(axis)
    return lax.ppermute(part, axis, [(each, (each + 1) % ways) for each in range(ways)])


def swap(part, bits):
    ways = lax.axis_size("dp")
    return lax.ppermute(part, "dp", [(each, each ^ bits) for each in range(ways)])


def small_rows(values, ways):
    return jnp.pad(values, ((0, 0), (0, -values.shape[1] % 2048))).reshape(-1, 128)


def shards(
    tokens,
    cotangent,
    segments,
    subsets,
    packs,
    master_blocks,
    left_stats,
    right_stats,
    local_vecs,
    local_vec_stats,
    shared_vecs,
    shared_vec_stats,
):
    tp_ways = lax.axis_size("tp")
    dp_ways = lax.axis_size("dp")
    tp_rank = lax.axis_index("tp")
    tok_dev, model_width = tokens.shape
    group_tok = tok_dev * tp_ways
    pack_count, pack_len = segments.shape
    seg_width = subsets.shape[1]
    heads_dev = HEADS // tp_ways
    ff_dev = FF // tp_ways
    head_cols = heads_dev * HD
    owned, block_size, _ = master_blocks.shape
    block_rows = model_width // block_size
    first_out = block_rows * (3 * head_cols // block_size)
    first_in = first_out + head_cols // block_size * block_rows
    first_down = first_in + block_rows * (ff_dev // block_size)
    all_count = owned * dp_ways
    vec_rows = 3 * heads_dev + ff_dev // HD

    vec_used = local_vecs.size
    shared_used = shared_vecs.size
    vec_flat = jnp.concatenate([local_vecs.reshape(-1), shared_vecs.reshape(-1)])
    extra = jnp.pad(vec_flat, (0, EXTRA_ROWS * block_size - vec_flat.size)).reshape(EXTRA_ROWS, block_size)
    rows16 = jnp.concatenate([master_blocks.reshape(-1, block_size), extra], 0).astype(jnp.bfloat16)
    blocks = lax.all_gather(rows16, "dp", axis=0, tiled=True)

    token_parts = [tokens]
    for step in range(1, tp_ways):
        token_parts.append(onward(token_parts[-1], "tp"))

    gathered = blocks.reshape(dp_ways, -1, block_size)[:, owned * block_size :].reshape(dp_ways, -1)
    vec_values = (
        gathered[:, :vec_used].reshape(dp_ways, vec_rows, -1).transpose(1, 0, 2).reshape(vec_rows, HD)
    ).astype(jnp.float32)
    shared_mine = gathered[:, vec_used : vec_used + shared_used]
    shared_all = jnp.zeros((tp_ways,) + shared_mine.shape, jnp.bfloat16)
    for step in range(tp_ways):
        part = shared_mine
        if step:
            part = lax.ppermute(
                part, "tp", [(each, (each + step) % tp_ways) for each in range(tp_ways)]
            )
        shared_all = lax.dynamic_update_slice(
            shared_all, part[None], ((tp_rank - step) % tp_ways, 0, 0)
        )
    norm_params = (
        shared_all.reshape(tp_ways, dp_ways, 6, -1).transpose(2, 1, 0, 3).reshape(6, model_width)
    ).astype(jnp.float32)
    bias_qkv = vec_values[: 3 * heads_dev].reshape(1, -1)
    bias_in = vec_values[3 * heads_dev :].reshape(1, -1)

    own_pos = tp_rank * tok_dev + jnp.arange(tok_dev)
    own_pack = own_pos // pack_len
    valid_own = (own_pack < packs[0]).astype(jnp.float32)
    owned_input_rows = tokens.astype(jnp.float32)
    owned_centred_scaled, owned_inverse_deviation = apply_layer_norm(owned_input_rows)

    group_pack = jnp.arange(group_tok) // pack_len
    lookup_key = group_pack * seg_width + segments.reshape(-1)
    onehot = lookup_key[:, None] == jnp.arange(pack_count * seg_width)[None, :]
    subset_tok = jnp.sum(jnp.where(onehot, subsets.reshape(-1)[None, :], 0), axis=1)
    weight = 0.5 + subset_tok.astype(jnp.float32) / (SUBSETS - 1)
    factor = (weight * (group_pack < packs[0]).astype(jnp.float32))[:, None]
    own_factor = lax.dynamic_slice_in_dim(factor, tp_rank * tok_dev, tok_dev, 0)
    seed16 = (cotangent.astype(jnp.float32) * own_factor).astype(jnp.bfloat16)

    rank = tp_rank.astype(jnp.int32)[None]
    cosines, sines = turn_tables(pack_len, 128)
    cotangent_parts = [cotangent, onward(after(cotangent, token_parts[-1]), "tp")]
    qkv16, first_turned, second_normed, second_turned, group_tokens, mean, inverse = project_qkv(
        token_parts, rank, blocks, owned, norm_params, bias_qkv, cosines, sines, heads_dev
    )
    attended, attended_turned = attend(qkv16, segments, heads_dev)
    cotangent_parts.append(onward(after(cotangent_parts[-1], attended), "tp"))
    active_turned, slope, partial_value = feed_forward(
        second_normed, attended, blocks, owned, bias_in, (first_out, first_in, first_down)
    )
    while len(cotangent_parts) < tp_ways:
        cotangent_parts.append(onward(after(cotangent_parts[-1], slope), "tp"))

    back_args = (
        tp_ways, rank, factor, slope, group_tokens, mean, inverse, blocks, owned, norm_params,
        (first_out, first_in, first_down), head_cols,
    )
    early = feed_back(cotangent_parts[:-1], 0, *back_args, ())
    late = feed_back(cotangent_parts[-1:], tp_ways - 1, *back_args, early[:4])
    seed_all, d_attended, d_hidden16, dz_part = late[:4]
    branch = lax.psum_scatter(
        after(partial_value, cotangent_parts[-1], early[5]), "tp", scatter_dimension=0, tiled=True
    )
    d_qkv16 = attend_back(qkv16, d_attended, segments, cosines, sines, heads_dev)
    dz16, first_sums, qkv_sums = qkv_back(
        d_qkv16, dz_part, group_tokens, mean, inverse, blocks, owned, norm_params
    )

    dz_rows = lambda back: lax.dynamic_slice_in_dim(dz16, (tp_rank - back) % tp_ways * tok_dev, tok_dev, 0)
    back = 2

    def pass_on(moving, back):
        total = moving.astype(jnp.float32) + dz_rows(back).astype(jnp.float32)
        return total if back == tp_ways else onward(total.astype(jnp.bfloat16), "tp")

    dp_rank = lax.axis_index("dp").astype(jnp.int32)
    lefts = (first_turned, second_turned, active_turned, attended_turned)
    d_qkv_late, first_rows = lax.optimization_barrier((d_qkv16, dz_rows(1)))
    moving = onward(first_rows, "tp")
    rights = (d_hidden16, seed_all, d_qkv_late)
    firsts = (0, first_out, first_in, first_down)
    qkv_blocks = 3 * head_cols // block_size
    parts = 4
    by_part = (
        dp_ways == 8
        and owned == parts * qkv_blocks
        and block_rows == 2 * parts
        and ff_dev == model_width
        and owned % block_rows == 0
        and first_out % block_rows == 0
        and first_in % block_rows == 0
    )
    results = ()
    if by_part:
        part_size = owned // parts
        span = block_rows // parts
        sums = []
        for part in range(parts):
            core = (dp_rank % 2)[None]
            if part >= 2:
                core = after(core, sums[part - 2][0])
            kept, away = weight_grads(
                part, parts, lefts, rights, firsts, core, owned, dp_ways, block_size
            )
            sums.append(pair_sum(kept, swap(away, 1), (dp_rank // 2)[None], dp_ways // 2))
        moving = pass_on(after(moving, kept), back)
        back += 1
        terms = []
        ready = []
        for part in range(parts):
            if part:
                sums[part] = [sums[part][0]] + [after(each, terms[-1][3]) for each in sums[part][1:]]
                ready.append(sums[part][3])
            terms.append([sums[part][0]] + [swap(sums[part][bits], 2 * bits) for bits in range(1, 4)])
        count = jnp.arange(part_size, dtype=jnp.int32)
        in_qkv = dp_rank * owned < first_out
        for part in range(parts):
            places = jnp.where(
                in_qkv,
                part * part_size + count,
                count // span * block_rows + part * span + count % span,
            )
            if part < parts - 1:
                places = after(places, ready[part])
            results = shampoo(terms[part], left_stats, right_stats, master_blocks, places, results)
            if part % 2 == 1 and back <= tp_ways:
                moving, first_result = lax.optimization_barrier((moving, results[0]))
                results = [first_result] + list(results[1:])
                moving = pass_on(moving, back)
                back += 1
    else:
        local = [
            to_blocks(jnp.dot(left, right, preferred_element_type=jnp.float32).astype(jnp.bfloat16), block_size)
            for left, right in (
                (first_turned, d_qkv_late),
                (attended_turned, seed_all),
                (second_turned, d_hidden16),
                (active_turned, seed_all),
            )
        ]
        grads16 = lax.psum_scatter(jnp.concatenate(local, 0), "dp", scatter_dimension=0, tiled=True)
        results = shampoo(
            [grads16], left_stats, right_stats, master_blocks, jnp.arange(owned, dtype=jnp.int32), results
        )
    while back <= tp_ways:
        moving = pass_on(moving, back)
        back += 1
    norm_input_gradient = moving
    own_grads, left_new, right_new, new_blocks = results
    output = (
        valid_own[:, None]
        * (owned_input_rows + branch.astype(jnp.float32) + norm_params[4] + norm_params[5])
    ).astype(jnp.bfloat16)

    average_gradient = jnp.mean(norm_input_gradient, axis=-1, keepdims=True)
    average_projection = jnp.mean(
        norm_input_gradient * owned_centred_scaled, axis=-1, keepdims=True
    )
    input_grad = seed16.astype(jnp.float32) + owned_inverse_deviation * (
        norm_input_gradient - average_gradient - owned_centred_scaled * average_projection
    )

    shared_local = jnp.concatenate(
        [
            jnp.sum(first_sums.reshape(2, 8, model_width), axis=1),
            jnp.sum((early[4][:16] + late[4][:16]).reshape(2, 8, model_width), axis=1),
            jnp.sum(early[4][16:], axis=0)[None],
        ],
        0,
    )
    vecs_local = jnp.concatenate(
        [
            jnp.sum(qkv_sums, axis=0).reshape(3 * heads_dev, HD),
            jnp.sum(early[5] + late[5], axis=0).reshape(ff_dev // HD, HD),
        ],
        0,
    )
    small = jnp.concatenate(
        [
            shared_local.reshape(5, dp_ways, -1).transpose(1, 0, 2).reshape(dp_ways, -1),
            vecs_local.reshape(vec_rows, dp_ways, -1).transpose(1, 0, 2).reshape(dp_ways, -1),
        ],
        1,
    )
    small_own = lax.psum_scatter(
        small_rows(small, dp_ways), "dp", scatter_dimension=0, tiled=True
    ).reshape(-1)
    shared_size = 5 * model_width // dp_ways
    own_vec_grads = small_own[shared_size : small.shape[1]].reshape(vec_rows, HD // dp_ways)
    shared_part = small_own[:shared_size].reshape(5, tp_ways, -1).transpose(1, 0, 2)
    shared_own = lax.psum_scatter(
        small_rows(shared_part.reshape(tp_ways, -1), tp_ways), "tp", scatter_dimension=0, tiled=True
    ).reshape(-1)
    shared_own = shared_own[: shared_size // tp_ways].reshape(5, -1)
    shared_grads = jnp.concatenate([shared_own, shared_own[4:]], 0)
    local_stat_new = DECAY * local_vec_stats + own_vec_grads * own_vec_grads
    local_new = local_vecs - RATE_VEC * own_vec_grads * lax.rsqrt(local_stat_new)
    shared_stat_new = DECAY * shared_vec_stats + shared_grads * shared_grads
    shared_new = shared_vecs - RATE_VEC * shared_grads * lax.rsqrt(shared_stat_new)
    return (
        output,
        input_grad,
        own_grads,
        left_new,
        right_new,
        new_blocks,
        own_vec_grads,
        local_stat_new,
        local_new,
        shared_grads,
        shared_stat_new,
        shared_new,
    )


def solution(mesh):
    placed = (
        P(("dp", "tp"), None),
        P(("dp", "tp"), None),
        P("dp", None),
        P("dp", None),
        P("dp"),
        P(("dp", "tp"), None, None),
        P(("dp", "tp"), None, None),
        P(("dp", "tp"), None, None),
        P("tp", "dp"),
        P("tp", "dp"),
        P(None, ("dp", "tp")),
        P(None, ("dp", "tp")),
    )
    return jax.shard_map(
        shards,
        mesh=mesh,
        in_specs=placed,
        out_specs=(
            P(("dp", "tp"), None),
            P(("dp", "tp"), None),
            P(("dp", "tp"), None, None),
            P(("dp", "tp"), None, None),
            P(("dp", "tp"), None, None),
            P(("dp", "tp"), None, None),
            P("tp", "dp"),
            P("tp", "dp"),
            P("tp", "dp"),
            P(None, ("dp", "tp")),
            P(None, ("dp", "tp")),
            P(None, ("dp", "tp")),
        ),
        check_vma=False,
    )
```

```python
import functools
import math

import jax
import jax.numpy as jnp
from jax import lax
from jax.experimental import pallas as pl
from jax.experimental.pallas import tpu as pltpu
from jax.sharding import PartitionSpec as P

HEADS = 8
HD = 256
ROT = 64
FF = 8192
SUBSETS = 22
ROOT_ITERS = 8


EPS_NORM = 1e-05
DECAY = 0.5
RATE_BLOCK = 0.6
RATE_VEC = 0.2
NEG_FILL = -1e30
DOC_MAX = 512
HALF_ROOT = 0.7071067811865476
DENSITY_SCALE = 0.3989422804014327


def apply_layer_norm(values):
    mean_val = jnp.mean(values, axis=-1, keepdims=True)
    centred = values - mean_val
    variance = jnp.mean(centred * centred, axis=-1, keepdims=True)
    inv_std = lax.rsqrt(variance + EPS_NORM)
    return (centred * inv_std, inv_std)


def to_blocks(matrix, block_size):
    block_rows = matrix.shape[0] // block_size
    block_cols = matrix.shape[1] // block_size
    return (
        matrix.reshape(block_rows, block_size, block_cols, block_size)
        .transpose(0, 2, 1, 3)
        .reshape(block_rows * block_cols, block_size, block_size)
    )


EXTRA_ROWS = 16
FEED_BACK_TILE = 512
VMEM_LIMIT = 60 << 20
NN = (((1,), (0,)), ((), ()))
NT = (((1,), (1,)), ((), ()))
TN = (((0,), (0,)), ((), ()))


def contract(left_arg, right_arg, dims):
    return lax.dot_general(left_arg, right_arg, dims, preferred_element_type=jnp.float32)


def kernel_params():
    return pltpu.CompilerParams(vmem_limit_bytes=VMEM_LIMIT)


def block_row(index, owned, size):
    return index // owned * (owned * size + EXTRA_ROWS) + index % owned * size


def block_copies(blocks_ref, owned, first, rows, cols, target, sems):
    size = blocks_ref.shape[-1]
    return [
        pltpu.make_async_copy(
            blocks_ref.at[pl.ds(block_row(first + row * cols + col, owned, size), size), :],
            target.at[pl.ds(row * size, size), pl.ds(col * size, size)],
            sems.at[row * cols + col],
        )
        for row in range(rows)
        for col in range(cols)
    ]


def begin_copies(copies):
    @pl.when(pl.program_id(0) == 0)
    def _():
        for copy in copies:
            copy.start()


def end_copies(copies):
    @pl.when(pl.program_id(0) == 0)
    def _():
        for copy in copies:
            copy.wait()


def turn(values, cosines, sines):
    lane = lax.broadcasted_iota(jnp.int32, values.shape, 1)
    half = ROT // 2
    wide = values.shape[1]
    swapped = jnp.where(
        lane < half, pltpu.roll(values, wide - half, 1), pltpu.roll(values, half, 1)
    )
    return values * cosines + swapped * sines


def turn_tables(pack_len, lanes):
    half = ROT // 2
    positions = jnp.arange(pack_len).astype(jnp.float32)
    freqs = 10000.0 ** (-(jnp.arange(half).astype(jnp.float32) * 2.0) / ROT)
    angles = positions[:, None] * freqs[None, :]
    cosines = jnp.cos(angles)
    sines = jnp.sin(angles)
    rest = jnp.zeros((pack_len, lanes - ROT), jnp.float32)
    return (
        jnp.concatenate([cosines, cosines, rest + 1.0], -1),
        jnp.concatenate([-sines, sines, rest], -1),
    )


def normed_rows(rows):
    mean = jnp.mean(rows, axis=1, keepdims=True)
    centred = rows - mean
    variance = jnp.mean(centred * centred, axis=1, keepdims=True)
    return mean, lax.rsqrt(variance + EPS_NORM)


def part_copies(part_refs, held, sems):
    return [
        pltpu.make_async_copy(part, held.at[index], sems.at[index])
        for index, part in enumerate(part_refs)
    ]


def await_part(copies, per_part):
    step = pl.program_id(0)
    for index, copy in enumerate(copies):

        @pl.when(step == index * per_part)
        def _():
            copy.wait()


def qkv_kernel(heads, owned, parts, rank_ref, *refs):
    part_refs = refs[:parts]
    blocks_ref, norm_ref, bias_ref, cos_ref, sin_ref = refs[parts : parts + 5]
    outs, (normed, weight, held, sems, part_sems) = refs[parts + 5 : parts + 12], refs[parts + 12 :]
    qkv_ref, first_turned, second_ref, second_turned, tokens_ref, mean_ref, inverse_ref = outs
    size = blocks_ref.shape[-1]
    copies = block_copies(blocks_ref, owned, 0, weight.shape[0] // size, weight.shape[1] // size, weight, sems)
    moves = part_copies(part_refs, held, part_sems)
    begin_copies(moves + copies)
    await_part(moves, 1)
    own = held[pl.program_id(0)]
    tokens_ref[...] = own
    rows = own.astype(jnp.float32)
    mean, inverse = normed_rows(rows)
    mean_ref[...] = mean
    inverse_ref[...] = inverse
    for col in range(rows.shape[1] // size):
        cols = pl.ds(col * size, size)
        scaled = (own[:, col * size : (col + 1) * size].astype(jnp.float32) - mean) * inverse
        second = (scaled * norm_ref[2:3, cols] + norm_ref[3:4, cols]).astype(jnp.bfloat16)
        second_ref[:, cols] = second
        second_turned[cols, :] = second.T
        first = (scaled * norm_ref[0:1, cols] + norm_ref[1:2, cols]).astype(jnp.bfloat16)
        normed[:, cols] = first
        first_turned[cols, :] = first.T
    end_copies(copies)
    lanes = cos_ref.shape[1]
    for head in range(heads):
        for part in range(3):
            cols = pl.ds((head * 3 + part) * HD, HD)
            result = contract(normed[...], weight[:, cols], NN) + bias_ref[:, cols]
            if part < 2:
                first = turn(result[:, :lanes], cos_ref[...], sin_ref[...])
                result = jnp.concatenate([first, result[:, lanes:]], 1)
            if part == 0:
                result = result * (1.0 / math.sqrt(HD))
            qkv_ref[:, cols] = result.astype(jnp.bfloat16)


def project_qkv(parts, rank, blocks, owned, norm_params, bias, cosines, sines, heads):
    ways = len(parts)
    tile, width = parts[0].shape
    tokens = ways * tile
    size = blocks.shape[-1]
    pack_len, lanes = cosines.shape
    cols = 3 * heads * HD
    per_pack = pack_len // tile
    place = lambda i, rank: (rank[0] - i + ways) % ways
    row = lambda n: pl.BlockSpec((tile, n), lambda i, rank: (place(i, rank), 0))
    table = pl.BlockSpec((tile, lanes), lambda i, rank: (place(i, rank) % per_pack, 0))
    anywhere = pl.BlockSpec(memory_space=pl.ANY)
    wide = jax.ShapeDtypeStruct((tokens, width), jnp.bfloat16)
    tall = jax.ShapeDtypeStruct((width, tokens), jnp.bfloat16)
    single = jax.ShapeDtypeStruct((tokens, 1), jnp.float32)
    turned = pl.BlockSpec((width, tile), lambda i, rank: (0, place(i, rank)))
    return pl.pallas_call(
        functools.partial(qkv_kernel, heads, owned, ways),
        grid_spec=pltpu.PrefetchScalarGridSpec(
            num_scalar_prefetch=1,
            grid=(ways,),
            in_specs=[anywhere] * (ways + 1)
            + [
                pl.BlockSpec(norm_params.shape, lambda i, rank: (0, 0)),
                pl.BlockSpec((1, cols), lambda i, rank: (0, 0)),
                table,
                table,
            ],
            out_specs=[row(cols), turned, row(width), turned, row(width), row(1), row(1)],
            scratch_shapes=[
                pltpu.VMEM((tile, width), jnp.bfloat16),
                pltpu.VMEM((width, cols), jnp.bfloat16),
                pltpu.VMEM((ways, tile, width), jnp.bfloat16),
                pltpu.SemaphoreType.DMA((width // size * (cols // size),)),
                pltpu.SemaphoreType.DMA((ways,)),
            ],
        ),
        out_shape=[jax.ShapeDtypeStruct((tokens, cols), jnp.bfloat16), tall, wide, tall, wide, single, single],
        compiler_params=kernel_params(),
        cost_estimate=pl.CostEstimate(
            flops=2 * tokens * width * cols, bytes_accessed=tokens * (4 * width + cols) * 2 + width * cols * 2, transcendentals=0
        ),
        name="qkv",
    )(rank, *parts, blocks, norm_params, bias, cosines, sines)


def attend_kernel(query_ref, key_ref, value_ref, seg_row, seg_col, out_ref, turned_ref):
    length = key_ref.shape[0]
    step = 256
    for start in range(0, length, step):
        first = max(0, start - DOC_MAX)
        stop = start + step
        scores = contract(query_ref[start:stop, :], key_ref[first:stop, :], NT)
        row = lax.broadcasted_iota(jnp.int32, scores.shape, 0) + start
        col = lax.broadcasted_iota(jnp.int32, scores.shape, 1) + first
        allowed = (col <= row) & (seg_col[0, start:stop, :] == seg_row[0, :, first:stop])
        masked = jnp.where(allowed, scores, NEG_FILL)
        exp_terms = jnp.exp(masked - jnp.max(masked, axis=1, keepdims=True))
        probs = exp_terms * (1.0 / jnp.sum(exp_terms, axis=1, keepdims=True))
        result = contract(probs.astype(jnp.bfloat16), value_ref[first:stop, :], NN).astype(jnp.bfloat16)
        out_ref[start:stop, :] = result
        turned_ref[:, start:stop] = result.T


def attend(qkv, segments, heads):
    packs, length = segments.shape
    part = lambda which: pl.BlockSpec((length, HD), lambda p, h: (p, h * 3 + which))
    return pl.pallas_call(
        attend_kernel,
        grid=(packs, heads),
        in_specs=[
            part(0),
            part(1),
            part(2),
            pl.BlockSpec((1, 1, length), lambda p, h: (p, 0, 0)),
            pl.BlockSpec((1, length, 1), lambda p, h: (p, 0, 0)),
        ],
        out_specs=[
            pl.BlockSpec((length, HD), lambda p, h: (p, h)),
            pl.BlockSpec((HD, length), lambda p, h: (h, p)),
        ],
        out_shape=[
            jax.ShapeDtypeStruct((packs * length, heads * HD), jnp.bfloat16),
            jax.ShapeDtypeStruct((heads * HD, packs * length), jnp.bfloat16),
        ],
        compiler_params=kernel_params(),
        cost_estimate=pl.CostEstimate(
            flops=packs * heads * length * length * HD * 3, bytes_accessed=packs * length * heads * HD * 8, transcendentals=0
        ),
        name="attend",
    )(qkv, qkv, qkv, segments[:, None, :], segments[:, :, None])


def attend_back_kernel(
    query_ref, key_ref, value_ref, d_out_ref, seg_row, seg_col, cos_ref, sin_ref, grad_ref, d_key, d_value
):
    length = key_ref.shape[0]
    step = 256
    lanes = cos_ref.shape[1]
    d_key[...] = jnp.zeros_like(d_key)
    d_value[...] = jnp.zeros_like(d_value)
    for start in range(0, length, step):
        first = max(0, start - DOC_MAX)
        stop = start + step
        query = query_ref[start:stop, :]
        d_out = d_out_ref[start:stop, :]
        keys = key_ref[first:stop, :]
        scores = contract(keys, query, NT)
        key_pos = lax.broadcasted_iota(jnp.int32, scores.shape, 0) + first
        query_pos = lax.broadcasted_iota(jnp.int32, scores.shape, 1) + start
        allowed = (key_pos <= query_pos) & (seg_col[0, first:stop, :] == seg_row[0, :, start:stop])
        masked = jnp.where(allowed, scores, NEG_FILL)
        exp_terms = jnp.exp(masked - jnp.max(masked, axis=0, keepdims=True))
        probs = exp_terms * (1.0 / jnp.sum(exp_terms, axis=0, keepdims=True))
        d_probs = contract(value_ref[first:stop, :], d_out, NT)
        row_dot = jnp.sum(probs * d_probs, axis=0, keepdims=True)
        d_scores = (probs * (d_probs - row_dot)).astype(jnp.bfloat16)
        d_value[first:stop, :] += contract(probs.astype(jnp.bfloat16), d_out, NN)
        d_key[first:stop, :] += contract(d_scores, query, NN)
        d_query = contract(d_scores, keys, TN) * (1.0 / math.sqrt(HD))
        back = turn(d_query[:, :lanes], cos_ref[start:stop, :], -sin_ref[start:stop, :])
        grad_ref[start:stop, :lanes] = back.astype(jnp.bfloat16)
        grad_ref[start:stop, lanes:HD] = d_query[:, lanes:].astype(jnp.bfloat16)
    back = turn(d_key[:, :lanes], cos_ref[...], -sin_ref[...])
    grad_ref[:, HD : HD + lanes] = back.astype(jnp.bfloat16)
    grad_ref[:, HD + lanes : 2 * HD] = d_key[:, lanes:].astype(jnp.bfloat16)
    grad_ref[:, 2 * HD :] = d_value[...].astype(jnp.bfloat16)


def attend_back(qkv, d_attended, segments, cosines, sines, heads):
    packs, length = segments.shape
    lanes = cosines.shape[1]
    part = lambda which: pl.BlockSpec((length, HD), lambda p, h: (p, h * 3 + which))
    table = pl.BlockSpec((length, lanes), lambda p, h: (0, 0))
    return pl.pallas_call(
        attend_back_kernel,
        grid=(packs, heads),
        in_specs=[
            part(0),
            part(1),
            part(2),
            pl.BlockSpec((length, HD), lambda p, h: (p, h)),
            pl.BlockSpec((1, 1, length), lambda p, h: (p, 0, 0)),
            pl.BlockSpec((1, length, 1), lambda p, h: (p, 0, 0)),
            table,
            table,
        ],
        out_specs=pl.BlockSpec((length, 3 * HD), lambda p, h: (p, h)),
        out_shape=jax.ShapeDtypeStruct((packs * length, 3 * heads * HD), jnp.bfloat16),
        scratch_shapes=[pltpu.VMEM((length, HD), jnp.float32)] * 2,
        compiler_params=kernel_params(),
        cost_estimate=pl.CostEstimate(
            flops=packs * heads * length * length * HD * 7, bytes_accessed=packs * length * heads * HD * 16, transcendentals=0
        ),
        name="attend_back",
    )(qkv, qkv, qkv, d_attended, segments[:, None, :], segments[:, :, None], cosines, sines)


def feed_kernel(
    offsets, owned, x_ref, attended_ref, blocks_ref, bias_ref, turned_ref, slope_ref, out_ref, act_ref, w_in, w_down, sems_in, sems_down
):
    size = blocks_ref.shape[-1]
    width, hidden_units = w_in.shape
    inner = hidden_units // size
    first_out, first_in, first_down = offsets
    head_rows = attended_ref.shape[1] // size
    outer = width // size
    copies_in = block_copies(blocks_ref, owned, first_in, outer, inner, w_in, sems_in)
    copies_down = block_copies(blocks_ref, owned, first_down, inner, outer, w_down.at[pl.ds(0, hidden_units)], sems_down)
    copies_down += block_copies(
        blocks_ref,
        owned,
        first_out,
        head_rows,
        outer,
        w_down.at[pl.ds(hidden_units, head_rows * size)],
        sems_down.at[pl.ds(inner * outer, head_rows * outer)],
    )
    begin_copies(copies_in + copies_down)
    end_copies(copies_in)
    values = x_ref[...]
    for col in range(inner):
        cols = pl.ds(col * size, size)
        hidden = contract(values, w_in[:, cols], NN) + bias_ref[:, cols]
        cdf = 0.5 + 0.5 * lax.erf(hidden * HALF_ROOT)
        density = jnp.exp(-0.5 * hidden * hidden) * DENSITY_SCALE
        activated = (hidden * cdf).astype(jnp.bfloat16)
        act_ref[:, cols] = activated
        turned_ref[cols, :] = activated.T
        slope_ref[:, cols] = (cdf + hidden * density).astype(jnp.bfloat16)
    end_copies(copies_down)
    for col in range(outer):
        cols = pl.ds(col * size, size)
        out_ref[:, cols] = (
            contract(act_ref[...], w_down[:hidden_units, cols], NN)
            + contract(attended_ref[...], w_down[hidden_units:, cols], NN)
        ).astype(jnp.bfloat16)


def feed_forward(normed, attended, blocks, owned, bias, offsets):
    tokens, width = normed.shape
    size = blocks.shape[-1]
    hidden_units = bias.shape[1]
    head_cols = attended.shape[1]
    tile = 512
    row = lambda cols: pl.BlockSpec((tile, cols), lambda i: (i, 0))
    inner, outer = hidden_units // size, width // size
    return pl.pallas_call(
        functools.partial(feed_kernel, offsets, owned),
        grid=(tokens // tile,),
        in_specs=[
            row(width),
            row(head_cols),
            pl.BlockSpec(memory_space=pl.ANY),
            pl.BlockSpec((1, hidden_units), lambda i: (0, 0)),
        ],
        out_specs=[
            pl.BlockSpec((hidden_units, tile), lambda i: (0, i)), row(hidden_units), row(width),
        ],
        out_shape=[
            jax.ShapeDtypeStruct((hidden_units, tokens), jnp.bfloat16),
            jax.ShapeDtypeStruct((tokens, hidden_units), jnp.bfloat16),
            jax.ShapeDtypeStruct((tokens, width), jnp.bfloat16),
        ],
        scratch_shapes=[
            pltpu.VMEM((tile, hidden_units), jnp.bfloat16),
            pltpu.VMEM((width, hidden_units), jnp.bfloat16),
            pltpu.VMEM((hidden_units + head_cols, width), jnp.bfloat16),
            pltpu.SemaphoreType.DMA((inner * outer,)),
            pltpu.SemaphoreType.DMA((inner * outer + head_cols // size * outer,)),
        ],
        compiler_params=kernel_params(),
        cost_estimate=pl.CostEstimate(
            flops=2 * tokens * width * (2 * hidden_units + head_cols), bytes_accessed=tokens * width * 10 + width * hidden_units * 4, transcendentals=0
        ),
        name="feed",
    )(normed, attended, blocks, bias)


def column_sum(values):
    rows, cols = values.shape
    return jnp.sum(values.reshape(rows // 8, 8, cols), axis=0)


def feed_back_kernel(offsets, owned, first_part, parts, held_count, rank_ref, *refs):
    part_refs = refs[:parts]
    factor_ref, slope_ref, tokens_ref, mean_ref, inverse_ref, blocks_ref, norm_ref = refs[parts : parts + 7]
    (
        seed_ref, d_attended_ref, d_hidden_ref, dz_ref, norm_sums, hidden_sums,
        w_in, w_down, w_out, held, sems_in, sems_down, sems_out, part_sems,
    ) = refs[parts + 7 + held_count :]
    size = blocks_ref.shape[-1]
    width, hidden_units = w_in.shape
    inner, outer = hidden_units // size, width // size
    first_out, first_in, first_down = offsets
    tile = seed_ref.shape[0]
    per_part = held.shape[1] // tile
    moves = part_copies(part_refs, held, part_sems)
    copies_out = block_copies(blocks_ref, owned, first_out, w_out.shape[0] // size, outer, w_out, sems_out)
    copies_down = block_copies(blocks_ref, owned, first_down, inner, outer, w_down, sems_down)
    copies_in = block_copies(blocks_ref, owned, first_in, outer, inner, w_in, sems_in)
    begin_copies(moves + copies_out + copies_down + copies_in)

    @pl.when(pl.program_id(0) == 0)
    def _():
        norm_sums[...] = jnp.zeros_like(norm_sums)
        hidden_sums[...] = jnp.zeros_like(hidden_sums)

    await_part(moves, per_part)
    step = pl.program_id(0)
    cotangent = held[step // per_part, pl.ds(pl.multiple_of(step % per_part * tile, tile), tile), :]
    seed_ref[...] = (cotangent.astype(jnp.float32) * factor_ref[...]).astype(jnp.bfloat16)
    seed = seed_ref[...]
    if first_part == 0:

        @pl.when(step < per_part)
        def _():
            norm_sums[16:24, :] += column_sum(seed_ref[...].astype(jnp.float32))

    end_copies(copies_out)
    d_attended_ref[...] = contract(seed, w_out[...], NT).astype(jnp.bfloat16)
    end_copies(copies_down)
    for col in range(inner):
        cols = pl.ds(col * size, size)
        d_act = contract(seed_ref[...], w_down[cols, :], NT)
        d_hidden = (d_act * slope_ref[:, cols].astype(jnp.float32)).astype(jnp.bfloat16)
        d_hidden_ref[:, cols] = d_hidden
        hidden_sums[:, cols] += column_sum(d_hidden.astype(jnp.float32))
    end_copies(copies_in)
    mean, inverse = mean_ref[...], inverse_ref[...]
    for col in range(outer):
        cols = pl.ds(col * size, size)
        scaled = (tokens_ref[:, cols].astype(jnp.float32) - mean) * inverse
        second = contract(d_hidden_ref[...], w_in[cols, :], NT)
        dz_ref[:, cols] = (second * norm_ref[2:3, cols]).astype(jnp.bfloat16)
        norm_sums[0:8, cols] += column_sum(second * scaled)
        norm_sums[8:16, cols] += column_sum(second)


def feed_back(parts, first_part, ways, rank, factor, slope, group_tokens, mean, inverse, blocks, owned, norm_params, offsets, head_cols, priors):
    chunk, width = parts[0].shape
    tokens = ways * chunk
    size = blocks.shape[-1]
    hidden_units = slope.shape[1]
    tile = min(FEED_BACK_TILE, chunk)
    per_part = chunk // tile
    inner, outer = hidden_units // size, width // size
    place = lambda i, rank: (rank[0] - first_part - i // per_part + ways) % ways * per_part + i % per_part
    row = lambda n: pl.BlockSpec((tile, n), lambda i, rank: (place(i, rank), 0))
    whole = lambda rows, cols: pl.BlockSpec((rows, cols), lambda i, rank: (0, 0))
    anywhere = pl.BlockSpec(memory_space=pl.ANY)
    count = len(parts)
    rows = count * chunk
    return pl.pallas_call(
        functools.partial(feed_back_kernel, offsets, owned, first_part, count, len(priors)),
        grid_spec=pltpu.PrefetchScalarGridSpec(
            num_scalar_prefetch=1,
            grid=(count * per_part,),
            in_specs=[anywhere] * count
            + [row(1), row(hidden_units), row(width), row(1), row(1), anywhere]
            + [whole(norm_params.shape[0], width)]
            + [anywhere] * len(priors),
            out_specs=[
                row(width), row(head_cols), row(hidden_units), row(width), whole(24, width), whole(8, hidden_units),
            ],
            scratch_shapes=[
                pltpu.VMEM((width, hidden_units), jnp.bfloat16),
                pltpu.VMEM((hidden_units, width), jnp.bfloat16),
                pltpu.VMEM((head_cols, width), jnp.bfloat16),
                pltpu.VMEM((count, chunk, width), jnp.bfloat16),
                pltpu.SemaphoreType.DMA((inner * outer,)),
                pltpu.SemaphoreType.DMA((inner * outer,)),
                pltpu.SemaphoreType.DMA((head_cols // size * outer,)),
                pltpu.SemaphoreType.DMA((count,)),
            ],
        ),
        out_shape=[
            jax.ShapeDtypeStruct((tokens, width), jnp.bfloat16),
            jax.ShapeDtypeStruct((tokens, head_cols), jnp.bfloat16),
            jax.ShapeDtypeStruct((tokens, hidden_units), jnp.bfloat16),
            jax.ShapeDtypeStruct((tokens, width), jnp.bfloat16),
            jax.ShapeDtypeStruct((24, width), jnp.float32),
            jax.ShapeDtypeStruct((8, hidden_units), jnp.float32),
        ],
        input_output_aliases={1 + count + 7 + index: index for index in range(len(priors))},
        compiler_params=kernel_params(),
        cost_estimate=pl.CostEstimate(
            flops=2 * rows * width * (2 * hidden_units + head_cols), bytes_accessed=rows * width * 14 + width * hidden_units * 4, transcendentals=0
        ),
        name="feed_back",
    )(rank, *parts, factor, slope, group_tokens, mean, inverse, blocks, norm_params, *priors)


def qkv_back_kernel(owned, d_qkv_ref, part_ref, tokens_ref, mean_ref, inverse_ref, blocks_ref, norm_ref, dz_ref, norm_sums, qkv_sums, w_qkv, sems):
    size = blocks_ref.shape[-1]
    outer = w_qkv.shape[0] // size
    copies = block_copies(blocks_ref, owned, 0, outer, w_qkv.shape[1] // size, w_qkv, sems)
    begin_copies(copies)

    @pl.when(pl.program_id(0) == 0)
    def _():
        norm_sums[...] = jnp.zeros_like(norm_sums)
        qkv_sums[...] = jnp.zeros_like(qkv_sums)

    qkv_sums[...] += column_sum(d_qkv_ref[...].astype(jnp.float32))
    mean, inverse = mean_ref[...], inverse_ref[...]
    end_copies(copies)
    for col in range(outer):
        cols = pl.ds(col * size, size)
        scaled = (tokens_ref[:, cols].astype(jnp.float32) - mean) * inverse
        first = contract(d_qkv_ref[...], w_qkv[cols, :], NT)
        dz_ref[:, cols] = (part_ref[:, cols].astype(jnp.float32) + first * norm_ref[0:1, cols]).astype(jnp.bfloat16)
        norm_sums[0:8, cols] += column_sum(first * scaled)
        norm_sums[8:16, cols] += column_sum(first)


def qkv_back(d_qkv, dz_part, group_tokens, mean, inverse, blocks, owned, norm_params):
    tokens, qkv_cols = d_qkv.shape
    width = dz_part.shape[1]
    size = blocks.shape[-1]
    tile = 512
    row = lambda cols: pl.BlockSpec((tile, cols), lambda i: (i, 0))
    whole = lambda rows, cols: pl.BlockSpec((rows, cols), lambda i: (0, 0))
    outer = width // size
    return pl.pallas_call(
        functools.partial(qkv_back_kernel, owned),
        grid=(tokens // tile,),
        in_specs=[
            row(qkv_cols), row(width), row(width), row(1), row(1), pl.BlockSpec(memory_space=pl.ANY), whole(norm_params.shape[0], width),
        ],
        out_specs=[row(width), whole(16, width), whole(8, qkv_cols)],
        out_shape=[
            jax.ShapeDtypeStruct((tokens, width), jnp.bfloat16),
            jax.ShapeDtypeStruct((16, width), jnp.float32),
            jax.ShapeDtypeStruct((8, qkv_cols), jnp.float32),
        ],
        scratch_shapes=[
            pltpu.VMEM((width, qkv_cols), jnp.bfloat16),
            pltpu.SemaphoreType.DMA((outer * (qkv_cols // size),)),
        ],
        compiler_params=kernel_params(),
        cost_estimate=pl.CostEstimate(
            flops=2 * tokens * width * qkv_cols, bytes_accessed=tokens * width * 11, transcendentals=0
        ),
        name="qkv_back",
    )(d_qkv, dz_part, group_tokens, mean, inverse, blocks, norm_params)


def weight_grad_kernel(steps, waits, core_ref, *refs):
    lefts, rights, refs = refs[:4], refs[4:7], refs[7 + waits :]
    outs, rows_held, rights_held = refs[:2], refs[2], refs[3:6]
    results, left_sems, right_sems, sems = refs[6:]
    size = results.shape[-1]
    core = core_ref[0]
    depth = rows_held.shape[0]

    def left_copy(index):
        left, first, rows, _, _, _ = steps[index]
        return pltpu.make_async_copy(
            lefts[left].at[pl.ds(first, rows), :],
            rows_held.at[index % depth, pl.ds(0, rows), :],
            left_sems.at[index % depth],
        )

    def right_copy(right, first):
        held = rights_held[right]
        return pltpu.make_async_copy(
            rights[right].at[:, pl.ds(first, held.shape[1])], held, right_sems.at[right]
        )

    def finish(index):
        for place in range(len(steps[index][5])):
            pltpu.make_async_copy(
                results.at[index % 2, place], outs[0].at[0], sems.at[index % 2, place]
            ).wait()

    order = []
    for step in steps:
        if step[3:5] not in order:
            order.append(step[3:5])
    right_copy(*order[0]).start()
    for index in range(min(depth - 1, len(steps))):
        left_copy(index).start()
    for right in order[1:]:
        right_copy(*right).start()
    for index, (left, first, rows, right, right_first, places) in enumerate(steps):
        left_copy(index).wait()
        if index + depth - 1 < len(steps):
            left_copy(index + depth - 1).start()
        if all(step[3:5] != (right, right_first) for step in steps[:index]):
            right_copy(right, right_first).wait()
        if index >= 2:
            finish(index - 2)
        held = rights_held[right]
        cols = held.shape[1] // size
        for col in range(cols):
            result = contract(rows_held[index % depth, :rows, :], held[:, col * size : (col + 1) * size], NN)
            for row in range(rows // size):
                results[index % 2, row * cols + col] = result[row * size : (row + 1) * size].astype(jnp.bfloat16)
        for number, (owner, place) in enumerate(places):
            for away in range(2):

                @pl.when((core == owner % 2) == (away == 0))
                def _():
                    pltpu.make_async_copy(
                        results.at[index % 2, number], outs[away].at[place], sems.at[index % 2, number]
                    ).start()

    for index in range(max(0, len(steps) - 2), len(steps)):
        finish(index)


def weight_grads(part, parts, lefts, rights, firsts, core, owned, dp_ways, size, waits):
    first_normed, second_normed, activated, attended = lefts
    d_hidden, seed, d_qkv = rights
    tokens = d_qkv.shape[0]
    width = seed.shape[1]
    part_size = owned // parts
    qkv_blocks = d_qkv.shape[1] // size
    per_row = width // size
    span = per_row // parts
    steps = []
    for left, right, first, rows_all in (
        (1, 0, firsts[2], second_normed.shape[0]),
        (2, 1, firsts[3], activated.shape[0]),
        (3, 1, firsts[1], attended.shape[0]),
    ):
        rows = min(512, rows_all)
        for begin in range(0, rows_all, rows):
            places = []
            for row in range(begin // size, (begin + rows) // size):
                for col in range(span):
                    block = first + row * per_row + part * span + col
                    owner, within = block // owned, block % owned
                    places.append((owner, owner // 2 * part_size + within // per_row * span + col))
            steps.append((left, begin, rows, right, part * span * size, tuple(places)))
    for owner in range(per_row // parts):
        row = owner * parts + part
        places = [(owner, owner // 2 * part_size + col) for col in range(qkv_blocks)]
        steps.append((0, row * size, size, 2, 0, tuple(places)))
    most = max(len(step[5]) for step in steps)
    anywhere = pl.BlockSpec(memory_space=pl.ANY)
    half = jax.ShapeDtypeStruct((dp_ways // 2 * part_size, size, size), jnp.bfloat16)
    flops = 2 * tokens * size * size * dp_ways * part_size
    return pl.pallas_call(
        functools.partial(weight_grad_kernel, tuple(steps), len(waits)),
        in_specs=[pl.BlockSpec(memory_space=pltpu.SMEM)] + [anywhere] * (7 + len(waits)),
        out_specs=[anywhere] * 2,
        out_shape=[half] * 2,
        scratch_shapes=[
            pltpu.VMEM((4, max(step[2] for step in steps), tokens), jnp.bfloat16),
            pltpu.VMEM((tokens, span * size), jnp.bfloat16),
            pltpu.VMEM((tokens, span * size), jnp.bfloat16),
            pltpu.VMEM((tokens, d_qkv.shape[1]), jnp.bfloat16),
            pltpu.VMEM((2, most, size, size), jnp.bfloat16),
            pltpu.SemaphoreType.DMA((4,)),
            pltpu.SemaphoreType.DMA((3,)),
            pltpu.SemaphoreType.DMA((2, most)),
        ],
        compiler_params=kernel_params(),
        cost_estimate=pl.CostEstimate(flops=flops, bytes_accessed=flops // 500, transcendentals=0),
        name="weight_grads",
    )(core, *lefts, *rights, *waits)


def pair_sum_kernel(chip_ref, *refs):
    chips = len(refs) // 3
    for index in range(chips):
        total = refs[index][...].astype(jnp.float32) + refs[chips + index][...].astype(jnp.float32)
        refs[2 * chips + index][...] = total.astype(refs[2 * chips + index].dtype)


def pair_sum(kept, received, chip, chips):
    rows, size, _ = kept.shape
    part = rows // chips
    spec = lambda away: pl.BlockSpec(
        (part, size, size), lambda i, chip: (jnp.bitwise_xor(chip[0], away), 0, 0)
    )
    plain = pl.BlockSpec((part, size, size), lambda i, chip: (0, 0, 0))
    dtypes = [jnp.float32] + [jnp.bfloat16] * (chips - 1)
    return pl.pallas_call(
        pair_sum_kernel,
        grid_spec=pltpu.PrefetchScalarGridSpec(
            num_scalar_prefetch=1,
            grid=(1,),
            in_specs=[spec(away) for away in range(chips)] * 2,
            out_specs=[plain] * chips,
        ),
        out_shape=[jax.ShapeDtypeStruct((part, size, size), dtype) for dtype in dtypes],
        compiler_params=kernel_params(),
        cost_estimate=pl.CostEstimate(flops=rows * size * size, bytes_accessed=rows * size * size * 6, transcendentals=0),
        name="pair_sum",
    )(chip, *([kept] * chips), *([received] * chips))


def dot32(left_arg, right_arg):
    return jnp.dot(left_arg, right_arg, preferred_element_type=jnp.float32)


def two_terms(values):
    high = values.astype(jnp.bfloat16)
    return high, (values - high.astype(jnp.float32)).astype(jnp.bfloat16)


def shampoo_kernel(count, terms, held, places_ref, *refs):
    grads, refs = refs[:terms], refs[terms:]
    left_refs, right_refs, master_refs = (refs[side * count : (side + 1) * count] for side in range(3))
    outs, refs = refs[3 * count + held : 3 * count + held + 4], refs[3 * count + held + 4 :]
    results, scaled, roots, pairs, powers, high, low, sems = refs
    size = results.shape[-1]
    step, steps = pl.program_id(0), pl.num_programs(0)
    slot = lax.rem(step, 2)
    chains = range(2 * count)
    stat_refs = (left_refs, right_refs)
    identity = (
        lax.broadcasted_iota(jnp.int32, (size, size), 0)
        == lax.broadcasted_iota(jnp.int32, (size, size), 1)
    ).astype(jnp.float32)

    def copies(of_step, of_slot):
        return [
            pltpu.make_async_copy(
                results.at[of_slot, kind, block],
                outs[kind].at[places_ref[of_step * count + block]],
                sems.at[of_slot, kind, block],
            )
            for kind in range(4)
            for block in range(count)
        ]

    @pl.when(step >= 2)
    def _():
        for copy in copies(step - 2, slot):
            copy.wait()

    grad16 = []
    for block in range(count):
        total = grads[0][block].astype(jnp.float32)
        for grad in grads[1:]:
            total = total + grad[block].astype(jnp.float32)
        results[slot, 0, block] = total
        grad16.append(total.astype(jnp.bfloat16))
    for item in chains:
        block, side = item // 2, item % 2
        dims = (((1 - side,), (1 - side,)), ((), ()))
        results[slot, 1 + side, block] = DECAY * stat_refs[side][block][0] + lax.dot_general(
            grad16[block], grad16[block], dims, preferred_element_type=jnp.float32
        )
    sums = []
    for item in chains:
        stat = results[slot, 1 + item % 2, item // 2]
        sums.append(jnp.sum(stat * stat, axis=0, keepdims=True))
    norms = [jnp.sqrt(jnp.sum(each, axis=1, keepdims=True)) for each in sums]
    for item in chains:
        scaled[item] = results[slot, 1 + item % 2, item // 2] * (1.0 / norms[item])
    factors = [lax.rsqrt(jnp.sqrt(norm)) for norm in norms]

    for repeat in range(ROOT_ITERS - 1):
        for item in chains:
            quarter = (identity - scaled[item]) * 0.25
            pairs[item, size:] = quarter.astype(jnp.bfloat16)
            if repeat == 0:
                roots[item] = identity + quarter
            else:
                pairs[item, :size] = roots[item].astype(jnp.bfloat16)
        if repeat == 0:
            squares = [dot32(pairs[item, size:], pairs[item, size:]) for item in chains]
        else:
            both = [dot32(pairs[item], pairs[item, size:]) for item in chains]
            for item in chains:
                roots[item] = roots[item] + both[item][:size]
            squares = [each[size:] for each in both]
        seconds = [(identity - scaled[item]) * 0.5 + squares[item] for item in chains]
        seconds16 = [second.astype(jnp.bfloat16) for second in seconds]
        fourths = [2.0 * seconds[item] + dot32(seconds16[item], seconds16[item]) for item in chains]
        for item in chains:
            high[item], low[item] = two_terms(scaled[item])
            powers[item, :size], powers[item, size:] = two_terms(fourths[item])
        for item in chains:
            both_terms = dot32(powers[item], high[item])
            scaled[item] = scaled[item] + (
                both_terms[:size] + both_terms[size:] + dot32(powers[item, :size], low[item])
            )
    for item in chains:
        pairs[item, size:] = ((identity - scaled[item]) * 0.25).astype(jnp.bfloat16)
        pairs[item, :size] = roots[item].astype(jnp.bfloat16)
    for item in chains:
        ends = two_terms(roots[item] + dot32(pairs[item, :size], pairs[item, size:]))
        if item % 2 == 0:
            powers[item, :size], powers[item, size:] = ends
        else:
            high[item], low[item] = ends
    halves = []
    for block in range(count):
        both_terms = dot32(powers[2 * block], grad16[block])
        halves.append(both_terms[:size] + both_terms[size:])
    for block in range(count):
        pairs[block, :size], pairs[block, size:] = two_terms(halves[block])
    for block in range(count):
        item = 2 * block + 1
        both_terms = dot32(pairs[block], high[item])
        product = both_terms[:size] + both_terms[size:] + dot32(pairs[block, :size], low[item])
        rate = RATE_BLOCK * factors[2 * block] * factors[item]
        results[slot, 3, block] = master_refs[block][0] - rate * product
    for copy in copies(step, slot):
        copy.start()

    @pl.when(step == steps - 1)
    def _():
        @pl.when(steps >= 2)
        def _():
            for copy in copies(step - 1, 1 - slot):
                copy.wait()

        for copy in copies(step, slot):
            copy.wait()


def shampoo(grads, left_stats, right_stats, master_blocks, places, priors, waits=()):
    part, size, _ = grads[0].shape
    count = next(each for each in (3, 2, 1) if part % each == 0)
    own = pl.BlockSpec((count, size, size), lambda step, places: (step, 0, 0))
    anywhere = pl.BlockSpec(memory_space=pl.ANY)

    def single(block):
        return pl.BlockSpec((1, size, size), lambda step, places: (places[step * count + block], 0, 0))

    result = jax.ShapeDtypeStruct(left_stats.shape, jnp.float32)
    held = len(priors)
    first_prior = 1 + len(grads) + 3 * count
    wide = pltpu.VMEM((2 * count, 2 * size, size), jnp.bfloat16)
    plain = pltpu.VMEM((2 * count, size, size), jnp.bfloat16)
    return pl.pallas_call(
        functools.partial(shampoo_kernel, count, len(grads), held + len(waits)),
        grid_spec=pltpu.PrefetchScalarGridSpec(
            num_scalar_prefetch=1,
            grid=(part // count,),
            in_specs=[own] * len(grads)
            + [single(block) for block in range(count)] * 3
            + [anywhere] * (held + len(waits)),
            out_specs=[anywhere] * 4,
            scratch_shapes=[
                pltpu.VMEM((2, 4, count, size, size), jnp.float32),
                pltpu.VMEM((2 * count, size, size), jnp.float32),
                pltpu.VMEM((2 * count, size, size), jnp.float32),
                wide,
                wide,
                plain,
                plain,
                pltpu.SemaphoreType.DMA((2, 4, count)),
            ],
        ),
        out_shape=[result] * 4,
        input_output_aliases={first_prior + index: index for index in range(held)},
        compiler_params=kernel_params(),
        cost_estimate=pl.CostEstimate(
            flops=part * 130 * 2 * size**3, bytes_accessed=part * size * size * 30, transcendentals=0
        ),
        name="shampoo",
    )(
        places,
        *grads,
        *([left_stats] * count),
        *([right_stats] * count),
        *([master_blocks] * count),
        *priors,
        *waits,
    )


def after(value, *earlier):
    return lax.optimization_barrier((value,) + earlier)[0]


def onward(part, axis):
    ways = lax.axis_size(axis)
    return lax.ppermute(part, axis, [(each, (each + 1) % ways) for each in range(ways)])


def swap(part, bits):
    ways = lax.axis_size("dp")
    return lax.ppermute(part, "dp", [(each, each ^ bits) for each in range(ways)])


def small_rows(values, ways):
    return jnp.pad(values, ((0, 0), (0, -values.shape[1] % 2048))).reshape(-1, 128)


def shards(
    tokens,
    cotangent,
    segments,
    subsets,
    packs,
    master_blocks,
    left_stats,
    right_stats,
    local_vecs,
    local_vec_stats,
    shared_vecs,
    shared_vec_stats,
):
    tp_ways = lax.axis_size("tp")
    dp_ways = lax.axis_size("dp")
    tp_rank = lax.axis_index("tp")
    tok_dev, model_width = tokens.shape
    group_tok = tok_dev * tp_ways
    pack_count, pack_len = segments.shape
    seg_width = subsets.shape[1]
    heads_dev = HEADS // tp_ways
    ff_dev = FF // tp_ways
    head_cols = heads_dev * HD
    owned, block_size, _ = master_blocks.shape
    block_rows = model_width // block_size
    first_out = block_rows * (3 * head_cols // block_size)
    first_in = first_out + head_cols // block_size * block_rows
    first_down = first_in + block_rows * (ff_dev // block_size)
    all_count = owned * dp_ways
    vec_rows = 3 * heads_dev + ff_dev // HD

    vec_used = local_vecs.size
    shared_used = shared_vecs.size
    vec_flat = jnp.concatenate([local_vecs.reshape(-1), shared_vecs.reshape(-1)])
    extra = jnp.pad(vec_flat, (0, EXTRA_ROWS * block_size - vec_flat.size)).reshape(EXTRA_ROWS, block_size)
    rows16 = jnp.concatenate([master_blocks.reshape(-1, block_size), extra], 0).astype(jnp.bfloat16)
    blocks = lax.all_gather(rows16, "dp", axis=0, tiled=True)

    token_parts = [tokens]
    for step in range(1, tp_ways):
        token_parts.append(onward(token_parts[-1], "tp"))

    gathered = blocks.reshape(dp_ways, -1, block_size)[:, owned * block_size :].reshape(dp_ways, -1)
    vec_values = (
        gathered[:, :vec_used].reshape(dp_ways, vec_rows, -1).transpose(1, 0, 2).reshape(vec_rows, HD)
    ).astype(jnp.float32)
    shared_mine = gathered[:, vec_used : vec_used + shared_used]
    shared_all = jnp.zeros((tp_ways,) + shared_mine.shape, jnp.bfloat16)
    for step in range(tp_ways):
        part = shared_mine
        if step:
            part = lax.ppermute(
                part, "tp", [(each, (each + step) % tp_ways) for each in range(tp_ways)]
            )
        shared_all = lax.dynamic_update_slice(
            shared_all, part[None], ((tp_rank - step) % tp_ways, 0, 0)
        )
    norm_params = (
        shared_all.reshape(tp_ways, dp_ways, 6, -1).transpose(2, 1, 0, 3).reshape(6, model_width)
    ).astype(jnp.float32)
    bias_qkv = vec_values[: 3 * heads_dev].reshape(1, -1)
    bias_in = vec_values[3 * heads_dev :].reshape(1, -1)

    own_pos = tp_rank * tok_dev + jnp.arange(tok_dev)
    own_pack = own_pos // pack_len
    valid_own = (own_pack < packs[0]).astype(jnp.float32)
    owned_input_rows = tokens.astype(jnp.float32)
    owned_centred_scaled, owned_inverse_deviation = apply_layer_norm(owned_input_rows)

    group_pack = jnp.arange(group_tok) // pack_len
    lookup_key = group_pack * seg_width + segments.reshape(-1)
    onehot = lookup_key[:, None] == jnp.arange(pack_count * seg_width)[None, :]
    subset_tok = jnp.sum(jnp.where(onehot, subsets.reshape(-1)[None, :], 0), axis=1)
    weight = 0.5 + subset_tok.astype(jnp.float32) / (SUBSETS - 1)
    factor = (weight * (group_pack < packs[0]).astype(jnp.float32))[:, None]
    own_factor = lax.dynamic_slice_in_dim(factor, tp_rank * tok_dev, tok_dev, 0)
    seed16 = (cotangent.astype(jnp.float32) * own_factor).astype(jnp.bfloat16)

    rank = tp_rank.astype(jnp.int32)[None]
    cosines, sines = turn_tables(pack_len, 128)
    cotangent_parts = [cotangent, onward(after(cotangent, token_parts[-1], shared_all), "tp")]
    qkv16, first_turned, second_normed, second_turned, group_tokens, mean, inverse = project_qkv(
        token_parts, rank, blocks, owned, norm_params, bias_qkv, cosines, sines, heads_dev
    )
    attended, attended_turned = attend(qkv16, segments, heads_dev)
    cotangent_parts.append(onward(after(cotangent_parts[-1], attended), "tp"))
    active_turned, slope, partial_value = feed_forward(
        second_normed, attended, blocks, owned, bias_in, (first_out, first_in, first_down)
    )
    while len(cotangent_parts) < tp_ways:
        cotangent_parts.append(onward(after(cotangent_parts[-1], slope), "tp"))

    back_args = (
        tp_ways, rank, factor, slope, group_tokens, mean, inverse, blocks, owned, norm_params,
        (first_out, first_in, first_down), head_cols,
    )
    early = feed_back(cotangent_parts[:-1], 0, *back_args, ())
    late = feed_back(cotangent_parts[-1:], tp_ways - 1, *back_args, early[:4])
    seed_all, d_attended, d_hidden16, dz_part = late[:4]
    branch = lax.psum_scatter(
        after(partial_value, cotangent_parts[-1], early[5]), "tp", scatter_dimension=0, tiled=True
    )
    d_qkv16 = attend_back(qkv16, d_attended, segments, cosines, sines, heads_dev)
    dz16, first_sums, qkv_sums = qkv_back(
        d_qkv16, dz_part, group_tokens, mean, inverse, blocks, owned, norm_params
    )

    dz_rows = lambda back: lax.dynamic_slice_in_dim(dz16, (tp_rank - back) % tp_ways * tok_dev, tok_dev, 0)
    back = 2

    def pass_on(moving, back):
        total = moving.astype(jnp.float32) + dz_rows(back).astype(jnp.float32)
        return total if back == tp_ways else onward(total.astype(jnp.bfloat16), "tp")

    shared_local = jnp.concatenate(
        [
            jnp.sum(first_sums.reshape(2, 8, model_width), axis=1),
            jnp.sum((early[4][:16] + late[4][:16]).reshape(2, 8, model_width), axis=1),
            jnp.sum(early[4][16:], axis=0)[None],
        ],
        0,
    )
    vecs_local = jnp.concatenate(
        [
            jnp.sum(qkv_sums, axis=0).reshape(3 * heads_dev, HD),
            jnp.sum(early[5] + late[5], axis=0).reshape(ff_dev // HD, HD),
        ],
        0,
    )
    small = jnp.concatenate(
        [
            shared_local.reshape(5, dp_ways, -1).transpose(1, 0, 2).reshape(dp_ways, -1),
            vecs_local.reshape(vec_rows, dp_ways, -1).transpose(1, 0, 2).reshape(dp_ways, -1),
        ],
        1,
    )
    small_in = after(small_rows(small, dp_ways), branch)
    small_own = lax.psum_scatter(small_in, "dp", scatter_dimension=0, tiled=True).reshape(-1)
    output = (
        valid_own[:, None]
        * (owned_input_rows + branch.astype(jnp.float32) + norm_params[4] + norm_params[5])
    ).astype(jnp.bfloat16)

    shared_size = 5 * model_width // dp_ways
    own_vec_grads = small_own[shared_size : small.shape[1]].reshape(vec_rows, HD // dp_ways)
    shared_part = small_own[:shared_size].reshape(5, tp_ways, -1).transpose(1, 0, 2)
    shared_own = lax.psum_scatter(
        small_rows(shared_part.reshape(tp_ways, -1), tp_ways), "tp", scatter_dimension=0, tiled=True
    ).reshape(-1)
    shared_own = shared_own[: shared_size // tp_ways].reshape(5, -1)
    shared_grads = jnp.concatenate([shared_own, shared_own[4:]], 0)
    dp_rank = lax.axis_index("dp").astype(jnp.int32)
    lefts = (first_turned, second_turned, active_turned, attended_turned)
    d_qkv_late, first_rows = lax.optimization_barrier((d_qkv16, dz_rows(1)))
    moving = onward(first_rows, "tp")
    rights = (d_hidden16, seed_all, d_qkv_late)
    firsts = (0, first_out, first_in, first_down)
    qkv_blocks = 3 * head_cols // block_size
    parts = 4
    by_part = (
        dp_ways == 8
        and owned == parts * qkv_blocks
        and block_rows == 2 * parts
        and ff_dev == model_width
        and owned % block_rows == 0
        and first_out % block_rows == 0
        and first_in % block_rows == 0
    )
    results = ()
    if by_part:
        part_size = owned // parts
        span = block_rows // parts
        sums = []
        terms = []
        ready = []

        def send_on(part):
            if part:
                sums[part] = [sums[part][0]] + [after(each, terms[-1][3]) for each in sums[part][1:]]
                ready.append(sums[part][3])
            terms.append([sums[part][0]] + [swap(sums[part][bits], 2 * bits) for bits in range(1, 4)])

        for part in range(parts):
            waits = (sums[part - 2][0],) if part >= 2 else ()
            if part == parts - 1:
                send_on(0)
                waits += tuple(terms[0][1:])
            kept, away = weight_grads(
                part, parts, lefts, rights, firsts, (dp_rank % 2)[None], owned, dp_ways, block_size, waits
            )
            sums.append(pair_sum(kept, swap(away, 1), (dp_rank // 2)[None], dp_ways // 2))
        moving = pass_on(after(moving, kept), back)
        back += 1
        for part in range(1, parts):
            send_on(part)
        count = jnp.arange(part_size, dtype=jnp.int32)
        in_qkv = dp_rank * owned < first_out
        for part in range(parts):
            places = jnp.where(
                in_qkv,
                part * part_size + count,
                count // span * block_rows + part * span + count % span,
            )
            waits = []
            if part < parts - 1:
                waits.append(ready[part])
            if part == 1:
                waits.append(small_in)
            if part == 2:
                waits.append(small_own)
            if part == 3:
                waits += [output, shared_own]
            results = shampoo(
                terms[part], left_stats, right_stats, master_blocks, places, results, waits
            )
            if part % 2 == 1 and back <= tp_ways:
                moving, first_result = lax.optimization_barrier((moving, results[0]))
                results = [first_result] + list(results[1:])
                moving = pass_on(moving, back)
                back += 1
    else:
        local = [
            to_blocks(jnp.dot(left, right, preferred_element_type=jnp.float32).astype(jnp.bfloat16), block_size)
            for left, right in (
                (first_turned, d_qkv_late),
                (attended_turned, seed_all),
                (second_turned, d_hidden16),
                (active_turned, seed_all),
            )
        ]
        grads16 = lax.psum_scatter(jnp.concatenate(local, 0), "dp", scatter_dimension=0, tiled=True)
        results = shampoo(
            [grads16], left_stats, right_stats, master_blocks, jnp.arange(owned, dtype=jnp.int32), results
        )
    while back <= tp_ways:
        moving = pass_on(moving, back)
        back += 1
    norm_input_gradient = moving
    own_grads, left_new, right_new, new_blocks = results
    average_gradient = jnp.mean(norm_input_gradient, axis=-1, keepdims=True)
    average_projection = jnp.mean(
        norm_input_gradient * owned_centred_scaled, axis=-1, keepdims=True
    )
    input_grad = seed16.astype(jnp.float32) + owned_inverse_deviation * (
        norm_input_gradient - average_gradient - owned_centred_scaled * average_projection
    )

    local_stat_new = DECAY * local_vec_stats + own_vec_grads * own_vec_grads
    local_new = local_vecs - RATE_VEC * own_vec_grads * lax.rsqrt(local_stat_new)
    shared_stat_new = DECAY * shared_vec_stats + shared_grads * shared_grads
    shared_new = shared_vecs - RATE_VEC * shared_grads * lax.rsqrt(shared_stat_new)
    return (
        output,
        input_grad,
        own_grads,
        left_new,
        right_new,
        new_blocks,
        own_vec_grads,
        local_stat_new,
        local_new,
        shared_grads,
        shared_stat_new,
        shared_new,
    )


def solution(mesh):
    placed = (
        P(("dp", "tp"), None),
        P(("dp", "tp"), None),
        P("dp", None),
        P("dp", None),
        P("dp"),
        P(("dp", "tp"), None, None),
        P(("dp", "tp"), None, None),
        P(("dp", "tp"), None, None),
        P("tp", "dp"),
        P("tp", "dp"),
        P(None, ("dp", "tp")),
        P(None, ("dp", "tp")),
    )
    return jax.shard_map(
        shards,
        mesh=mesh,
        in_specs=placed,
        out_specs=(
            P(("dp", "tp"), None),
            P(("dp", "tp"), None),
            P(("dp", "tp"), None, None),
            P(("dp", "tp"), None, None),
            P(("dp", "tp"), None, None),
            P(("dp", "tp"), None, None),
            P("tp", "dp"),
            P("tp", "dp"),
            P("tp", "dp"),
            P(None, ("dp", "tp")),
            P(None, ("dp", "tp")),
            P(None, ("dp", "tp")),
        ),
        check_vma=False,
    )
```

```python
import functools
import math

import jax
import jax.numpy as jnp
from jax import lax
from jax.experimental import pallas as pl
from jax.experimental.pallas import tpu as pltpu
from jax.sharding import PartitionSpec as P

HEADS = 8
HD = 256
ROT = 64
FF = 8192
SUBSETS = 22
ROOT_ITERS = 8


EPS_NORM = 1e-05
DECAY = 0.5
RATE_BLOCK = 0.6
RATE_VEC = 0.2
NEG_FILL = -1e30
DOC_MAX = 512
HALF_ROOT = 0.7071067811865476
DENSITY_SCALE = 0.3989422804014327


def to_blocks(matrix, block_size):
    block_rows = matrix.shape[0] // block_size
    block_cols = matrix.shape[1] // block_size
    return (
        matrix.reshape(block_rows, block_size, block_cols, block_size)
        .transpose(0, 2, 1, 3)
        .reshape(block_rows * block_cols, block_size, block_size)
    )


EXTRA_ROWS = 16
FEED_BACK_TILE = 512
VMEM_LIMIT = 60 << 20
NN = (((1,), (0,)), ((), ()))
NT = (((1,), (1,)), ((), ()))
TN = (((0,), (0,)), ((), ()))


def contract(left_arg, right_arg, dims):
    return lax.dot_general(left_arg, right_arg, dims, preferred_element_type=jnp.float32)


def kernel_params():
    return pltpu.CompilerParams(vmem_limit_bytes=VMEM_LIMIT)


def block_row(index, owned, size):
    return index // owned * (owned * size + EXTRA_ROWS) + index % owned * size


def block_copies(blocks_ref, owned, first, rows, cols, target, sems):
    size = blocks_ref.shape[-1]
    return [
        pltpu.make_async_copy(
            blocks_ref.at[pl.ds(block_row(first + row * cols + col, owned, size), size), :],
            target.at[pl.ds(row * size, size), pl.ds(col * size, size)],
            sems.at[row * cols + col],
        )
        for row in range(rows)
        for col in range(cols)
    ]


def begin_copies(copies):
    @pl.when(pl.program_id(0) == 0)
    def _():
        for copy in copies:
            copy.start()


def end_copies(copies):
    @pl.when(pl.program_id(0) == 0)
    def _():
        for copy in copies:
            copy.wait()


def wait_for(copies):
    for copy in copies:
        copy.wait()


def both_ways(steps, work):
    if steps == 1:
        work(True)
        return
    step = pl.program_id(0)

    @pl.when(step == 0)
    def _():
        work(True)

    @pl.when(step > 0)
    def _():
        work(False)


def turn(values, cosines, sines):
    lane = lax.broadcasted_iota(jnp.int32, values.shape, 1)
    half = ROT // 2
    wide = values.shape[1]
    swapped = jnp.where(
        lane < half, pltpu.roll(values, wide - half, 1), pltpu.roll(values, half, 1)
    )
    return values * cosines + swapped * sines


def turn_tables(pack_len, lanes):
    half = ROT // 2
    positions = jnp.arange(pack_len).astype(jnp.float32)
    freqs = 10000.0 ** (-(jnp.arange(half).astype(jnp.float32) * 2.0) / ROT)
    angles = positions[:, None] * freqs[None, :]
    cosines = jnp.cos(angles)
    sines = jnp.sin(angles)
    rest = jnp.zeros((pack_len, lanes - ROT), jnp.float32)
    return (
        jnp.concatenate([cosines, cosines, rest + 1.0], -1),
        jnp.concatenate([-sines, sines, rest], -1),
    )


def normed_rows(rows):
    mean = jnp.mean(rows, axis=1, keepdims=True)
    centred = rows - mean
    variance = jnp.mean(centred * centred, axis=1, keepdims=True)
    return mean, lax.rsqrt(variance + EPS_NORM)


def part_copies(part_refs, held, sems):
    return [
        pltpu.make_async_copy(part, held.at[index], sems.at[index])
        for index, part in enumerate(part_refs)
    ]


def await_part(copies, per_part):
    step = pl.program_id(0)
    for index, copy in enumerate(copies):

        @pl.when(step == index * per_part)
        def _():
            copy.wait()


def qkv_kernel(heads, owned, parts, rank_ref, *refs):
    part_refs = refs[:parts]
    blocks_ref, norm_ref, bias_ref, cos_ref, sin_ref = refs[parts : parts + 5]
    outs, (normed, weight, held, sems, part_sems) = refs[parts + 5 : parts + 12], refs[parts + 12 :]
    qkv_ref, first_turned, second_ref, second_turned, tokens_ref, mean_ref, inverse_ref = outs
    size = blocks_ref.shape[-1]
    copies = block_copies(blocks_ref, owned, 0, weight.shape[0] // size, weight.shape[1] // size, weight, sems)
    moves = part_copies(part_refs, held, part_sems)
    cols_all = weight.shape[1] // size
    begin_copies(moves + [copy for col in range(cols_all) for copy in copies[col::cols_all]])
    await_part(moves, 1)
    own = held[pl.program_id(0)]
    tokens_ref[...] = own
    rows = own.astype(jnp.float32)
    mean, inverse = normed_rows(rows)
    mean_ref[...] = mean
    inverse_ref[...] = inverse
    for col in range(rows.shape[1] // size):
        cols = pl.ds(col * size, size)
        scaled = (own[:, col * size : (col + 1) * size].astype(jnp.float32) - mean) * inverse
        second = (scaled * norm_ref[2:3, cols] + norm_ref[3:4, cols]).astype(jnp.bfloat16)
        second_ref[:, cols] = second
        second_turned[cols, :] = second.T
        first = (scaled * norm_ref[0:1, cols] + norm_ref[1:2, cols]).astype(jnp.bfloat16)
        normed[:, cols] = first
        first_turned[cols, :] = first.T
    lanes = cos_ref.shape[1]

    def work(fresh):
        for head in range(heads):
            for part in range(3):
                index = head * 3 + part
                if fresh:
                    wait_for(copies[index::cols_all])
                cols = pl.ds(index * HD, HD)
                result = contract(normed[...], weight[:, cols], NN) + bias_ref[:, cols]
                if part < 2:
                    first = turn(result[:, :lanes], cos_ref[...], sin_ref[...])
                    result = jnp.concatenate([first, result[:, lanes:]], 1)
                if part == 0:
                    result = result * (1.0 / math.sqrt(HD))
                qkv_ref[:, cols] = result.astype(jnp.bfloat16)

    both_ways(parts, work)


def project_qkv(parts, rank, blocks, owned, norm_params, bias, cosines, sines, heads):
    ways = len(parts)
    tile, width = parts[0].shape
    tokens = ways * tile
    size = blocks.shape[-1]
    pack_len, lanes = cosines.shape
    cols = 3 * heads * HD
    per_pack = pack_len // tile
    place = lambda i, rank: (rank[0] - i + ways) % ways
    row = lambda n: pl.BlockSpec((tile, n), lambda i, rank: (place(i, rank), 0))
    table = pl.BlockSpec((tile, lanes), lambda i, rank: (place(i, rank) % per_pack, 0))
    anywhere = pl.BlockSpec(memory_space=pl.ANY)
    wide = jax.ShapeDtypeStruct((tokens, width), jnp.bfloat16)
    tall = jax.ShapeDtypeStruct((width, tokens), jnp.bfloat16)
    single = jax.ShapeDtypeStruct((tokens, 1), jnp.float32)
    turned = pl.BlockSpec((width, tile), lambda i, rank: (0, place(i, rank)))
    return pl.pallas_call(
        functools.partial(qkv_kernel, heads, owned, ways),
        grid_spec=pltpu.PrefetchScalarGridSpec(
            num_scalar_prefetch=1,
            grid=(ways,),
            in_specs=[anywhere] * (ways + 1)
            + [
                pl.BlockSpec(norm_params.shape, lambda i, rank: (0, 0)),
                pl.BlockSpec((1, cols), lambda i, rank: (0, 0)),
                table,
                table,
            ],
            out_specs=[row(cols), turned, row(width), turned, row(width), row(1), row(1)],
            scratch_shapes=[
                pltpu.VMEM((tile, width), jnp.bfloat16),
                pltpu.VMEM((width, cols), jnp.bfloat16),
                pltpu.VMEM((ways, tile, width), jnp.bfloat16),
                pltpu.SemaphoreType.DMA((width // size * (cols // size),)),
                pltpu.SemaphoreType.DMA((ways,)),
            ],
        ),
        out_shape=[jax.ShapeDtypeStruct((tokens, cols), jnp.bfloat16), tall, wide, tall, wide, single, single],
        compiler_params=kernel_params(),
        cost_estimate=pl.CostEstimate(
            flops=2 * tokens * width * cols, bytes_accessed=tokens * (4 * width + cols) * 2 + width * cols * 2, transcendentals=0
        ),
        name="qkv",
    )(rank, *parts, blocks, norm_params, bias, cosines, sines)


def attend_kernel(query_ref, key_ref, value_ref, seg_row, seg_col, out_ref, turned_ref):
    length = key_ref.shape[0]
    step = 256
    for start in range(0, length, step):
        first = max(0, start - DOC_MAX)
        stop = start + step
        scores = contract(query_ref[start:stop, :], key_ref[first:stop, :], NT)
        row = lax.broadcasted_iota(jnp.int32, scores.shape, 0) + start
        col = lax.broadcasted_iota(jnp.int32, scores.shape, 1) + first
        allowed = (col <= row) & (seg_col[0, start:stop, :] == seg_row[0, :, first:stop])
        masked = jnp.where(allowed, scores, NEG_FILL)
        exp_terms = jnp.exp(masked - jnp.max(masked, axis=1, keepdims=True))
        probs = exp_terms * (1.0 / jnp.sum(exp_terms, axis=1, keepdims=True))
        result = contract(probs.astype(jnp.bfloat16), value_ref[first:stop, :], NN).astype(jnp.bfloat16)
        out_ref[start:stop, :] = result
        turned_ref[:, start:stop] = result.T


def attend(qkv, segments, heads):
    packs, length = segments.shape
    part = lambda which: pl.BlockSpec((length, HD), lambda p, h: (p, h * 3 + which))
    return pl.pallas_call(
        attend_kernel,
        grid=(packs, heads),
        in_specs=[
            part(0),
            part(1),
            part(2),
            pl.BlockSpec((1, 1, length), lambda p, h: (p, 0, 0)),
            pl.BlockSpec((1, length, 1), lambda p, h: (p, 0, 0)),
        ],
        out_specs=[
            pl.BlockSpec((length, HD), lambda p, h: (p, h)),
            pl.BlockSpec((HD, length), lambda p, h: (h, p)),
        ],
        out_shape=[
            jax.ShapeDtypeStruct((packs * length, heads * HD), jnp.bfloat16),
            jax.ShapeDtypeStruct((heads * HD, packs * length), jnp.bfloat16),
        ],
        compiler_params=kernel_params(),
        cost_estimate=pl.CostEstimate(
            flops=packs * heads * length * length * HD * 3, bytes_accessed=packs * length * heads * HD * 8, transcendentals=0
        ),
        name="attend",
    )(qkv, qkv, qkv, segments[:, None, :], segments[:, :, None])


def attend_back_kernel(
    query_ref, key_ref, value_ref, d_out_ref, seg_row, seg_col, cos_ref, sin_ref, grad_ref, d_key, d_value
):
    length = key_ref.shape[0]
    step = 256
    lanes = cos_ref.shape[1]
    d_key[...] = jnp.zeros_like(d_key)
    d_value[...] = jnp.zeros_like(d_value)
    for start in range(0, length, step):
        first = max(0, start - DOC_MAX)
        stop = start + step
        query = query_ref[start:stop, :]
        d_out = d_out_ref[start:stop, :]
        keys = key_ref[first:stop, :]
        scores = contract(keys, query, NT)
        key_pos = lax.broadcasted_iota(jnp.int32, scores.shape, 0) + first
        query_pos = lax.broadcasted_iota(jnp.int32, scores.shape, 1) + start
        allowed = (key_pos <= query_pos) & (seg_col[0, first:stop, :] == seg_row[0, :, start:stop])
        masked = jnp.where(allowed, scores, NEG_FILL)
        exp_terms = jnp.exp(masked - jnp.max(masked, axis=0, keepdims=True))
        probs = exp_terms * (1.0 / jnp.sum(exp_terms, axis=0, keepdims=True))
        d_probs = contract(value_ref[first:stop, :], d_out, NT)
        row_dot = jnp.sum(probs * d_probs, axis=0, keepdims=True)
        d_scores = (probs * (d_probs - row_dot)).astype(jnp.bfloat16)
        d_value[first:stop, :] += contract(probs.astype(jnp.bfloat16), d_out, NN)
        d_key[first:stop, :] += contract(d_scores, query, NN)
        d_query = contract(d_scores, keys, TN) * (1.0 / math.sqrt(HD))
        back = turn(d_query[:, :lanes], cos_ref[start:stop, :], -sin_ref[start:stop, :])
        grad_ref[start:stop, :lanes] = back.astype(jnp.bfloat16)
        grad_ref[start:stop, lanes:HD] = d_query[:, lanes:].astype(jnp.bfloat16)
    back = turn(d_key[:, :lanes], cos_ref[...], -sin_ref[...])
    grad_ref[:, HD : HD + lanes] = back.astype(jnp.bfloat16)
    grad_ref[:, HD + lanes : 2 * HD] = d_key[:, lanes:].astype(jnp.bfloat16)
    grad_ref[:, 2 * HD :] = d_value[...].astype(jnp.bfloat16)


def attend_back(qkv, d_attended, segments, cosines, sines, heads):
    packs, length = segments.shape
    lanes = cosines.shape[1]
    part = lambda which: pl.BlockSpec((length, HD), lambda p, h: (p, h * 3 + which))
    table = pl.BlockSpec((length, lanes), lambda p, h: (0, 0))
    return pl.pallas_call(
        attend_back_kernel,
        grid=(packs, heads),
        in_specs=[
            part(0),
            part(1),
            part(2),
            pl.BlockSpec((length, HD), lambda p, h: (p, h)),
            pl.BlockSpec((1, 1, length), lambda p, h: (p, 0, 0)),
            pl.BlockSpec((1, length, 1), lambda p, h: (p, 0, 0)),
            table,
            table,
        ],
        out_specs=pl.BlockSpec((length, 3 * HD), lambda p, h: (p, h)),
        out_shape=jax.ShapeDtypeStruct((packs * length, 3 * heads * HD), jnp.bfloat16),
        scratch_shapes=[pltpu.VMEM((length, HD), jnp.float32)] * 2,
        compiler_params=kernel_params(),
        cost_estimate=pl.CostEstimate(
            flops=packs * heads * length * length * HD * 7, bytes_accessed=packs * length * heads * HD * 16, transcendentals=0
        ),
        name="attend_back",
    )(qkv, qkv, qkv, d_attended, segments[:, None, :], segments[:, :, None], cosines, sines)


def feed_kernel(
    steps, offsets, owned, x_ref, attended_ref, blocks_ref, bias_ref, turned_ref, slope_ref, out_ref, act_ref, w_in, w_down, sems_in, sems_down
):
    size = blocks_ref.shape[-1]
    width, hidden_units = w_in.shape
    inner = hidden_units // size
    first_out, first_in, first_down = offsets
    head_rows = attended_ref.shape[1] // size
    outer = width // size
    copies_in = block_copies(blocks_ref, owned, first_in, outer, inner, w_in, sems_in)
    copies_down = block_copies(blocks_ref, owned, first_down, inner, outer, w_down.at[pl.ds(0, hidden_units)], sems_down)
    copies_down += block_copies(
        blocks_ref,
        owned,
        first_out,
        head_rows,
        outer,
        w_down.at[pl.ds(hidden_units, head_rows * size)],
        sems_down.at[pl.ds(inner * outer, head_rows * outer)],
    )
    begin_copies(
        [copy for col in range(inner) for copy in copies_in[col::inner]]
        + [copy for col in range(outer) for copy in copies_down[col::outer]]
    )

    def work(fresh):
        for col in range(inner):
            if fresh:
                wait_for(copies_in[col::inner])
            cols = pl.ds(col * size, size)
            hidden = contract(x_ref[...], w_in[:, cols], NN) + bias_ref[:, cols]
            cdf = 0.5 + 0.5 * lax.erf(hidden * HALF_ROOT)
            density = jnp.exp(-0.5 * hidden * hidden) * DENSITY_SCALE
            activated = (hidden * cdf).astype(jnp.bfloat16)
            act_ref[:, cols] = activated
            turned_ref[cols, :] = activated.T
            slope_ref[:, cols] = (cdf + hidden * density).astype(jnp.bfloat16)
        for col in range(outer):
            if fresh:
                wait_for(copies_down[col::outer])
            cols = pl.ds(col * size, size)
            out_ref[:, cols] = (
                contract(act_ref[...], w_down[:hidden_units, cols], NN)
                + contract(attended_ref[...], w_down[hidden_units:, cols], NN)
            ).astype(jnp.bfloat16)

    both_ways(steps, work)


def feed_forward(normed, attended, blocks, owned, bias, offsets):
    tokens, width = normed.shape
    size = blocks.shape[-1]
    hidden_units = bias.shape[1]
    head_cols = attended.shape[1]
    tile = 512
    row = lambda cols: pl.BlockSpec((tile, cols), lambda i: (i, 0))
    inner, outer = hidden_units // size, width // size
    return pl.pallas_call(
        functools.partial(feed_kernel, tokens // tile, offsets, owned),
        grid=(tokens // tile,),
        in_specs=[
            row(width),
            row(head_cols),
            pl.BlockSpec(memory_space=pl.ANY),
            pl.BlockSpec((1, hidden_units), lambda i: (0, 0)),
        ],
        out_specs=[
            pl.BlockSpec((hidden_units, tile), lambda i: (0, i)), row(hidden_units), row(width),
        ],
        out_shape=[
            jax.ShapeDtypeStruct((hidden_units, tokens), jnp.bfloat16),
            jax.ShapeDtypeStruct((tokens, hidden_units), jnp.bfloat16),
            jax.ShapeDtypeStruct((tokens, width), jnp.bfloat16),
        ],
        scratch_shapes=[
            pltpu.VMEM((tile, hidden_units), jnp.bfloat16),
            pltpu.VMEM((width, hidden_units), jnp.bfloat16),
            pltpu.VMEM((hidden_units + head_cols, width), jnp.bfloat16),
            pltpu.SemaphoreType.DMA((inner * outer,)),
            pltpu.SemaphoreType.DMA((inner * outer + head_cols // size * outer,)),
        ],
        compiler_params=kernel_params(),
        cost_estimate=pl.CostEstimate(
            flops=2 * tokens * width * (2 * hidden_units + head_cols), bytes_accessed=tokens * width * 10 + width * hidden_units * 4, transcendentals=0
        ),
        name="feed",
    )(normed, attended, blocks, bias)


def column_sum(values):
    rows, cols = values.shape
    return jnp.sum(values.reshape(rows // 8, 8, cols), axis=0)


def feed_back_kernel(offsets, owned, first_part, parts, held_count, rank_ref, *refs):
    part_refs = refs[:parts]
    factor_ref, slope_ref, tokens_ref, mean_ref, inverse_ref, blocks_ref, norm_ref = refs[parts : parts + 7]
    (
        seed_ref, d_attended_ref, d_hidden_ref, dz_ref, norm_sums, hidden_sums,
        w_in, w_down, w_out, held, sems_in, sems_down, sems_out, part_sems,
    ) = refs[parts + 7 + held_count :]
    size = blocks_ref.shape[-1]
    width, hidden_units = w_in.shape
    inner, outer = hidden_units // size, width // size
    first_out, first_in, first_down = offsets
    tile = seed_ref.shape[0]
    per_part = held.shape[1] // tile
    moves = part_copies(part_refs, held, part_sems)
    copies_out = block_copies(blocks_ref, owned, first_out, w_out.shape[0] // size, outer, w_out, sems_out)
    copies_down = block_copies(blocks_ref, owned, first_down, inner, outer, w_down, sems_down)
    copies_in = block_copies(blocks_ref, owned, first_in, outer, inner, w_in, sems_in)
    begin_copies(moves + copies_out + copies_down + copies_in)

    @pl.when(pl.program_id(0) == 0)
    def _():
        norm_sums[...] = jnp.zeros_like(norm_sums)
        hidden_sums[...] = jnp.zeros_like(hidden_sums)

    await_part(moves, per_part)
    step = pl.program_id(0)
    cotangent = held[step // per_part, pl.ds(pl.multiple_of(step % per_part * tile, tile), tile), :]
    seed_ref[...] = (cotangent.astype(jnp.float32) * factor_ref[...]).astype(jnp.bfloat16)
    if first_part == 0:

        @pl.when(step < per_part)
        def _():
            norm_sums[16:24, :] += column_sum(seed_ref[...].astype(jnp.float32))

    def work(fresh):
        if fresh:
            wait_for(copies_out)
        d_attended_ref[...] = contract(seed_ref[...], w_out[...], NT).astype(jnp.bfloat16)
        for col in range(inner):
            if fresh:
                wait_for(copies_down[col * outer : (col + 1) * outer])
            cols = pl.ds(col * size, size)
            d_act = contract(seed_ref[...], w_down[cols, :], NT)
            d_hidden = (d_act * slope_ref[:, cols].astype(jnp.float32)).astype(jnp.bfloat16)
            d_hidden_ref[:, cols] = d_hidden
            hidden_sums[:, cols] += column_sum(d_hidden.astype(jnp.float32))
        mean, inverse = mean_ref[...], inverse_ref[...]
        for col in range(outer):
            if fresh:
                wait_for(copies_in[col * inner : (col + 1) * inner])
            cols = pl.ds(col * size, size)
            scaled = (tokens_ref[:, cols].astype(jnp.float32) - mean) * inverse
            second = contract(d_hidden_ref[...], w_in[cols, :], NT)
            dz_ref[:, cols] = (second * norm_ref[2:3, cols]).astype(jnp.bfloat16)
            norm_sums[0:8, cols] += column_sum(second * scaled)
            norm_sums[8:16, cols] += column_sum(second)

    both_ways(parts * per_part, work)


def feed_back(parts, first_part, ways, rank, factor, slope, group_tokens, mean, inverse, blocks, owned, norm_params, offsets, head_cols, priors):
    chunk, width = parts[0].shape
    tokens = ways * chunk
    size = blocks.shape[-1]
    hidden_units = slope.shape[1]
    tile = min(FEED_BACK_TILE, chunk)
    per_part = chunk // tile
    inner, outer = hidden_units // size, width // size
    place = lambda i, rank: (rank[0] - first_part - i // per_part + ways) % ways * per_part + i % per_part
    row = lambda n: pl.BlockSpec((tile, n), lambda i, rank: (place(i, rank), 0))
    whole = lambda rows, cols: pl.BlockSpec((rows, cols), lambda i, rank: (0, 0))
    anywhere = pl.BlockSpec(memory_space=pl.ANY)
    count = len(parts)
    rows = count * chunk
    return pl.pallas_call(
        functools.partial(feed_back_kernel, offsets, owned, first_part, count, len(priors)),
        grid_spec=pltpu.PrefetchScalarGridSpec(
            num_scalar_prefetch=1,
            grid=(count * per_part,),
            in_specs=[anywhere] * count
            + [row(1), row(hidden_units), row(width), row(1), row(1), anywhere]
            + [whole(norm_params.shape[0], width)]
            + [anywhere] * len(priors),
            out_specs=[
                row(width), row(head_cols), row(hidden_units), row(width), whole(24, width), whole(8, hidden_units),
            ],
            scratch_shapes=[
                pltpu.VMEM((width, hidden_units), jnp.bfloat16),
                pltpu.VMEM((hidden_units, width), jnp.bfloat16),
                pltpu.VMEM((head_cols, width), jnp.bfloat16),
                pltpu.VMEM((count, chunk, width), jnp.bfloat16),
                pltpu.SemaphoreType.DMA((inner * outer,)),
                pltpu.SemaphoreType.DMA((inner * outer,)),
                pltpu.SemaphoreType.DMA((head_cols // size * outer,)),
                pltpu.SemaphoreType.DMA((count,)),
            ],
        ),
        out_shape=[
            jax.ShapeDtypeStruct((tokens, width), jnp.bfloat16),
            jax.ShapeDtypeStruct((tokens, head_cols), jnp.bfloat16),
            jax.ShapeDtypeStruct((tokens, hidden_units), jnp.bfloat16),
            jax.ShapeDtypeStruct((tokens, width), jnp.bfloat16),
            jax.ShapeDtypeStruct((24, width), jnp.float32),
            jax.ShapeDtypeStruct((8, hidden_units), jnp.float32),
        ],
        input_output_aliases={1 + count + 7 + index: index for index in range(len(priors))},
        compiler_params=kernel_params(),
        cost_estimate=pl.CostEstimate(
            flops=2 * rows * width * (2 * hidden_units + head_cols), bytes_accessed=rows * width * 14 + width * hidden_units * 4, transcendentals=0
        ),
        name="feed_back",
    )(rank, *parts, factor, slope, group_tokens, mean, inverse, blocks, norm_params, *priors)


def qkv_back_kernel(
    steps, owned, waits, d_qkv_ref, part_ref, tokens_ref, mean_ref, inverse_ref, blocks_ref, norm_ref, *refs
):
    dz_ref, norm_sums, qkv_sums, w_qkv, sems = refs[waits:]
    size = blocks_ref.shape[-1]
    outer = w_qkv.shape[0] // size
    copies = block_copies(blocks_ref, owned, 0, outer, w_qkv.shape[1] // size, w_qkv, sems)
    begin_copies(copies)

    @pl.when(pl.program_id(0) == 0)
    def _():
        norm_sums[...] = jnp.zeros_like(norm_sums)
        qkv_sums[...] = jnp.zeros_like(qkv_sums)

    qkv_sums[...] += column_sum(d_qkv_ref[...].astype(jnp.float32))
    mean, inverse = mean_ref[...], inverse_ref[...]
    inner = w_qkv.shape[1] // size

    def work(fresh):
        for col in range(outer):
            if fresh:
                wait_for(copies[col * inner : (col + 1) * inner])
            cols = pl.ds(col * size, size)
            scaled = (tokens_ref[:, cols].astype(jnp.float32) - mean) * inverse
            first = contract(d_qkv_ref[...], w_qkv[cols, :], NT)
            dz_ref[:, cols] = (part_ref[:, cols].astype(jnp.float32) + first * norm_ref[0:1, cols]).astype(jnp.bfloat16)
            norm_sums[0:8, cols] += column_sum(first * scaled)
            norm_sums[8:16, cols] += column_sum(first)

    both_ways(steps, work)


def qkv_back(d_qkv, dz_part, group_tokens, mean, inverse, blocks, owned, norm_params, waits):
    tokens, qkv_cols = d_qkv.shape
    width = dz_part.shape[1]
    size = blocks.shape[-1]
    tile = 512
    row = lambda cols: pl.BlockSpec((tile, cols), lambda i: (i, 0))
    whole = lambda rows, cols: pl.BlockSpec((rows, cols), lambda i: (0, 0))
    outer = width // size
    return pl.pallas_call(
        functools.partial(qkv_back_kernel, tokens // tile, owned, len(waits)),
        grid=(tokens // tile,),
        in_specs=[
            row(qkv_cols), row(width), row(width), row(1), row(1), pl.BlockSpec(memory_space=pl.ANY), whole(norm_params.shape[0], width),
        ]
        + [pl.BlockSpec(memory_space=pl.ANY)] * len(waits),
        out_specs=[row(width), whole(16, width), whole(8, qkv_cols)],
        out_shape=[
            jax.ShapeDtypeStruct((tokens, width), jnp.bfloat16),
            jax.ShapeDtypeStruct((16, width), jnp.float32),
            jax.ShapeDtypeStruct((8, qkv_cols), jnp.float32),
        ],
        scratch_shapes=[
            pltpu.VMEM((width, qkv_cols), jnp.bfloat16),
            pltpu.SemaphoreType.DMA((outer * (qkv_cols // size),)),
        ],
        compiler_params=kernel_params(),
        cost_estimate=pl.CostEstimate(
            flops=2 * tokens * width * qkv_cols, bytes_accessed=tokens * width * 11, transcendentals=0
        ),
        name="qkv_back",
    )(d_qkv, dz_part, group_tokens, mean, inverse, blocks, norm_params, *waits)


def weight_grad_kernel(steps, waits, core_ref, *refs):
    lefts, rights, refs = refs[:4], refs[4:7], refs[7 + waits :]
    outs, rows_held, rights_held = refs[:2], refs[2], refs[3:6]
    results, left_sems, right_sems, sems = refs[6:]
    size = results.shape[-1]
    core = core_ref[0]
    depth = rows_held.shape[0]

    def left_copy(index):
        left, first, rows, _, _, _ = steps[index]
        return pltpu.make_async_copy(
            lefts[left].at[pl.ds(first, rows), :],
            rows_held.at[index % depth, pl.ds(0, rows), :],
            left_sems.at[index % depth],
        )

    def right_copy(right, first):
        held = rights_held[right]
        return pltpu.make_async_copy(
            rights[right].at[:, pl.ds(first, held.shape[1])], held, right_sems.at[right]
        )

    def finish(index):
        for place in range(len(steps[index][5])):
            pltpu.make_async_copy(
                results.at[index % 2, place], outs[0].at[0], sems.at[index % 2, place]
            ).wait()

    order = []
    for step in steps:
        if step[3:5] not in order:
            order.append(step[3:5])
    right_copy(*order[0]).start()
    for index in range(min(depth - 1, len(steps))):
        left_copy(index).start()
    for right in order[1:]:
        right_copy(*right).start()
    for index, (left, first, rows, right, right_first, places) in enumerate(steps):
        left_copy(index).wait()
        if index + depth - 1 < len(steps):
            left_copy(index + depth - 1).start()
        if all(step[3:5] != (right, right_first) for step in steps[:index]):
            right_copy(right, right_first).wait()
        if index >= 2:
            finish(index - 2)
        held = rights_held[right]
        cols = held.shape[1] // size
        for col in range(cols):
            result = contract(rows_held[index % depth, :rows, :], held[:, col * size : (col + 1) * size], NN)
            for row in range(rows // size):
                results[index % 2, row * cols + col] = result[row * size : (row + 1) * size].astype(jnp.bfloat16)
        for number, (owner, place) in enumerate(places):
            for away in range(2):

                @pl.when((core == owner % 2) == (away == 0))
                def _():
                    pltpu.make_async_copy(
                        results.at[index % 2, number], outs[away].at[place], sems.at[index % 2, number]
                    ).start()

    for index in range(max(0, len(steps) - 2), len(steps)):
        finish(index)


def weight_grads(part, parts, lefts, rights, firsts, core, owned, dp_ways, size, waits):
    first_normed, second_normed, activated, attended = lefts
    d_hidden, seed, d_qkv = rights
    tokens = d_qkv.shape[0]
    width = seed.shape[1]
    part_size = owned // parts
    qkv_blocks = d_qkv.shape[1] // size
    per_row = width // size
    span = per_row // parts
    steps = []
    for left, right, first, rows_all in (
        (1, 0, firsts[2], second_normed.shape[0]),
        (2, 1, firsts[3], activated.shape[0]),
        (3, 1, firsts[1], attended.shape[0]),
    ):
        rows = min(512, rows_all)
        for begin in range(0, rows_all, rows):
            places = []
            for row in range(begin // size, (begin + rows) // size):
                for col in range(span):
                    block = first + row * per_row + part * span + col
                    owner, within = block // owned, block % owned
                    places.append((owner, owner // 2 * part_size + within // per_row * span + col))
            steps.append((left, begin, rows, right, part * span * size, tuple(places)))
    for owner in range(per_row // parts):
        row = owner * parts + part
        places = [(owner, owner // 2 * part_size + col) for col in range(qkv_blocks)]
        steps.append((0, row * size, size, 2, 0, tuple(places)))
    most = max(len(step[5]) for step in steps)
    anywhere = pl.BlockSpec(memory_space=pl.ANY)
    half = jax.ShapeDtypeStruct((dp_ways // 2 * part_size, size, size), jnp.bfloat16)
    flops = 2 * tokens * size * size * dp_ways * part_size
    return pl.pallas_call(
        functools.partial(weight_grad_kernel, tuple(steps), len(waits)),
        in_specs=[pl.BlockSpec(memory_space=pltpu.SMEM)] + [anywhere] * (7 + len(waits)),
        out_specs=[anywhere] * 2,
        out_shape=[half] * 2,
        scratch_shapes=[
            pltpu.VMEM((4, max(step[2] for step in steps), tokens), jnp.bfloat16),
            pltpu.VMEM((tokens, span * size), jnp.bfloat16),
            pltpu.VMEM((tokens, span * size), jnp.bfloat16),
            pltpu.VMEM((tokens, d_qkv.shape[1]), jnp.bfloat16),
            pltpu.VMEM((2, most, size, size), jnp.bfloat16),
            pltpu.SemaphoreType.DMA((4,)),
            pltpu.SemaphoreType.DMA((3,)),
            pltpu.SemaphoreType.DMA((2, most)),
        ],
        compiler_params=kernel_params(),
        cost_estimate=pl.CostEstimate(flops=flops, bytes_accessed=flops // 500, transcendentals=0),
        name="weight_grads",
    )(core, *lefts, *rights, *waits)


def pair_sum_kernel(chip_ref, *refs):
    chips = len(refs) // 3
    for index in range(chips):
        total = refs[index][...].astype(jnp.float32) + refs[chips + index][...].astype(jnp.float32)
        refs[2 * chips + index][...] = total.astype(refs[2 * chips + index].dtype)


def pair_sum(kept, received, chip, chips):
    rows, size, _ = kept.shape
    part = rows // chips
    spec = lambda away: pl.BlockSpec(
        (part, size, size), lambda i, chip: (jnp.bitwise_xor(chip[0], away), 0, 0)
    )
    plain = pl.BlockSpec((part, size, size), lambda i, chip: (0, 0, 0))
    dtypes = [jnp.float32] + [jnp.bfloat16] * (chips - 1)
    return pl.pallas_call(
        pair_sum_kernel,
        grid_spec=pltpu.PrefetchScalarGridSpec(
            num_scalar_prefetch=1,
            grid=(1,),
            in_specs=[spec(away) for away in range(chips)] * 2,
            out_specs=[plain] * chips,
        ),
        out_shape=[jax.ShapeDtypeStruct((part, size, size), dtype) for dtype in dtypes],
        compiler_params=kernel_params(),
        cost_estimate=pl.CostEstimate(flops=rows * size * size, bytes_accessed=rows * size * size * 6, transcendentals=0),
        name="pair_sum",
    )(chip, *([kept] * chips), *([received] * chips))


def input_grad_kernel(moved_ref, last_ref, tokens_ref, seed_ref, mean_ref, inverse_ref, out_ref):
    d_scaled = moved_ref[...].astype(jnp.float32) + last_ref[...].astype(jnp.float32)
    inverse = inverse_ref[...]
    scaled = (tokens_ref[...].astype(jnp.float32) - mean_ref[...]) * inverse
    average = jnp.mean(d_scaled, axis=1, keepdims=True)
    projection = jnp.mean(d_scaled * scaled, axis=1, keepdims=True)
    out_ref[...] = seed_ref[...].astype(jnp.float32) + inverse * (d_scaled - average - scaled * projection)


def input_gradient(moved, dz, tokens, seed, mean, inverse, rank, waits):
    rows, width = moved.shape
    tile = min(128, rows)
    per = rows // tile
    own = lambda n: pl.BlockSpec((tile, n), lambda i, rank: (i, 0))
    ranked = lambda n: pl.BlockSpec((tile, n), lambda i, rank: (rank[0] * per + i, 0))

    def kernel(rank_ref, *refs):
        input_grad_kernel(*refs[:6], refs[-1])

    return pl.pallas_call(
        kernel,
        grid_spec=pltpu.PrefetchScalarGridSpec(
            num_scalar_prefetch=1,
            grid=(per,),
            in_specs=[own(width), ranked(width), own(width), ranked(width), ranked(1), ranked(1)]
            + [pl.BlockSpec(memory_space=pl.ANY)] * len(waits),
            out_specs=own(width),
        ),
        out_shape=jax.ShapeDtypeStruct((rows, width), jnp.float32),
        compiler_params=kernel_params(),
        cost_estimate=pl.CostEstimate(flops=rows * width * 12, bytes_accessed=rows * width * 12, transcendentals=0),
        name="input_gradient",
    )(rank, moved, dz, tokens, seed, mean, inverse, *waits)


def dot32(left_arg, right_arg):
    return jnp.dot(left_arg, right_arg, preferred_element_type=jnp.float32)


def two_terms(values):
    high = values.astype(jnp.bfloat16)
    return high, (values - high.astype(jnp.float32)).astype(jnp.bfloat16)


def shampoo_kernel(count, terms, held, places_ref, *refs):
    grads, refs = refs[:terms], refs[terms:]
    left_refs, right_refs, master_refs = (refs[side * count : (side + 1) * count] for side in range(3))
    outs, refs = refs[3 * count + held : 3 * count + held + 4], refs[3 * count + held + 4 :]
    results, scaled, roots, pairs, powers, high, low, sems = refs
    size = results.shape[-1]
    step, steps = pl.program_id(0), pl.num_programs(0)
    slot = lax.rem(step, 2)
    chains = range(2 * count)
    stat_refs = (left_refs, right_refs)
    identity = (
        lax.broadcasted_iota(jnp.int32, (size, size), 0)
        == lax.broadcasted_iota(jnp.int32, (size, size), 1)
    ).astype(jnp.float32)

    def copies(of_step, of_slot):
        return [
            pltpu.make_async_copy(
                results.at[of_slot, kind, block],
                outs[kind].at[places_ref[of_step * count + block]],
                sems.at[of_slot, kind, block],
            )
            for kind in range(4)
            for block in range(count)
        ]

    @pl.when(step >= 2)
    def _():
        for copy in copies(step - 2, slot):
            copy.wait()

    grad16 = []
    for block in range(count):
        total = grads[0][block].astype(jnp.float32)
        for grad in grads[1:]:
            total = total + grad[block].astype(jnp.float32)
        results[slot, 0, block] = total
        grad16.append(total.astype(jnp.bfloat16))
    for item in chains:
        block, side = item // 2, item % 2
        dims = (((1 - side,), (1 - side,)), ((), ()))
        results[slot, 1 + side, block] = DECAY * stat_refs[side][block][0] + lax.dot_general(
            grad16[block], grad16[block], dims, preferred_element_type=jnp.float32
        )
    sums = []
    for item in chains:
        stat = results[slot, 1 + item % 2, item // 2]
        sums.append(jnp.sum(stat * stat, axis=0, keepdims=True))
    norms = [jnp.sqrt(jnp.sum(each, axis=1, keepdims=True)) for each in sums]
    for item in chains:
        scaled[item] = results[slot, 1 + item % 2, item // 2] * (1.0 / norms[item])
    factors = [lax.rsqrt(jnp.sqrt(norm)) for norm in norms]

    for repeat in range(ROOT_ITERS - 1):
        for item in chains:
            quarter = (identity - scaled[item]) * 0.25
            pairs[item, size:] = quarter.astype(jnp.bfloat16)
            if repeat == 0:
                roots[item] = identity + quarter
            else:
                pairs[item, :size] = roots[item].astype(jnp.bfloat16)
        if repeat == 0:
            squares = [dot32(pairs[item, size:], pairs[item, size:]) for item in chains]
        else:
            both = [dot32(pairs[item], pairs[item, size:]) for item in chains]
            for item in chains:
                roots[item] = roots[item] + both[item][:size]
            squares = [each[size:] for each in both]
        seconds = [(identity - scaled[item]) * 0.5 + squares[item] for item in chains]
        seconds16 = [second.astype(jnp.bfloat16) for second in seconds]
        fourths = [2.0 * seconds[item] + dot32(seconds16[item], seconds16[item]) for item in chains]
        for item in chains:
            high[item], low[item] = two_terms(scaled[item])
            powers[item, :size], powers[item, size:] = two_terms(fourths[item])
        for item in chains:
            both_terms = dot32(powers[item], high[item])
            scaled[item] = scaled[item] + (
                both_terms[:size] + both_terms[size:] + dot32(powers[item, :size], low[item])
            )
    for item in chains:
        pairs[item, size:] = ((identity - scaled[item]) * 0.25).astype(jnp.bfloat16)
        pairs[item, :size] = roots[item].astype(jnp.bfloat16)
    for item in chains:
        ends = two_terms(roots[item] + dot32(pairs[item, :size], pairs[item, size:]))
        if item % 2 == 0:
            powers[item, :size], powers[item, size:] = ends
        else:
            high[item], low[item] = ends
    halves = []
    for block in range(count):
        both_terms = dot32(powers[2 * block], grad16[block])
        halves.append(both_terms[:size] + both_terms[size:])
    for block in range(count):
        pairs[block, :size], pairs[block, size:] = two_terms(halves[block])
    for block in range(count):
        item = 2 * block + 1
        both_terms = dot32(pairs[block], high[item])
        product = both_terms[:size] + both_terms[size:] + dot32(pairs[block, :size], low[item])
        rate = RATE_BLOCK * factors[2 * block] * factors[item]
        results[slot, 3, block] = master_refs[block][0] - rate * product
    for copy in copies(step, slot):
        copy.start()

    @pl.when(step == steps - 1)
    def _():
        @pl.when(steps >= 2)
        def _():
            for copy in copies(step - 1, 1 - slot):
                copy.wait()

        for copy in copies(step, slot):
            copy.wait()


def shampoo(grads, left_stats, right_stats, master_blocks, places, priors, waits=()):
    part, size, _ = grads[0].shape
    count = next(each for each in (3, 2, 1) if part % each == 0)
    own = pl.BlockSpec((count, size, size), lambda step, places: (step, 0, 0))
    anywhere = pl.BlockSpec(memory_space=pl.ANY)

    def single(block):
        return pl.BlockSpec((1, size, size), lambda step, places: (places[step * count + block], 0, 0))

    result = jax.ShapeDtypeStruct(left_stats.shape, jnp.float32)
    held = len(priors)
    first_prior = 1 + len(grads) + 3 * count
    wide = pltpu.VMEM((2 * count, 2 * size, size), jnp.bfloat16)
    plain = pltpu.VMEM((2 * count, size, size), jnp.bfloat16)
    return pl.pallas_call(
        functools.partial(shampoo_kernel, count, len(grads), held + len(waits)),
        grid_spec=pltpu.PrefetchScalarGridSpec(
            num_scalar_prefetch=1,
            grid=(part // count,),
            in_specs=[own] * len(grads)
            + [single(block) for block in range(count)] * 3
            + [anywhere] * (held + len(waits)),
            out_specs=[anywhere] * 4,
            scratch_shapes=[
                pltpu.VMEM((2, 4, count, size, size), jnp.float32),
                pltpu.VMEM((2 * count, size, size), jnp.float32),
                pltpu.VMEM((2 * count, size, size), jnp.float32),
                wide,
                wide,
                plain,
                plain,
                pltpu.SemaphoreType.DMA((2, 4, count)),
            ],
        ),
        out_shape=[result] * 4,
        input_output_aliases={first_prior + index: index for index in range(held)},
        compiler_params=kernel_params(),
        cost_estimate=pl.CostEstimate(
            flops=part * 130 * 2 * size**3, bytes_accessed=part * size * size * 30, transcendentals=0
        ),
        name="shampoo",
    )(
        places,
        *grads,
        *([left_stats] * count),
        *([right_stats] * count),
        *([master_blocks] * count),
        *priors,
        *waits,
    )


def after(value, *earlier):
    return lax.optimization_barrier((value,) + earlier)[0]


def onward(part, axis):
    ways = lax.axis_size(axis)
    return lax.ppermute(part, axis, [(each, (each + 1) % ways) for each in range(ways)])


def swap(part, bits):
    ways = lax.axis_size("dp")
    return lax.ppermute(part, "dp", [(each, each ^ bits) for each in range(ways)])


def small_rows(values, ways):
    return jnp.pad(values, ((0, 0), (0, -values.shape[1] % 2048))).reshape(-1, 128)


def shards(
    tokens,
    cotangent,
    segments,
    subsets,
    packs,
    master_blocks,
    left_stats,
    right_stats,
    local_vecs,
    local_vec_stats,
    shared_vecs,
    shared_vec_stats,
):
    tp_ways = lax.axis_size("tp")
    dp_ways = lax.axis_size("dp")
    tp_rank = lax.axis_index("tp")
    tok_dev, model_width = tokens.shape
    group_tok = tok_dev * tp_ways
    pack_count, pack_len = segments.shape
    seg_width = subsets.shape[1]
    heads_dev = HEADS // tp_ways
    ff_dev = FF // tp_ways
    head_cols = heads_dev * HD
    owned, block_size, _ = master_blocks.shape
    block_rows = model_width // block_size
    first_out = block_rows * (3 * head_cols // block_size)
    first_in = first_out + head_cols // block_size * block_rows
    first_down = first_in + block_rows * (ff_dev // block_size)
    all_count = owned * dp_ways
    vec_rows = 3 * heads_dev + ff_dev // HD

    vec_used = local_vecs.size
    shared_used = shared_vecs.size
    vec_flat = jnp.concatenate([local_vecs.reshape(-1), shared_vecs.reshape(-1)])
    extra = jnp.pad(vec_flat, (0, EXTRA_ROWS * block_size - vec_flat.size)).reshape(EXTRA_ROWS, block_size)
    rows16 = jnp.concatenate([master_blocks.reshape(-1, block_size), extra], 0).astype(jnp.bfloat16)
    blocks = lax.all_gather(rows16, "dp", axis=0, tiled=True)

    token_parts = [tokens]
    for step in range(1, tp_ways):
        token_parts.append(onward(token_parts[-1], "tp"))

    gathered = blocks.reshape(dp_ways, -1, block_size)[:, owned * block_size :].reshape(dp_ways, -1)
    vec_values = (
        gathered[:, :vec_used].reshape(dp_ways, vec_rows, -1).transpose(1, 0, 2).reshape(vec_rows, HD)
    ).astype(jnp.float32)
    shared_mine = gathered[:, vec_used : vec_used + shared_used]
    shared_all = jnp.zeros((tp_ways,) + shared_mine.shape, jnp.bfloat16)
    for step in range(tp_ways):
        part = shared_mine
        if step:
            part = lax.ppermute(
                part, "tp", [(each, (each + step) % tp_ways) for each in range(tp_ways)]
            )
        shared_all = lax.dynamic_update_slice(
            shared_all, part[None], ((tp_rank - step) % tp_ways, 0, 0)
        )
    norm_params = (
        shared_all.reshape(tp_ways, dp_ways, 6, -1).transpose(2, 1, 0, 3).reshape(6, model_width)
    ).astype(jnp.float32)
    bias_qkv = vec_values[: 3 * heads_dev].reshape(1, -1)
    bias_in = vec_values[3 * heads_dev :].reshape(1, -1)

    own_pos = tp_rank * tok_dev + jnp.arange(tok_dev)
    own_pack = own_pos // pack_len
    valid_own = (own_pack < packs[0]).astype(jnp.float32)
    owned_input_rows = tokens.astype(jnp.float32)

    group_pack = jnp.arange(group_tok) // pack_len
    lookup_key = group_pack * seg_width + segments.reshape(-1)
    onehot = lookup_key[:, None] == jnp.arange(pack_count * seg_width)[None, :]
    subset_tok = jnp.sum(jnp.where(onehot, subsets.reshape(-1)[None, :], 0), axis=1)
    weight = 0.5 + subset_tok.astype(jnp.float32) / (SUBSETS - 1)
    factor = (weight * (group_pack < packs[0]).astype(jnp.float32))[:, None]

    rank = tp_rank.astype(jnp.int32)[None]
    cosines, sines = turn_tables(pack_len, 128)
    cotangent_parts = [cotangent, onward(after(cotangent, token_parts[-1], shared_all), "tp")]
    qkv16, first_turned, second_normed, second_turned, group_tokens, mean, inverse = project_qkv(
        token_parts, rank, blocks, owned, norm_params, bias_qkv, cosines, sines, heads_dev
    )
    attended, attended_turned = attend(qkv16, segments, heads_dev)
    cotangent_parts.append(onward(after(cotangent_parts[-1], attended), "tp"))
    active_turned, slope, partial_value = feed_forward(
        second_normed, attended, blocks, owned, bias_in, (first_out, first_in, first_down)
    )
    while len(cotangent_parts) < tp_ways:
        cotangent_parts.append(onward(after(cotangent_parts[-1], slope), "tp"))

    back_args = (
        tp_ways, rank, factor, slope, group_tokens, mean, inverse, blocks, owned, norm_params,
        (first_out, first_in, first_down), head_cols,
    )
    early = feed_back(cotangent_parts[:-1], 0, *back_args, ())
    late = feed_back(cotangent_parts[-1:], tp_ways - 1, *back_args, early[:4])
    seed_all, d_attended, d_hidden16, dz_part = late[:4]
    branch = lax.psum_scatter(
        after(partial_value, cotangent_parts[-1], early[5]), "tp", scatter_dimension=0, tiled=True
    )
    d_qkv16 = attend_back(qkv16, d_attended, segments, cosines, sines, heads_dev)
    dp_rank = lax.axis_index("dp").astype(jnp.int32)
    lefts = (first_turned, second_turned, active_turned, attended_turned)
    rights = (d_hidden16, seed_all, d_qkv16)
    firsts = (0, first_out, first_in, first_down)
    qkv_blocks = 3 * head_cols // block_size
    parts = 4
    by_part = (
        dp_ways == 8
        and owned == parts * qkv_blocks
        and block_rows == 2 * parts
        and ff_dev == model_width
        and owned % block_rows == 0
        and first_out % block_rows == 0
        and first_in % block_rows == 0
    )
    sums = []

    def quarter(part, waits):
        kept, away = weight_grads(
            part, parts, lefts, rights, firsts, (dp_rank % 2)[None], owned, dp_ways, block_size, waits
        )
        sums.append(pair_sum(kept, swap(away, 1), (dp_rank // 2)[None], dp_ways // 2))
        return kept

    first_waits = ()
    if by_part:
        quarter(0, ())
        quarter(1, ())
        first_waits = (sums[0][0],)
    dz16, first_sums, qkv_sums = qkv_back(
        d_qkv16, dz_part, group_tokens, mean, inverse, blocks, owned, norm_params, first_waits
    )
    dz_rows = lambda back: lax.dynamic_slice_in_dim(dz16, (tp_rank - back) % tp_ways * tok_dev, tok_dev, 0)
    back = 2

    def pass_on(moving, back):
        total = moving.astype(jnp.float32) + dz_rows(back).astype(jnp.float32)
        return total.astype(jnp.bfloat16)

    moving = onward(dz_rows(1), "tp")
    shared_local = jnp.concatenate(
        [
            jnp.sum(first_sums.reshape(2, 8, model_width), axis=1),
            jnp.sum((early[4][:16] + late[4][:16]).reshape(2, 8, model_width), axis=1),
            jnp.sum(early[4][16:], axis=0)[None],
        ],
        0,
    )
    vecs_local = jnp.concatenate(
        [
            jnp.sum(qkv_sums, axis=0).reshape(3 * heads_dev, HD),
            jnp.sum(early[5] + late[5], axis=0).reshape(ff_dev // HD, HD),
        ],
        0,
    )
    small = jnp.concatenate(
        [
            shared_local.reshape(5, dp_ways, -1).transpose(1, 0, 2).reshape(dp_ways, -1),
            vecs_local.reshape(vec_rows, dp_ways, -1).transpose(1, 0, 2).reshape(dp_ways, -1),
        ],
        1,
    )
    small_in = after(small_rows(small, dp_ways), branch)
    small_own = lax.psum_scatter(small_in, "dp", scatter_dimension=0, tiled=True).reshape(-1)
    output = (
        valid_own[:, None]
        * (owned_input_rows + branch.astype(jnp.float32) + norm_params[4] + norm_params[5])
    ).astype(jnp.bfloat16)

    shared_size = 5 * model_width // dp_ways
    own_vec_grads = small_own[shared_size : small.shape[1]].reshape(vec_rows, HD // dp_ways)
    shared_part = small_own[:shared_size].reshape(5, tp_ways, -1).transpose(1, 0, 2)
    shared_in = small_rows(shared_part.reshape(tp_ways, -1), tp_ways)
    shared_own = lax.psum_scatter(shared_in, "tp", scatter_dimension=0, tiled=True).reshape(-1)
    shared_own = shared_own[: shared_size // tp_ways].reshape(5, -1)
    shared_grads = jnp.concatenate([shared_own, shared_own[4:]], 0)
    results = ()
    if by_part:
        part_size = owned // parts
        span = block_rows // parts
        terms = []
        ready = []

        def send_on(part):
            if part:
                sums[part] = [sums[part][0]] + [after(each, terms[-1][3]) for each in sums[part][1:]]
                ready.append(sums[part][3])
            terms.append([sums[part][0]] + [swap(sums[part][bits], 2 * bits) for bits in range(1, 4)])

        send_on(0)
        quarter(2, (dz16, sums[1][0]) + tuple(terms[0][1:]))
        quarter(3, tuple(terms[0][1:]))
        for part in range(1, parts):
            send_on(part)
        count = jnp.arange(part_size, dtype=jnp.int32)
        in_qkv = dp_rank * owned < first_out
        for part in range(parts):
            places = jnp.where(
                in_qkv,
                part * part_size + count,
                count // span * block_rows + part * span + count % span,
            )
            waits = []
            if part < parts - 1:
                waits.append(ready[part])
            if part == 0:
                waits += terms[1][1:]
            if part % 2 == 1 and back < tp_ways:
                if part:
                    moving, first_result = lax.optimization_barrier((moving, results[0]))
                    results = [first_result] + list(results[1:])
                total = pass_on(moving, back)
                waits.append(total)
                moving = onward(total, "tp")
                back += 1
            if part == 1:
                waits.append(small_in)
            if part == 2:
                waits += [small_own, shared_in]
            if part == 3:
                waits += [output, shared_own]
            results = shampoo(
                terms[part], left_stats, right_stats, master_blocks, places, results, waits
            )
    else:
        local = [
            to_blocks(jnp.dot(left, right, preferred_element_type=jnp.float32).astype(jnp.bfloat16), block_size)
            for left, right in (
                (first_turned, d_qkv16),
                (attended_turned, seed_all),
                (second_turned, d_hidden16),
                (active_turned, seed_all),
            )
        ]
        grads16 = lax.psum_scatter(jnp.concatenate(local, 0), "dp", scatter_dimension=0, tiled=True)
        results = shampoo(
            [grads16], left_stats, right_stats, master_blocks, jnp.arange(owned, dtype=jnp.int32), results
        )
    while back < tp_ways:
        moving = onward(pass_on(moving, back), "tp")
        back += 1
    input_grad = input_gradient(moving, dz16, tokens, seed_all, mean, inverse, rank, results[:1])
    own_grads, left_new, right_new, new_blocks = results
    local_stat_new = DECAY * local_vec_stats + own_vec_grads * own_vec_grads
    local_new = local_vecs - RATE_VEC * own_vec_grads * lax.rsqrt(local_stat_new)
    shared_stat_new = DECAY * shared_vec_stats + shared_grads * shared_grads
    shared_new = shared_vecs - RATE_VEC * shared_grads * lax.rsqrt(shared_stat_new)
    return (
        output,
        input_grad,
        own_grads,
        left_new,
        right_new,
        new_blocks,
        own_vec_grads,
        local_stat_new,
        local_new,
        shared_grads,
        shared_stat_new,
        shared_new,
    )


def solution(mesh):
    placed = (
        P(("dp", "tp"), None),
        P(("dp", "tp"), None),
        P("dp", None),
        P("dp", None),
        P("dp"),
        P(("dp", "tp"), None, None),
        P(("dp", "tp"), None, None),
        P(("dp", "tp"), None, None),
        P("tp", "dp"),
        P("tp", "dp"),
        P(None, ("dp", "tp")),
        P(None, ("dp", "tp")),
    )
    return jax.shard_map(
        shards,
        mesh=mesh,
        in_specs=placed,
        out_specs=(
            P(("dp", "tp"), None),
            P(("dp", "tp"), None),
            P(("dp", "tp"), None, None),
            P(("dp", "tp"), None, None),
            P(("dp", "tp"), None, None),
            P(("dp", "tp"), None, None),
            P("tp", "dp"),
            P("tp", "dp"),
            P("tp", "dp"),
            P(None, ("dp", "tp")),
            P(None, ("dp", "tp")),
            P(None, ("dp", "tp")),
        ),
        check_vma=False,
    )
```

```python
import functools
import math

import jax
import jax.numpy as jnp
from jax import lax
from jax.experimental import pallas as pl
from jax.experimental.pallas import tpu as pltpu
from jax.sharding import PartitionSpec as P

HEADS = 8
HD = 256
ROT = 64
FF = 8192
SUBSETS = 22
ROOT_ITERS = 8


EPS_NORM = 1e-05
DECAY = 0.5
RATE_BLOCK = 0.6
RATE_VEC = 0.2
NEG_FILL = -1e30
DOC_MAX = 512
HALF_ROOT = 0.7071067811865476
DENSITY_SCALE = 0.3989422804014327


def to_blocks(matrix, block_size):
    block_rows = matrix.shape[0] // block_size
    block_cols = matrix.shape[1] // block_size
    return (
        matrix.reshape(block_rows, block_size, block_cols, block_size)
        .transpose(0, 2, 1, 3)
        .reshape(block_rows * block_cols, block_size, block_size)
    )


EXTRA_ROWS = 16
FEED_BACK_TILE = 512
VMEM_LIMIT = 60 << 20
NN = (((1,), (0,)), ((), ()))
NT = (((1,), (1,)), ((), ()))
TN = (((0,), (0,)), ((), ()))


def contract(left_arg, right_arg, dims):
    return lax.dot_general(left_arg, right_arg, dims, preferred_element_type=jnp.float32)


def kernel_params():
    return pltpu.CompilerParams(vmem_limit_bytes=VMEM_LIMIT)


def block_row(index, owned, size):
    return index // owned * (owned * size + EXTRA_ROWS) + index % owned * size


def block_copies(blocks_ref, owned, first, rows, cols, target, sems):
    size = blocks_ref.shape[-1]
    return [
        pltpu.make_async_copy(
            blocks_ref.at[pl.ds(block_row(first + row * cols + col, owned, size), size), :],
            target.at[pl.ds(row * size, size), pl.ds(col * size, size)],
            sems.at[row * cols + col],
        )
        for row in range(rows)
        for col in range(cols)
    ]


def begin_copies(copies):
    @pl.when(pl.program_id(0) == 0)
    def _():
        for copy in copies:
            copy.start()


def end_copies(copies):
    @pl.when(pl.program_id(0) == 0)
    def _():
        for copy in copies:
            copy.wait()


def turn(values, cosines, sines):
    lane = lax.broadcasted_iota(jnp.int32, values.shape, 1)
    half = ROT // 2
    wide = values.shape[1]
    swapped = jnp.where(
        lane < half, pltpu.roll(values, wide - half, 1), pltpu.roll(values, half, 1)
    )
    return values * cosines + swapped * sines


def turn_tables(pack_len, lanes):
    half = ROT // 2
    positions = jnp.arange(pack_len).astype(jnp.float32)
    freqs = 10000.0 ** (-(jnp.arange(half).astype(jnp.float32) * 2.0) / ROT)
    angles = positions[:, None] * freqs[None, :]
    cosines = jnp.cos(angles)
    sines = jnp.sin(angles)
    rest = jnp.zeros((pack_len, lanes - ROT), jnp.float32)
    return (
        jnp.concatenate([cosines, cosines, rest + 1.0], -1),
        jnp.concatenate([-sines, sines, rest], -1),
    )


def normed_rows(rows):
    mean = jnp.mean(rows, axis=1, keepdims=True)
    centred = rows - mean
    variance = jnp.mean(centred * centred, axis=1, keepdims=True)
    return mean, lax.rsqrt(variance + EPS_NORM)


def part_copies(part_refs, held, sems):
    return [
        pltpu.make_async_copy(part, held.at[index], sems.at[index])
        for index, part in enumerate(part_refs)
    ]


def await_part(copies, per_part):
    step = pl.program_id(0)
    for index, copy in enumerate(copies):

        @pl.when(step == index * per_part)
        def _():
            copy.wait()


def qkv_kernel(heads, owned, parts, rank_ref, *refs):
    part_refs = refs[:parts]
    blocks_ref, norm_ref, bias_ref, cos_ref, sin_ref = refs[parts : parts + 5]
    outs, (normed, weight, held, sems, part_sems) = refs[parts + 5 : parts + 12], refs[parts + 12 :]
    qkv_ref, first_turned, second_ref, second_turned, tokens_ref, mean_ref, inverse_ref = outs
    size = blocks_ref.shape[-1]
    copies = block_copies(blocks_ref, owned, 0, weight.shape[0] // size, weight.shape[1] // size, weight, sems)
    moves = part_copies(part_refs, held, part_sems)
    begin_copies(moves + copies)
    await_part(moves, 1)
    own = held[pl.program_id(0)]
    tokens_ref[...] = own
    rows = own.astype(jnp.float32)
    mean, inverse = normed_rows(rows)
    mean_ref[...] = mean
    inverse_ref[...] = inverse
    for col in range(rows.shape[1] // size):
        cols = pl.ds(col * size, size)
        scaled = (own[:, col * size : (col + 1) * size].astype(jnp.float32) - mean) * inverse
        second = (scaled * norm_ref[2:3, cols] + norm_ref[3:4, cols]).astype(jnp.bfloat16)
        second_ref[:, cols] = second
        second_turned[cols, :] = second.T
        first = (scaled * norm_ref[0:1, cols] + norm_ref[1:2, cols]).astype(jnp.bfloat16)
        normed[:, cols] = first
        first_turned[cols, :] = first.T
    end_copies(copies)
    lanes = cos_ref.shape[1]
    for head in range(heads):
        for part in range(3):
            cols = pl.ds((head * 3 + part) * HD, HD)
            result = contract(normed[...], weight[:, cols], NN) + bias_ref[:, cols]
            if part < 2:
                first = turn(result[:, :lanes], cos_ref[...], sin_ref[...])
                result = jnp.concatenate([first, result[:, lanes:]], 1)
            if part == 0:
                result = result * (1.0 / math.sqrt(HD))
            qkv_ref[:, cols] = result.astype(jnp.bfloat16)


def project_qkv(parts, rank, blocks, owned, norm_params, bias, cosines, sines, heads):
    ways = len(parts)
    tile, width = parts[0].shape
    tokens = ways * tile
    size = blocks.shape[-1]
    pack_len, lanes = cosines.shape
    cols = 3 * heads * HD
    per_pack = pack_len // tile
    place = lambda i, rank: (rank[0] - i + ways) % ways
    row = lambda n: pl.BlockSpec((tile, n), lambda i, rank: (place(i, rank), 0))
    table = pl.BlockSpec((tile, lanes), lambda i, rank: (place(i, rank) % per_pack, 0))
    anywhere = pl.BlockSpec(memory_space=pl.ANY)
    wide = jax.ShapeDtypeStruct((tokens, width), jnp.bfloat16)
    tall = jax.ShapeDtypeStruct((width, tokens), jnp.bfloat16)
    single = jax.ShapeDtypeStruct((tokens, 1), jnp.float32)
    turned = pl.BlockSpec((width, tile), lambda i, rank: (0, place(i, rank)))
    return pl.pallas_call(
        functools.partial(qkv_kernel, heads, owned, ways),
        grid_spec=pltpu.PrefetchScalarGridSpec(
            num_scalar_prefetch=1,
            grid=(ways,),
            in_specs=[anywhere] * (ways + 1)
            + [
                pl.BlockSpec(norm_params.shape, lambda i, rank: (0, 0)),
                pl.BlockSpec((1, cols), lambda i, rank: (0, 0)),
                table,
                table,
            ],
            out_specs=[row(cols), turned, row(width), turned, row(width), row(1), row(1)],
            scratch_shapes=[
                pltpu.VMEM((tile, width), jnp.bfloat16),
                pltpu.VMEM((width, cols), jnp.bfloat16),
                pltpu.VMEM((ways, tile, width), jnp.bfloat16),
                pltpu.SemaphoreType.DMA((width // size * (cols // size),)),
                pltpu.SemaphoreType.DMA((ways,)),
            ],
        ),
        out_shape=[jax.ShapeDtypeStruct((tokens, cols), jnp.bfloat16), tall, wide, tall, wide, single, single],
        compiler_params=kernel_params(),
        cost_estimate=pl.CostEstimate(
            flops=2 * tokens * width * cols, bytes_accessed=tokens * (4 * width + cols) * 2 + width * cols * 2, transcendentals=0
        ),
        name="qkv",
    )(rank, *parts, blocks, norm_params, bias, cosines, sines)


def attend_kernel(query_ref, key_ref, value_ref, seg_row, seg_col, out_ref, turned_ref):
    length = key_ref.shape[0]
    step = 256
    for start in range(0, length, step):
        first = max(0, start - DOC_MAX)
        stop = start + step
        scores = contract(query_ref[start:stop, :], key_ref[first:stop, :], NT)
        row = lax.broadcasted_iota(jnp.int32, scores.shape, 0) + start
        col = lax.broadcasted_iota(jnp.int32, scores.shape, 1) + first
        allowed = (col <= row) & (seg_col[0, start:stop, :] == seg_row[0, :, first:stop])
        masked = jnp.where(allowed, scores, NEG_FILL)
        exp_terms = jnp.exp(masked - jnp.max(masked, axis=1, keepdims=True))
        probs = exp_terms * (1.0 / jnp.sum(exp_terms, axis=1, keepdims=True))
        result = contract(probs.astype(jnp.bfloat16), value_ref[first:stop, :], NN).astype(jnp.bfloat16)
        out_ref[start:stop, :] = result
        turned_ref[:, start:stop] = result.T


def attend(qkv, segments, heads):
    packs, length = segments.shape
    part = lambda which: pl.BlockSpec((length, HD), lambda p, h: (p, h * 3 + which))
    return pl.pallas_call(
        attend_kernel,
        grid=(packs, heads),
        in_specs=[
            part(0),
            part(1),
            part(2),
            pl.BlockSpec((1, 1, length), lambda p, h: (p, 0, 0)),
            pl.BlockSpec((1, length, 1), lambda p, h: (p, 0, 0)),
        ],
        out_specs=[
            pl.BlockSpec((length, HD), lambda p, h: (p, h)),
            pl.BlockSpec((HD, length), lambda p, h: (h, p)),
        ],
        out_shape=[
            jax.ShapeDtypeStruct((packs * length, heads * HD), jnp.bfloat16),
            jax.ShapeDtypeStruct((heads * HD, packs * length), jnp.bfloat16),
        ],
        compiler_params=kernel_params(),
        cost_estimate=pl.CostEstimate(
            flops=packs * heads * length * length * HD * 3, bytes_accessed=packs * length * heads * HD * 8, transcendentals=0
        ),
        name="attend",
    )(qkv, qkv, qkv, segments[:, None, :], segments[:, :, None])


def attend_back_kernel(
    query_ref, key_ref, value_ref, d_out_ref, seg_row, seg_col, cos_ref, sin_ref, grad_ref, d_key, d_value
):
    length = key_ref.shape[0]
    step = 256
    lanes = cos_ref.shape[1]
    d_key[...] = jnp.zeros_like(d_key)
    d_value[...] = jnp.zeros_like(d_value)
    for start in range(0, length, step):
        first = max(0, start - DOC_MAX)
        stop = start + step
        query = query_ref[start:stop, :]
        d_out = d_out_ref[start:stop, :]
        keys = key_ref[first:stop, :]
        scores = contract(keys, query, NT)
        key_pos = lax.broadcasted_iota(jnp.int32, scores.shape, 0) + first
        query_pos = lax.broadcasted_iota(jnp.int32, scores.shape, 1) + start
        allowed = (key_pos <= query_pos) & (seg_col[0, first:stop, :] == seg_row[0, :, start:stop])
        masked = jnp.where(allowed, scores, NEG_FILL)
        exp_terms = jnp.exp(masked - jnp.max(masked, axis=0, keepdims=True))
        probs = exp_terms * (1.0 / jnp.sum(exp_terms, axis=0, keepdims=True))
        d_probs = contract(value_ref[first:stop, :], d_out, NT)
        row_dot = jnp.sum(probs * d_probs, axis=0, keepdims=True)
        d_scores = (probs * (d_probs - row_dot)).astype(jnp.bfloat16)
        d_value[first:stop, :] += contract(probs.astype(jnp.bfloat16), d_out, NN)
        d_key[first:stop, :] += contract(d_scores, query, NN)
        d_query = contract(d_scores, keys, TN) * (1.0 / math.sqrt(HD))
        back = turn(d_query[:, :lanes], cos_ref[start:stop, :], -sin_ref[start:stop, :])
        grad_ref[start:stop, :lanes] = back.astype(jnp.bfloat16)
        grad_ref[start:stop, lanes:HD] = d_query[:, lanes:].astype(jnp.bfloat16)
    back = turn(d_key[:, :lanes], cos_ref[...], -sin_ref[...])
    grad_ref[:, HD : HD + lanes] = back.astype(jnp.bfloat16)
    grad_ref[:, HD + lanes : 2 * HD] = d_key[:, lanes:].astype(jnp.bfloat16)
    grad_ref[:, 2 * HD :] = d_value[...].astype(jnp.bfloat16)


def attend_back(qkv, d_attended, segments, cosines, sines, heads):
    packs, length = segments.shape
    lanes = cosines.shape[1]
    part = lambda which: pl.BlockSpec((length, HD), lambda p, h: (p, h * 3 + which))
    table = pl.BlockSpec((length, lanes), lambda p, h: (0, 0))
    return pl.pallas_call(
        attend_back_kernel,
        grid=(packs, heads),
        in_specs=[
            part(0),
            part(1),
            part(2),
            pl.BlockSpec((length, HD), lambda p, h: (p, h)),
            pl.BlockSpec((1, 1, length), lambda p, h: (p, 0, 0)),
            pl.BlockSpec((1, length, 1), lambda p, h: (p, 0, 0)),
            table,
            table,
        ],
        out_specs=pl.BlockSpec((length, 3 * HD), lambda p, h: (p, h)),
        out_shape=jax.ShapeDtypeStruct((packs * length, 3 * heads * HD), jnp.bfloat16),
        scratch_shapes=[pltpu.VMEM((length, HD), jnp.float32)] * 2,
        compiler_params=kernel_params(),
        cost_estimate=pl.CostEstimate(
            flops=packs * heads * length * length * HD * 7, bytes_accessed=packs * length * heads * HD * 16, transcendentals=0
        ),
        name="attend_back",
    )(qkv, qkv, qkv, d_attended, segments[:, None, :], segments[:, :, None], cosines, sines)


def feed_kernel(
    offsets, owned, x_ref, attended_ref, blocks_ref, bias_ref, turned_ref, slope_ref, out_ref, act_ref, w_in, w_down, sems_in, sems_down
):
    size = blocks_ref.shape[-1]
    width, hidden_units = w_in.shape
    inner = hidden_units // size
    first_out, first_in, first_down = offsets
    head_rows = attended_ref.shape[1] // size
    outer = width // size
    copies_in = block_copies(blocks_ref, owned, first_in, outer, inner, w_in, sems_in)
    copies_down = block_copies(blocks_ref, owned, first_down, inner, outer, w_down.at[pl.ds(0, hidden_units)], sems_down)
    copies_down += block_copies(
        blocks_ref,
        owned,
        first_out,
        head_rows,
        outer,
        w_down.at[pl.ds(hidden_units, head_rows * size)],
        sems_down.at[pl.ds(inner * outer, head_rows * outer)],
    )
    begin_copies(copies_in + copies_down)
    end_copies(copies_in)
    values = x_ref[...]
    for col in range(inner):
        cols = pl.ds(col * size, size)
        hidden = contract(values, w_in[:, cols], NN) + bias_ref[:, cols]
        cdf = 0.5 + 0.5 * lax.erf(hidden * HALF_ROOT)
        density = jnp.exp(-0.5 * hidden * hidden) * DENSITY_SCALE
        activated = (hidden * cdf).astype(jnp.bfloat16)
        act_ref[:, cols] = activated
        turned_ref[cols, :] = activated.T
        slope_ref[:, cols] = (cdf + hidden * density).astype(jnp.bfloat16)
    end_copies(copies_down)
    for col in range(outer):
        cols = pl.ds(col * size, size)
        out_ref[:, cols] = (
            contract(act_ref[...], w_down[:hidden_units, cols], NN)
            + contract(attended_ref[...], w_down[hidden_units:, cols], NN)
        ).astype(jnp.bfloat16)


def feed_forward(normed, attended, blocks, owned, bias, offsets):
    tokens, width = normed.shape
    size = blocks.shape[-1]
    hidden_units = bias.shape[1]
    head_cols = attended.shape[1]
    tile = 512
    row = lambda cols: pl.BlockSpec((tile, cols), lambda i: (i, 0))
    inner, outer = hidden_units // size, width // size
    return pl.pallas_call(
        functools.partial(feed_kernel, offsets, owned),
        grid=(tokens // tile,),
        in_specs=[
            row(width),
            row(head_cols),
            pl.BlockSpec(memory_space=pl.ANY),
            pl.BlockSpec((1, hidden_units), lambda i: (0, 0)),
        ],
        out_specs=[
            pl.BlockSpec((hidden_units, tile), lambda i: (0, i)), row(hidden_units), row(width),
        ],
        out_shape=[
            jax.ShapeDtypeStruct((hidden_units, tokens), jnp.bfloat16),
            jax.ShapeDtypeStruct((tokens, hidden_units), jnp.bfloat16),
            jax.ShapeDtypeStruct((tokens, width), jnp.bfloat16),
        ],
        scratch_shapes=[
            pltpu.VMEM((tile, hidden_units), jnp.bfloat16),
            pltpu.VMEM((width, hidden_units), jnp.bfloat16),
            pltpu.VMEM((hidden_units + head_cols, width), jnp.bfloat16),
            pltpu.SemaphoreType.DMA((inner * outer,)),
            pltpu.SemaphoreType.DMA((inner * outer + head_cols // size * outer,)),
        ],
        compiler_params=kernel_params(),
        cost_estimate=pl.CostEstimate(
            flops=2 * tokens * width * (2 * hidden_units + head_cols), bytes_accessed=tokens * width * 10 + width * hidden_units * 4, transcendentals=0
        ),
        name="feed",
    )(normed, attended, blocks, bias)


def column_sum(values):
    rows, cols = values.shape
    return jnp.sum(values.reshape(rows // 8, 8, cols), axis=0)


def feed_back_kernel(offsets, owned, first_part, parts, held_count, rank_ref, *refs):
    part_refs = refs[:parts]
    factor_ref, slope_ref, tokens_ref, mean_ref, inverse_ref, blocks_ref, norm_ref = refs[parts : parts + 7]
    (
        seed_ref, d_attended_ref, d_hidden_ref, dz_ref, norm_sums, hidden_sums,
        w_in, w_down, w_out, held, sems_in, sems_down, sems_out, part_sems,
    ) = refs[parts + 7 + held_count :]
    size = blocks_ref.shape[-1]
    width, hidden_units = w_in.shape
    inner, outer = hidden_units // size, width // size
    first_out, first_in, first_down = offsets
    tile = seed_ref.shape[0]
    per_part = held.shape[1] // tile
    moves = part_copies(part_refs, held, part_sems)
    copies_out = block_copies(blocks_ref, owned, first_out, w_out.shape[0] // size, outer, w_out, sems_out)
    copies_down = block_copies(blocks_ref, owned, first_down, inner, outer, w_down, sems_down)
    copies_in = block_copies(blocks_ref, owned, first_in, outer, inner, w_in, sems_in)
    begin_copies(moves + copies_out + copies_down + copies_in)

    @pl.when(pl.program_id(0) == 0)
    def _():
        norm_sums[...] = jnp.zeros_like(norm_sums)
        hidden_sums[...] = jnp.zeros_like(hidden_sums)

    await_part(moves, per_part)
    step = pl.program_id(0)
    cotangent = held[step // per_part, pl.ds(pl.multiple_of(step % per_part * tile, tile), tile), :]
    seed_ref[...] = (cotangent.astype(jnp.float32) * factor_ref[...]).astype(jnp.bfloat16)
    seed = seed_ref[...]
    if first_part == 0:

        @pl.when(step < per_part)
        def _():
            norm_sums[16:24, :] += column_sum(seed_ref[...].astype(jnp.float32))

    end_copies(copies_out)
    d_attended_ref[...] = contract(seed, w_out[...], NT).astype(jnp.bfloat16)
    end_copies(copies_down)
    for col in range(inner):
        cols = pl.ds(col * size, size)
        d_act = contract(seed_ref[...], w_down[cols, :], NT)
        d_hidden = (d_act * slope_ref[:, cols].astype(jnp.float32)).astype(jnp.bfloat16)
        d_hidden_ref[:, cols] = d_hidden
        hidden_sums[:, cols] += column_sum(d_hidden.astype(jnp.float32))
    end_copies(copies_in)
    mean, inverse = mean_ref[...], inverse_ref[...]
    for col in range(outer):
        cols = pl.ds(col * size, size)
        scaled = (tokens_ref[:, cols].astype(jnp.float32) - mean) * inverse
        second = contract(d_hidden_ref[...], w_in[cols, :], NT)
        dz_ref[:, cols] = (second * norm_ref[2:3, cols]).astype(jnp.bfloat16)
        norm_sums[0:8, cols] += column_sum(second * scaled)
        norm_sums[8:16, cols] += column_sum(second)


def feed_back(parts, first_part, ways, rank, factor, slope, group_tokens, mean, inverse, blocks, owned, norm_params, offsets, head_cols, priors):
    chunk, width = parts[0].shape
    tokens = ways * chunk
    size = blocks.shape[-1]
    hidden_units = slope.shape[1]
    tile = min(FEED_BACK_TILE, chunk)
    per_part = chunk // tile
    inner, outer = hidden_units // size, width // size
    place = lambda i, rank: (rank[0] - first_part - i // per_part + ways) % ways * per_part + i % per_part
    row = lambda n: pl.BlockSpec((tile, n), lambda i, rank: (place(i, rank), 0))
    whole = lambda rows, cols: pl.BlockSpec((rows, cols), lambda i, rank: (0, 0))
    anywhere = pl.BlockSpec(memory_space=pl.ANY)
    count = len(parts)
    rows = count * chunk
    return pl.pallas_call(
        functools.partial(feed_back_kernel, offsets, owned, first_part, count, len(priors)),
        grid_spec=pltpu.PrefetchScalarGridSpec(
            num_scalar_prefetch=1,
            grid=(count * per_part,),
            in_specs=[anywhere] * count
            + [row(1), row(hidden_units), row(width), row(1), row(1), anywhere]
            + [whole(norm_params.shape[0], width)]
            + [anywhere] * len(priors),
            out_specs=[
                row(width), row(head_cols), row(hidden_units), row(width), whole(24, width), whole(8, hidden_units),
            ],
            scratch_shapes=[
                pltpu.VMEM((width, hidden_units), jnp.bfloat16),
                pltpu.VMEM((hidden_units, width), jnp.bfloat16),
                pltpu.VMEM((head_cols, width), jnp.bfloat16),
                pltpu.VMEM((count, chunk, width), jnp.bfloat16),
                pltpu.SemaphoreType.DMA((inner * outer,)),
                pltpu.SemaphoreType.DMA((inner * outer,)),
                pltpu.SemaphoreType.DMA((head_cols // size * outer,)),
                pltpu.SemaphoreType.DMA((count,)),
            ],
        ),
        out_shape=[
            jax.ShapeDtypeStruct((tokens, width), jnp.bfloat16),
            jax.ShapeDtypeStruct((tokens, head_cols), jnp.bfloat16),
            jax.ShapeDtypeStruct((tokens, hidden_units), jnp.bfloat16),
            jax.ShapeDtypeStruct((tokens, width), jnp.bfloat16),
            jax.ShapeDtypeStruct((24, width), jnp.float32),
            jax.ShapeDtypeStruct((8, hidden_units), jnp.float32),
        ],
        input_output_aliases={1 + count + 7 + index: index for index in range(len(priors))},
        compiler_params=kernel_params(),
        cost_estimate=pl.CostEstimate(
            flops=2 * rows * width * (2 * hidden_units + head_cols), bytes_accessed=rows * width * 14 + width * hidden_units * 4, transcendentals=0
        ),
        name="feed_back",
    )(rank, *parts, factor, slope, group_tokens, mean, inverse, blocks, norm_params, *priors)


def qkv_back_kernel(
    owned, waits, d_qkv_ref, part_ref, tokens_ref, mean_ref, inverse_ref, blocks_ref, norm_ref, *refs
):
    dz_ref, norm_sums, qkv_sums, w_qkv, sems = refs[waits:]
    size = blocks_ref.shape[-1]
    outer = w_qkv.shape[0] // size
    copies = block_copies(blocks_ref, owned, 0, outer, w_qkv.shape[1] // size, w_qkv, sems)
    begin_copies(copies)

    @pl.when(pl.program_id(0) == 0)
    def _():
        norm_sums[...] = jnp.zeros_like(norm_sums)
        qkv_sums[...] = jnp.zeros_like(qkv_sums)

    qkv_sums[...] += column_sum(d_qkv_ref[...].astype(jnp.float32))
    mean, inverse = mean_ref[...], inverse_ref[...]
    end_copies(copies)
    for col in range(outer):
        cols = pl.ds(col * size, size)
        scaled = (tokens_ref[:, cols].astype(jnp.float32) - mean) * inverse
        first = contract(d_qkv_ref[...], w_qkv[cols, :], NT)
        dz_ref[:, cols] = (part_ref[:, cols].astype(jnp.float32) + first * norm_ref[0:1, cols]).astype(jnp.bfloat16)
        norm_sums[0:8, cols] += column_sum(first * scaled)
        norm_sums[8:16, cols] += column_sum(first)


def qkv_back(d_qkv, dz_part, group_tokens, mean, inverse, blocks, owned, norm_params, waits):
    tokens, qkv_cols = d_qkv.shape
    width = dz_part.shape[1]
    size = blocks.shape[-1]
    tile = 512
    row = lambda cols: pl.BlockSpec((tile, cols), lambda i: (i, 0))
    whole = lambda rows, cols: pl.BlockSpec((rows, cols), lambda i: (0, 0))
    outer = width // size
    return pl.pallas_call(
        functools.partial(qkv_back_kernel, owned, len(waits)),
        grid=(tokens // tile,),
        in_specs=[
            row(qkv_cols), row(width), row(width), row(1), row(1), pl.BlockSpec(memory_space=pl.ANY), whole(norm_params.shape[0], width),
        ]
        + [pl.BlockSpec(memory_space=pl.ANY)] * len(waits),
        out_specs=[row(width), whole(16, width), whole(8, qkv_cols)],
        out_shape=[
            jax.ShapeDtypeStruct((tokens, width), jnp.bfloat16),
            jax.ShapeDtypeStruct((16, width), jnp.float32),
            jax.ShapeDtypeStruct((8, qkv_cols), jnp.float32),
        ],
        scratch_shapes=[
            pltpu.VMEM((width, qkv_cols), jnp.bfloat16),
            pltpu.SemaphoreType.DMA((outer * (qkv_cols // size),)),
        ],
        compiler_params=kernel_params(),
        cost_estimate=pl.CostEstimate(
            flops=2 * tokens * width * qkv_cols, bytes_accessed=tokens * width * 11, transcendentals=0
        ),
        name="qkv_back",
    )(d_qkv, dz_part, group_tokens, mean, inverse, blocks, norm_params, *waits)


def weight_grad_kernel(steps, waits, core_ref, *refs):
    lefts, rights, refs = refs[:4], refs[4:7], refs[7 + waits :]
    outs, rows_held, rights_held = refs[:2], refs[2], refs[3:6]
    results, left_sems, right_sems, sems = refs[6:]
    size = results.shape[-1]
    core = core_ref[0]
    depth = rows_held.shape[0]

    def left_copy(index):
        left, first, rows, _, _, _ = steps[index]
        return pltpu.make_async_copy(
            lefts[left].at[pl.ds(first, rows), :],
            rows_held.at[index % depth, pl.ds(0, rows), :],
            left_sems.at[index % depth],
        )

    def right_copy(right, first):
        held = rights_held[right]
        return pltpu.make_async_copy(
            rights[right].at[:, pl.ds(first, held.shape[1])], held, right_sems.at[right]
        )

    def finish(index):
        for place in range(len(steps[index][5])):
            pltpu.make_async_copy(
                results.at[index % 2, place], outs[0].at[0], sems.at[index % 2, place]
            ).wait()

    order = []
    for step in steps:
        if step[3:5] not in order:
            order.append(step[3:5])
    right_copy(*order[0]).start()
    for index in range(min(depth - 1, len(steps))):
        left_copy(index).start()
    for right in order[1:]:
        right_copy(*right).start()
    for index, (left, first, rows, right, right_first, places) in enumerate(steps):
        left_copy(index).wait()
        if index + depth - 1 < len(steps):
            left_copy(index + depth - 1).start()
        if all(step[3:5] != (right, right_first) for step in steps[:index]):
            right_copy(right, right_first).wait()
        if index >= 2:
            finish(index - 2)
        held = rights_held[right]
        cols = held.shape[1] // size
        for col in range(cols):
            result = contract(rows_held[index % depth, :rows, :], held[:, col * size : (col + 1) * size], NN)
            for row in range(rows // size):
                results[index % 2, row * cols + col] = result[row * size : (row + 1) * size].astype(jnp.bfloat16)
        for number, (owner, place) in enumerate(places):
            for away in range(2):

                @pl.when((core == owner % 2) == (away == 0))
                def _():
                    pltpu.make_async_copy(
                        results.at[index % 2, number], outs[away].at[place], sems.at[index % 2, number]
                    ).start()

    for index in range(max(0, len(steps) - 2), len(steps)):
        finish(index)


def weight_grads(part, parts, lefts, rights, firsts, core, owned, dp_ways, size, waits):
    first_normed, second_normed, activated, attended = lefts
    d_hidden, seed, d_qkv = rights
    tokens = d_qkv.shape[0]
    width = seed.shape[1]
    part_size = owned // parts
    qkv_blocks = d_qkv.shape[1] // size
    per_row = width // size
    span = per_row // parts
    steps = []
    for left, right, first, rows_all in (
        (1, 0, firsts[2], second_normed.shape[0]),
        (2, 1, firsts[3], activated.shape[0]),
        (3, 1, firsts[1], attended.shape[0]),
    ):
        rows = min(512, rows_all)
        for begin in range(0, rows_all, rows):
            places = []
            for row in range(begin // size, (begin + rows) // size):
                for col in range(span):
                    block = first + row * per_row + part * span + col
                    owner, within = block // owned, block % owned
                    places.append((owner, owner // 2 * part_size + within // per_row * span + col))
            steps.append((left, begin, rows, right, part * span * size, tuple(places)))
    for owner in range(per_row // parts):
        row = owner * parts + part
        places = [(owner, owner // 2 * part_size + col) for col in range(qkv_blocks)]
        steps.append((0, row * size, size, 2, 0, tuple(places)))
    most = max(len(step[5]) for step in steps)
    anywhere = pl.BlockSpec(memory_space=pl.ANY)
    half = jax.ShapeDtypeStruct((dp_ways // 2 * part_size, size, size), jnp.bfloat16)
    flops = 2 * tokens * size * size * dp_ways * part_size
    return pl.pallas_call(
        functools.partial(weight_grad_kernel, tuple(steps), len(waits)),
        in_specs=[pl.BlockSpec(memory_space=pltpu.SMEM)] + [anywhere] * (7 + len(waits)),
        out_specs=[anywhere] * 2,
        out_shape=[half] * 2,
        scratch_shapes=[
            pltpu.VMEM((4, max(step[2] for step in steps), tokens), jnp.bfloat16),
            pltpu.VMEM((tokens, span * size), jnp.bfloat16),
            pltpu.VMEM((tokens, span * size), jnp.bfloat16),
            pltpu.VMEM((tokens, d_qkv.shape[1]), jnp.bfloat16),
            pltpu.VMEM((2, most, size, size), jnp.bfloat16),
            pltpu.SemaphoreType.DMA((4,)),
            pltpu.SemaphoreType.DMA((3,)),
            pltpu.SemaphoreType.DMA((2, most)),
        ],
        compiler_params=kernel_params(),
        cost_estimate=pl.CostEstimate(flops=flops, bytes_accessed=flops // 500, transcendentals=0),
        name="weight_grads",
    )(core, *lefts, *rights, *waits)


def pair_sum_kernel(chip_ref, *refs):
    chips = len(refs) // 3
    for index in range(chips):
        total = refs[index][...].astype(jnp.float32) + refs[chips + index][...].astype(jnp.float32)
        refs[2 * chips + index][...] = total.astype(refs[2 * chips + index].dtype)


def pair_sum(kept, received, chip, chips):
    rows, size, _ = kept.shape
    part = rows // chips
    spec = lambda away: pl.BlockSpec(
        (part, size, size), lambda i, chip: (jnp.bitwise_xor(chip[0], away), 0, 0)
    )
    plain = pl.BlockSpec((part, size, size), lambda i, chip: (0, 0, 0))
    dtypes = [jnp.float32] + [jnp.bfloat16] * (chips - 1)
    return pl.pallas_call(
        pair_sum_kernel,
        grid_spec=pltpu.PrefetchScalarGridSpec(
            num_scalar_prefetch=1,
            grid=(1,),
            in_specs=[spec(away) for away in range(chips)] * 2,
            out_specs=[plain] * chips,
        ),
        out_shape=[jax.ShapeDtypeStruct((part, size, size), dtype) for dtype in dtypes],
        compiler_params=kernel_params(),
        cost_estimate=pl.CostEstimate(flops=rows * size * size, bytes_accessed=rows * size * size * 6, transcendentals=0),
        name="pair_sum",
    )(chip, *([kept] * chips), *([received] * chips))


def input_grad_kernel(moved_ref, last_ref, tokens_ref, seed_ref, mean_ref, inverse_ref, out_ref):
    d_scaled = moved_ref[...].astype(jnp.float32) + last_ref[...].astype(jnp.float32)
    inverse = inverse_ref[...]
    scaled = (tokens_ref[...].astype(jnp.float32) - mean_ref[...]) * inverse
    average = jnp.mean(d_scaled, axis=1, keepdims=True)
    projection = jnp.mean(d_scaled * scaled, axis=1, keepdims=True)
    out_ref[...] = seed_ref[...].astype(jnp.float32) + inverse * (d_scaled - average - scaled * projection)


def input_gradient(moved, dz, tokens, seed, mean, inverse, rank, waits):
    rows, width = moved.shape
    tile = min(128, rows)
    per = rows // tile
    own = lambda n: pl.BlockSpec((tile, n), lambda i, rank: (i, 0))
    ranked = lambda n: pl.BlockSpec((tile, n), lambda i, rank: (rank[0] * per + i, 0))

    def kernel(rank_ref, *refs):
        input_grad_kernel(*refs[:6], refs[-1])

    return pl.pallas_call(
        kernel,
        grid_spec=pltpu.PrefetchScalarGridSpec(
            num_scalar_prefetch=1,
            grid=(per,),
            in_specs=[own(width), ranked(width), own(width), ranked(width), ranked(1), ranked(1)]
            + [pl.BlockSpec(memory_space=pl.ANY)] * len(waits),
            out_specs=own(width),
        ),
        out_shape=jax.ShapeDtypeStruct((rows, width), jnp.float32),
        compiler_params=kernel_params(),
        cost_estimate=pl.CostEstimate(flops=rows * width * 12, bytes_accessed=rows * width * 12, transcendentals=0),
        name="input_gradient",
    )(rank, moved, dz, tokens, seed, mean, inverse, *waits)


def dot32(left_arg, right_arg):
    return jnp.dot(left_arg, right_arg, preferred_element_type=jnp.float32)


def two_terms(values):
    high = values.astype(jnp.bfloat16)
    return high, (values - high.astype(jnp.float32)).astype(jnp.bfloat16)


def shampoo_kernel(count, terms, held, places_ref, *refs):
    grads, refs = refs[:terms], refs[terms:]
    left_refs, right_refs, master_refs = (refs[side * count : (side + 1) * count] for side in range(3))
    outs, refs = refs[3 * count + held : 3 * count + held + 4], refs[3 * count + held + 4 :]
    results, scaled, roots, pairs, powers, high, low, sems = refs
    size = results.shape[-1]
    step, steps = pl.program_id(0), pl.num_programs(0)
    slot = lax.rem(step, 2)
    chains = range(2 * count)
    stat_refs = (left_refs, right_refs)
    identity = (
        lax.broadcasted_iota(jnp.int32, (size, size), 0)
        == lax.broadcasted_iota(jnp.int32, (size, size), 1)
    ).astype(jnp.float32)

    def copies(of_step, of_slot):
        return [
            pltpu.make_async_copy(
                results.at[of_slot, kind, block],
                outs[kind].at[places_ref[of_step * count + block]],
                sems.at[of_slot, kind, block],
            )
            for kind in range(4)
            for block in range(count)
        ]

    @pl.when(step >= 2)
    def _():
        for copy in copies(step - 2, slot):
            copy.wait()

    grad16 = []
    for block in range(count):
        total = grads[0][block].astype(jnp.float32)
        for grad in grads[1:]:
            total = total + grad[block].astype(jnp.float32)
        results[slot, 0, block] = total
        grad16.append(total.astype(jnp.bfloat16))
    for item in chains:
        block, side = item // 2, item % 2
        dims = (((1 - side,), (1 - side,)), ((), ()))
        results[slot, 1 + side, block] = DECAY * stat_refs[side][block][0] + lax.dot_general(
            grad16[block], grad16[block], dims, preferred_element_type=jnp.float32
        )
    sums = []
    for item in chains:
        stat = results[slot, 1 + item % 2, item // 2]
        sums.append(jnp.sum(stat * stat, axis=0, keepdims=True))
    norms = [jnp.sqrt(jnp.sum(each, axis=1, keepdims=True)) for each in sums]
    for item in chains:
        scaled[item] = results[slot, 1 + item % 2, item // 2] * (1.0 / norms[item])
    factors = [lax.rsqrt(jnp.sqrt(norm)) for norm in norms]

    for repeat in range(ROOT_ITERS - 1):
        for item in chains:
            quarter = (identity - scaled[item]) * 0.25
            pairs[item, size:] = quarter.astype(jnp.bfloat16)
            if repeat == 0:
                roots[item] = identity + quarter
            else:
                pairs[item, :size] = roots[item].astype(jnp.bfloat16)
        if repeat == 0:
            squares = [dot32(pairs[item, size:], pairs[item, size:]) for item in chains]
        else:
            both = [dot32(pairs[item], pairs[item, size:]) for item in chains]
            for item in chains:
                roots[item] = roots[item] + both[item][:size]
            squares = [each[size:] for each in both]
        seconds = [(identity - scaled[item]) * 0.5 + squares[item] for item in chains]
        seconds16 = [second.astype(jnp.bfloat16) for second in seconds]
        fourths = [2.0 * seconds[item] + dot32(seconds16[item], seconds16[item]) for item in chains]
        for item in chains:
            high[item], low[item] = two_terms(scaled[item])
            powers[item, :size], powers[item, size:] = two_terms(fourths[item])
        for item in chains:
            both_terms = dot32(powers[item], high[item])
            scaled[item] = scaled[item] + (
                both_terms[:size] + both_terms[size:] + dot32(powers[item, :size], low[item])
            )
    for item in chains:
        pairs[item, size:] = ((identity - scaled[item]) * 0.25).astype(jnp.bfloat16)
        pairs[item, :size] = roots[item].astype(jnp.bfloat16)
    for item in chains:
        ends = two_terms(roots[item] + dot32(pairs[item, :size], pairs[item, size:]))
        if item % 2 == 0:
            powers[item, :size], powers[item, size:] = ends
        else:
            high[item], low[item] = ends
    halves = []
    for block in range(count):
        both_terms = dot32(powers[2 * block], grad16[block])
        halves.append(both_terms[:size] + both_terms[size:])
    for block in range(count):
        pairs[block, :size], pairs[block, size:] = two_terms(halves[block])
    for block in range(count):
        item = 2 * block + 1
        both_terms = dot32(pairs[block], high[item])
        product = both_terms[:size] + both_terms[size:] + dot32(pairs[block, :size], low[item])
        rate = RATE_BLOCK * factors[2 * block] * factors[item]
        results[slot, 3, block] = master_refs[block][0] - rate * product
    for copy in copies(step, slot):
        copy.start()

    @pl.when(step == steps - 1)
    def _():
        @pl.when(steps >= 2)
        def _():
            for copy in copies(step - 1, 1 - slot):
                copy.wait()

        for copy in copies(step, slot):
            copy.wait()


def shampoo(grads, left_stats, right_stats, master_blocks, places, priors, waits=()):
    part, size, _ = grads[0].shape
    count = next(each for each in (3, 2, 1) if part % each == 0)
    own = pl.BlockSpec((count, size, size), lambda step, places: (step, 0, 0))
    anywhere = pl.BlockSpec(memory_space=pl.ANY)

    def single(block):
        return pl.BlockSpec((1, size, size), lambda step, places: (places[step * count + block], 0, 0))

    result = jax.ShapeDtypeStruct(left_stats.shape, jnp.float32)
    held = len(priors)
    first_prior = 1 + len(grads) + 3 * count
    wide = pltpu.VMEM((2 * count, 2 * size, size), jnp.bfloat16)
    plain = pltpu.VMEM((2 * count, size, size), jnp.bfloat16)
    return pl.pallas_call(
        functools.partial(shampoo_kernel, count, len(grads), held + len(waits)),
        grid_spec=pltpu.PrefetchScalarGridSpec(
            num_scalar_prefetch=1,
            grid=(part // count,),
            in_specs=[own] * len(grads)
            + [single(block) for block in range(count)] * 3
            + [anywhere] * (held + len(waits)),
            out_specs=[anywhere] * 4,
            scratch_shapes=[
                pltpu.VMEM((2, 4, count, size, size), jnp.float32),
                pltpu.VMEM((2 * count, size, size), jnp.float32),
                pltpu.VMEM((2 * count, size, size), jnp.float32),
                wide,
                wide,
                plain,
                plain,
                pltpu.SemaphoreType.DMA((2, 4, count)),
            ],
        ),
        out_shape=[result] * 4,
        input_output_aliases={first_prior + index: index for index in range(held)},
        compiler_params=kernel_params(),
        cost_estimate=pl.CostEstimate(
            flops=part * 130 * 2 * size**3, bytes_accessed=part * size * size * 30, transcendentals=0
        ),
        name="shampoo",
    )(
        places,
        *grads,
        *([left_stats] * count),
        *([right_stats] * count),
        *([master_blocks] * count),
        *priors,
        *waits,
    )


def after(value, *earlier):
    return lax.optimization_barrier((value,) + earlier)[0]


def onward(part, axis):
    ways = lax.axis_size(axis)
    return lax.ppermute(part, axis, [(each, (each + 1) % ways) for each in range(ways)])


def swap(part, bits):
    ways = lax.axis_size("dp")
    return lax.ppermute(part, "dp", [(each, each ^ bits) for each in range(ways)])


def small_rows(values, ways):
    return jnp.pad(values, ((0, 0), (0, -values.shape[1] % 2048))).reshape(-1, 128)


def shards(
    tokens,
    cotangent,
    segments,
    subsets,
    packs,
    master_blocks,
    left_stats,
    right_stats,
    local_vecs,
    local_vec_stats,
    shared_vecs,
    shared_vec_stats,
):
    tp_ways = lax.axis_size("tp")
    dp_ways = lax.axis_size("dp")
    tp_rank = lax.axis_index("tp")
    tok_dev, model_width = tokens.shape
    group_tok = tok_dev * tp_ways
    pack_count, pack_len = segments.shape
    seg_width = subsets.shape[1]
    heads_dev = HEADS // tp_ways
    ff_dev = FF // tp_ways
    head_cols = heads_dev * HD
    owned, block_size, _ = master_blocks.shape
    block_rows = model_width // block_size
    first_out = block_rows * (3 * head_cols // block_size)
    first_in = first_out + head_cols // block_size * block_rows
    first_down = first_in + block_rows * (ff_dev // block_size)
    all_count = owned * dp_ways
    vec_rows = 3 * heads_dev + ff_dev // HD

    vec_used = local_vecs.size
    shared_used = shared_vecs.size
    vec_flat = jnp.concatenate([local_vecs.reshape(-1), shared_vecs.reshape(-1)])
    extra = jnp.pad(vec_flat, (0, EXTRA_ROWS * block_size - vec_flat.size)).reshape(EXTRA_ROWS, block_size)
    rows16 = jnp.concatenate([master_blocks.reshape(-1, block_size), extra], 0).astype(jnp.bfloat16)
    blocks = lax.all_gather(rows16, "dp", axis=0, tiled=True)

    token_parts = [tokens]
    for step in range(1, tp_ways):
        token_parts.append(onward(token_parts[-1], "tp"))

    gathered = blocks.reshape(dp_ways, -1, block_size)[:, owned * block_size :].reshape(dp_ways, -1)
    vec_values = (
        gathered[:, :vec_used].reshape(dp_ways, vec_rows, -1).transpose(1, 0, 2).reshape(vec_rows, HD)
    ).astype(jnp.float32)
    shared_mine = gathered[:, vec_used : vec_used + shared_used]
    shared_all = jnp.zeros((tp_ways,) + shared_mine.shape, jnp.bfloat16)
    for step in range(tp_ways):
        part = shared_mine
        if step:
            part = lax.ppermute(
                part, "tp", [(each, (each + step) % tp_ways) for each in range(tp_ways)]
            )
        shared_all = lax.dynamic_update_slice(
            shared_all, part[None], ((tp_rank - step) % tp_ways, 0, 0)
        )
    norm_params = (
        shared_all.reshape(tp_ways, dp_ways, 6, -1).transpose(2, 1, 0, 3).reshape(6, model_width)
    ).astype(jnp.float32)
    bias_qkv = vec_values[: 3 * heads_dev].reshape(1, -1)
    bias_in = vec_values[3 * heads_dev :].reshape(1, -1)

    own_pos = tp_rank * tok_dev + jnp.arange(tok_dev)
    own_pack = own_pos // pack_len
    valid_own = (own_pack < packs[0]).astype(jnp.float32)
    owned_input_rows = tokens.astype(jnp.float32)

    group_pack = jnp.arange(group_tok) // pack_len
    lookup_key = group_pack * seg_width + segments.reshape(-1)
    onehot = lookup_key[:, None] == jnp.arange(pack_count * seg_width)[None, :]
    subset_tok = jnp.sum(jnp.where(onehot, subsets.reshape(-1)[None, :], 0), axis=1)
    weight = 0.5 + subset_tok.astype(jnp.float32) / (SUBSETS - 1)
    factor = (weight * (group_pack < packs[0]).astype(jnp.float32))[:, None]

    rank = tp_rank.astype(jnp.int32)[None]
    cosines, sines = turn_tables(pack_len, 128)
    cotangent_parts = [cotangent, onward(after(cotangent, token_parts[-1], shared_all), "tp")]
    qkv16, first_turned, second_normed, second_turned, group_tokens, mean, inverse = project_qkv(
        token_parts, rank, blocks, owned, norm_params, bias_qkv, cosines, sines, heads_dev
    )
    attended, attended_turned = attend(qkv16, segments, heads_dev)
    cotangent_parts.append(onward(after(cotangent_parts[-1], attended), "tp"))
    active_turned, slope, partial_value = feed_forward(
        second_normed, attended, blocks, owned, bias_in, (first_out, first_in, first_down)
    )
    while len(cotangent_parts) < tp_ways:
        cotangent_parts.append(onward(after(cotangent_parts[-1], slope), "tp"))

    back_args = (
        tp_ways, rank, factor, slope, group_tokens, mean, inverse, blocks, owned, norm_params,
        (first_out, first_in, first_down), head_cols,
    )
    early = feed_back(cotangent_parts[:-1], 0, *back_args, ())
    late = feed_back(cotangent_parts[-1:], tp_ways - 1, *back_args, early[:4])
    seed_all, d_attended, d_hidden16, dz_part = late[:4]
    branch = lax.psum_scatter(
        after(partial_value, cotangent_parts[-1], early[5]), "tp", scatter_dimension=0, tiled=True
    )
    d_qkv16 = attend_back(qkv16, d_attended, segments, cosines, sines, heads_dev)
    dp_rank = lax.axis_index("dp").astype(jnp.int32)
    lefts = (first_turned, second_turned, active_turned, attended_turned)
    rights = (d_hidden16, seed_all, d_qkv16)
    firsts = (0, first_out, first_in, first_down)
    qkv_blocks = 3 * head_cols // block_size
    parts = 4
    by_part = (
        dp_ways == 8
        and owned == parts * qkv_blocks
        and block_rows == 2 * parts
        and ff_dev == model_width
        and owned % block_rows == 0
        and first_out % block_rows == 0
        and first_in % block_rows == 0
    )
    sums = []

    def quarter(part, waits):
        kept, away = weight_grads(
            part, parts, lefts, rights, firsts, (dp_rank % 2)[None], owned, dp_ways, block_size, waits
        )
        sums.append(pair_sum(kept, swap(away, 1), (dp_rank // 2)[None], dp_ways // 2))
        return kept

    first_waits = ()
    if by_part:
        quarter(0, ())
        quarter(1, ())
        first_waits = (sums[0][0],)
    dz16, first_sums, qkv_sums = qkv_back(
        d_qkv16, dz_part, group_tokens, mean, inverse, blocks, owned, norm_params, first_waits
    )
    dz_rows = lambda back: lax.dynamic_slice_in_dim(dz16, (tp_rank - back) % tp_ways * tok_dev, tok_dev, 0)
    back = 2

    def pass_on(moving, back):
        total = moving.astype(jnp.float32) + dz_rows(back).astype(jnp.float32)
        return total.astype(jnp.bfloat16)

    moving = onward(dz_rows(1), "tp")
    shared_local = jnp.concatenate(
        [
            jnp.sum(first_sums.reshape(2, 8, model_width), axis=1),
            jnp.sum((early[4][:16] + late[4][:16]).reshape(2, 8, model_width), axis=1),
            jnp.sum(early[4][16:], axis=0)[None],
        ],
        0,
    )
    vecs_local = jnp.concatenate(
        [
            jnp.sum(qkv_sums, axis=0).reshape(3 * heads_dev, HD),
            jnp.sum(early[5] + late[5], axis=0).reshape(ff_dev // HD, HD),
        ],
        0,
    )
    small = jnp.concatenate(
        [
            shared_local.reshape(5, dp_ways, -1).transpose(1, 0, 2).reshape(dp_ways, -1),
            vecs_local.reshape(vec_rows, dp_ways, -1).transpose(1, 0, 2).reshape(dp_ways, -1),
        ],
        1,
    )
    small_in = after(small_rows(small, dp_ways), branch)
    small_own = lax.psum_scatter(small_in, "dp", scatter_dimension=0, tiled=True).reshape(-1)
    output = (
        valid_own[:, None]
        * (owned_input_rows + branch.astype(jnp.float32) + norm_params[4] + norm_params[5])
    ).astype(jnp.bfloat16)

    shared_size = 5 * model_width // dp_ways
    own_vec_grads = small_own[shared_size : small.shape[1]].reshape(vec_rows, HD // dp_ways)
    shared_part = small_own[:shared_size].reshape(5, tp_ways, -1).transpose(1, 0, 2)
    shared_in = small_rows(shared_part.reshape(tp_ways, -1), tp_ways)
    shared_own = lax.psum_scatter(shared_in, "tp", scatter_dimension=0, tiled=True).reshape(-1)
    shared_own = shared_own[: shared_size // tp_ways].reshape(5, -1)
    shared_grads = jnp.concatenate([shared_own, shared_own[4:]], 0)
    results = ()
    if by_part:
        part_size = owned // parts
        span = block_rows // parts
        terms = []
        ready = []

        def send_on(part):
            if part:
                sums[part] = [sums[part][0]] + [after(each, terms[-1][3]) for each in sums[part][1:]]
                ready.append(sums[part][3])
            terms.append([sums[part][0]] + [swap(sums[part][bits], 2 * bits) for bits in range(1, 4)])

        send_on(0)
        quarter(2, (dz16, sums[1][0]) + tuple(terms[0][1:]))
        quarter(3, tuple(terms[0][1:]))
        for part in range(1, parts):
            send_on(part)
        count = jnp.arange(part_size, dtype=jnp.int32)
        in_qkv = dp_rank * owned < first_out
        for part in range(parts):
            places = jnp.where(
                in_qkv,
                part * part_size + count,
                count // span * block_rows + part * span + count % span,
            )
            waits = []
            if part < parts - 1:
                waits.append(ready[part])
            if part == 0:
                waits += terms[1][1:]
            if part % 2 == 0 and back < tp_ways:
                if part:
                    moving, first_result = lax.optimization_barrier((moving, results[0]))
                    results = [first_result] + list(results[1:])
                total = pass_on(moving, back)
                waits.append(total)
                moving = onward(total, "tp")
                back += 1
            if part == 1:
                waits.append(small_in)
            if part == 2:
                waits += [small_own, shared_in]
            if part == 3:
                waits += [output, shared_own]
            results = shampoo(
                terms[part], left_stats, right_stats, master_blocks, places, results, waits
            )
    else:
        local = [
            to_blocks(jnp.dot(left, right, preferred_element_type=jnp.float32).astype(jnp.bfloat16), block_size)
            for left, right in (
                (first_turned, d_qkv16),
                (attended_turned, seed_all),
                (second_turned, d_hidden16),
                (active_turned, seed_all),
            )
        ]
        grads16 = lax.psum_scatter(jnp.concatenate(local, 0), "dp", scatter_dimension=0, tiled=True)
        results = shampoo(
            [grads16], left_stats, right_stats, master_blocks, jnp.arange(owned, dtype=jnp.int32), results
        )
    while back < tp_ways:
        moving = onward(pass_on(moving, back), "tp")
        back += 1
    input_grad = input_gradient(moving, dz16, tokens, seed_all, mean, inverse, rank, results[:1])
    own_grads, left_new, right_new, new_blocks = results
    local_stat_new = DECAY * local_vec_stats + own_vec_grads * own_vec_grads
    local_new = local_vecs - RATE_VEC * own_vec_grads * lax.rsqrt(local_stat_new)
    shared_stat_new = DECAY * shared_vec_stats + shared_grads * shared_grads
    shared_new = shared_vecs - RATE_VEC * shared_grads * lax.rsqrt(shared_stat_new)
    return (
        output,
        input_grad,
        own_grads,
        left_new,
        right_new,
        new_blocks,
        own_vec_grads,
        local_stat_new,
        local_new,
        shared_grads,
        shared_stat_new,
        shared_new,
    )


def solution(mesh):
    placed = (
        P(("dp", "tp"), None),
        P(("dp", "tp"), None),
        P("dp", None),
        P("dp", None),
        P("dp"),
        P(("dp", "tp"), None, None),
        P(("dp", "tp"), None, None),
        P(("dp", "tp"), None, None),
        P("tp", "dp"),
        P("tp", "dp"),
        P(None, ("dp", "tp")),
        P(None, ("dp", "tp")),
    )
    return jax.shard_map(
        shards,
        mesh=mesh,
        in_specs=placed,
        out_specs=(
            P(("dp", "tp"), None),
            P(("dp", "tp"), None),
            P(("dp", "tp"), None, None),
            P(("dp", "tp"), None, None),
            P(("dp", "tp"), None, None),
            P(("dp", "tp"), None, None),
            P("tp", "dp"),
            P("tp", "dp"),
            P("tp", "dp"),
            P(None, ("dp", "tp")),
            P(None, ("dp", "tp")),
            P(None, ("dp", "tp")),
        ),
        check_vma=False,
    )
```

```python
import functools
import math

import jax
import jax.numpy as jnp
from jax import lax
from jax.experimental import pallas as pl
from jax.experimental.pallas import tpu as pltpu
from jax.sharding import PartitionSpec as P

HEADS = 8
HD = 256
ROT = 64
FF = 8192
SUBSETS = 22
ROOT_ITERS = 8


EPS_NORM = 1e-05
DECAY = 0.5
RATE_BLOCK = 0.6
RATE_VEC = 0.2
NEG_FILL = -1e30
DOC_MAX = 512
HALF_ROOT = 0.7071067811865476
DENSITY_SCALE = 0.3989422804014327


def to_blocks(matrix, block_size):
    block_rows = matrix.shape[0] // block_size
    block_cols = matrix.shape[1] // block_size
    return (
        matrix.reshape(block_rows, block_size, block_cols, block_size)
        .transpose(0, 2, 1, 3)
        .reshape(block_rows * block_cols, block_size, block_size)
    )


EXTRA_ROWS = 16
FEED_BACK_TILE = 512
VMEM_LIMIT = 60 << 20
NN = (((1,), (0,)), ((), ()))
NT = (((1,), (1,)), ((), ()))
TN = (((0,), (0,)), ((), ()))


def contract(left_arg, right_arg, dims):
    return lax.dot_general(left_arg, right_arg, dims, preferred_element_type=jnp.float32)


def kernel_params():
    return pltpu.CompilerParams(vmem_limit_bytes=VMEM_LIMIT)


def block_row(index, owned, size):
    return index // owned * (owned * size + EXTRA_ROWS) + index % owned * size


def block_copies(blocks_ref, owned, first, rows, cols, target, sems):
    size = blocks_ref.shape[-1]
    return [
        pltpu.make_async_copy(
            blocks_ref.at[pl.ds(block_row(first + row * cols + col, owned, size), size), :],
            target.at[pl.ds(row * size, size), pl.ds(col * size, size)],
            sems.at[row * cols + col],
        )
        for row in range(rows)
        for col in range(cols)
    ]


def begin_copies(copies):
    @pl.when(pl.program_id(0) == 0)
    def _():
        for copy in copies:
            copy.start()


def end_copies(copies):
    @pl.when(pl.program_id(0) == 0)
    def _():
        for copy in copies:
            copy.wait()


def turn(values, cosines, sines):
    lane = lax.broadcasted_iota(jnp.int32, values.shape, 1)
    half = ROT // 2
    wide = values.shape[1]
    swapped = jnp.where(
        lane < half, pltpu.roll(values, wide - half, 1), pltpu.roll(values, half, 1)
    )
    return values * cosines + swapped * sines


def turn_tables(pack_len, lanes):
    half = ROT // 2
    positions = jnp.arange(pack_len).astype(jnp.float32)
    freqs = 10000.0 ** (-(jnp.arange(half).astype(jnp.float32) * 2.0) / ROT)
    angles = positions[:, None] * freqs[None, :]
    cosines = jnp.cos(angles)
    sines = jnp.sin(angles)
    rest = jnp.zeros((pack_len, lanes - ROT), jnp.float32)
    return (
        jnp.concatenate([cosines, cosines, rest + 1.0], -1),
        jnp.concatenate([-sines, sines, rest], -1),
    )


def normed_rows(rows):
    mean = jnp.mean(rows, axis=1, keepdims=True)
    centred = rows - mean
    variance = jnp.mean(centred * centred, axis=1, keepdims=True)
    return mean, lax.rsqrt(variance + EPS_NORM)


def part_copies(part_refs, held, sems):
    return [
        pltpu.make_async_copy(part, held.at[index], sems.at[index])
        for index, part in enumerate(part_refs)
    ]


def await_part(copies, per_part):
    step = pl.program_id(0)
    for index, copy in enumerate(copies):

        @pl.when(step == index * per_part)
        def _():
            copy.wait()


def qkv_kernel(heads, owned, parts, rank_ref, *refs):
    part_refs = refs[:parts]
    blocks_ref, norm_ref, bias_ref, cos_ref, sin_ref = refs[parts : parts + 5]
    outs, (normed, weight, held, sems, part_sems) = refs[parts + 5 : parts + 12], refs[parts + 12 :]
    qkv_ref, first_turned, second_ref, second_turned, tokens_ref, mean_ref, inverse_ref = outs
    size = blocks_ref.shape[-1]
    copies = block_copies(blocks_ref, owned, 0, weight.shape[0] // size, weight.shape[1] // size, weight, sems)
    moves = part_copies(part_refs, held, part_sems)
    begin_copies(moves + copies)
    await_part(moves, 1)
    own = held[pl.program_id(0)]
    tokens_ref[...] = own
    rows = own.astype(jnp.float32)
    mean, inverse = normed_rows(rows)
    mean_ref[...] = mean
    inverse_ref[...] = inverse
    for col in range(rows.shape[1] // size):
        cols = pl.ds(col * size, size)
        scaled = (own[:, col * size : (col + 1) * size].astype(jnp.float32) - mean) * inverse
        second = (scaled * norm_ref[2:3, cols] + norm_ref[3:4, cols]).astype(jnp.bfloat16)
        second_ref[:, cols] = second
        second_turned[cols, :] = second.T
        first = (scaled * norm_ref[0:1, cols] + norm_ref[1:2, cols]).astype(jnp.bfloat16)
        normed[:, cols] = first
        first_turned[cols, :] = first.T
    end_copies(copies)
    lanes = cos_ref.shape[1]
    for head in range(heads):
        for part in range(3):
            cols = pl.ds((head * 3 + part) * HD, HD)
            result = contract(normed[...], weight[:, cols], NN) + bias_ref[:, cols]
            if part < 2:
                first = turn(result[:, :lanes], cos_ref[...], sin_ref[...])
                result = jnp.concatenate([first, result[:, lanes:]], 1)
            if part == 0:
                result = result * (1.0 / math.sqrt(HD))
            qkv_ref[:, cols] = result.astype(jnp.bfloat16)


def project_qkv(parts, rank, blocks, owned, norm_params, bias, cosines, sines, heads):
    ways = len(parts)
    tile, width = parts[0].shape
    tokens = ways * tile
    size = blocks.shape[-1]
    pack_len, lanes = cosines.shape
    cols = 3 * heads * HD
    per_pack = pack_len // tile
    place = lambda i, rank: (rank[0] - i + ways) % ways
    row = lambda n: pl.BlockSpec((tile, n), lambda i, rank: (place(i, rank), 0))
    table = pl.BlockSpec((tile, lanes), lambda i, rank: (place(i, rank) % per_pack, 0))
    anywhere = pl.BlockSpec(memory_space=pl.ANY)
    wide = jax.ShapeDtypeStruct((tokens, width), jnp.bfloat16)
    tall = jax.ShapeDtypeStruct((width, tokens), jnp.bfloat16)
    single = jax.ShapeDtypeStruct((tokens, 1), jnp.float32)
    turned = pl.BlockSpec((width, tile), lambda i, rank: (0, place(i, rank)))
    return pl.pallas_call(
        functools.partial(qkv_kernel, heads, owned, ways),
        grid_spec=pltpu.PrefetchScalarGridSpec(
            num_scalar_prefetch=1,
            grid=(ways,),
            in_specs=[anywhere] * (ways + 1)
            + [
                pl.BlockSpec(norm_params.shape, lambda i, rank: (0, 0)),
                pl.BlockSpec((1, cols), lambda i, rank: (0, 0)),
                table,
                table,
            ],
            out_specs=[row(cols), turned, row(width), turned, row(width), row(1), row(1)],
            scratch_shapes=[
                pltpu.VMEM((tile, width), jnp.bfloat16),
                pltpu.VMEM((width, cols), jnp.bfloat16),
                pltpu.VMEM((ways, tile, width), jnp.bfloat16),
                pltpu.SemaphoreType.DMA((width // size * (cols // size),)),
                pltpu.SemaphoreType.DMA((ways,)),
            ],
        ),
        out_shape=[jax.ShapeDtypeStruct((tokens, cols), jnp.bfloat16), tall, wide, tall, wide, single, single],
        compiler_params=kernel_params(),
        cost_estimate=pl.CostEstimate(
            flops=2 * tokens * width * cols, bytes_accessed=tokens * (4 * width + cols) * 2 + width * cols * 2, transcendentals=0
        ),
        name="qkv",
    )(rank, *parts, blocks, norm_params, bias, cosines, sines)


def attend_kernel(query_ref, key_ref, value_ref, seg_row, seg_col, out_ref, turned_ref):
    length = key_ref.shape[0]
    step = 256
    for start in range(0, length, step):
        first = max(0, start - DOC_MAX)
        stop = start + step
        scores = contract(query_ref[start:stop, :], key_ref[first:stop, :], NT)
        row = lax.broadcasted_iota(jnp.int32, scores.shape, 0) + start
        col = lax.broadcasted_iota(jnp.int32, scores.shape, 1) + first
        allowed = (col <= row) & (seg_col[0, start:stop, :] == seg_row[0, :, first:stop])
        masked = jnp.where(allowed, scores, NEG_FILL)
        exp_terms = jnp.exp(masked - jnp.max(masked, axis=1, keepdims=True))
        probs = exp_terms * (1.0 / jnp.sum(exp_terms, axis=1, keepdims=True))
        result = contract(probs.astype(jnp.bfloat16), value_ref[first:stop, :], NN).astype(jnp.bfloat16)
        out_ref[start:stop, :] = result
        turned_ref[:, start:stop] = result.T


def attend(qkv, segments, heads):
    packs, length = segments.shape
    part = lambda which: pl.BlockSpec((length, HD), lambda p, h: (p, h * 3 + which))
    return pl.pallas_call(
        attend_kernel,
        grid=(packs, heads),
        in_specs=[
            part(0),
            part(1),
            part(2),
            pl.BlockSpec((1, 1, length), lambda p, h: (p, 0, 0)),
            pl.BlockSpec((1, length, 1), lambda p, h: (p, 0, 0)),
        ],
        out_specs=[
            pl.BlockSpec((length, HD), lambda p, h: (p, h)),
            pl.BlockSpec((HD, length), lambda p, h: (h, p)),
        ],
        out_shape=[
            jax.ShapeDtypeStruct((packs * length, heads * HD), jnp.bfloat16),
            jax.ShapeDtypeStruct((heads * HD, packs * length), jnp.bfloat16),
        ],
        compiler_params=kernel_params(),
        cost_estimate=pl.CostEstimate(
            flops=packs * heads * length * length * HD * 3, bytes_accessed=packs * length * heads * HD * 8, transcendentals=0
        ),
        name="attend",
    )(qkv, qkv, qkv, segments[:, None, :], segments[:, :, None])


def attend_back_kernel(
    query_ref, key_ref, value_ref, d_out_ref, seg_row, seg_col, cos_ref, sin_ref, grad_ref, d_key, d_value
):
    length = key_ref.shape[0]
    step = 256
    lanes = cos_ref.shape[1]
    d_key[...] = jnp.zeros_like(d_key)
    d_value[...] = jnp.zeros_like(d_value)
    for start in range(0, length, step):
        first = max(0, start - DOC_MAX)
        stop = start + step
        query = query_ref[start:stop, :]
        d_out = d_out_ref[start:stop, :]
        keys = key_ref[first:stop, :]
        scores = contract(keys, query, NT)
        key_pos = lax.broadcasted_iota(jnp.int32, scores.shape, 0) + first
        query_pos = lax.broadcasted_iota(jnp.int32, scores.shape, 1) + start
        allowed = (key_pos <= query_pos) & (seg_col[0, first:stop, :] == seg_row[0, :, start:stop])
        masked = jnp.where(allowed, scores, NEG_FILL)
        exp_terms = jnp.exp(masked - jnp.max(masked, axis=0, keepdims=True))
        probs = exp_terms * (1.0 / jnp.sum(exp_terms, axis=0, keepdims=True))
        d_probs = contract(value_ref[first:stop, :], d_out, NT)
        row_dot = jnp.sum(probs * d_probs, axis=0, keepdims=True)
        d_scores = (probs * (d_probs - row_dot)).astype(jnp.bfloat16)
        d_value[first:stop, :] += contract(probs.astype(jnp.bfloat16), d_out, NN)
        d_key[first:stop, :] += contract(d_scores, query, NN)
        d_query = contract(d_scores, keys, TN) * (1.0 / math.sqrt(HD))
        back = turn(d_query[:, :lanes], cos_ref[start:stop, :], -sin_ref[start:stop, :])
        grad_ref[start:stop, :lanes] = back.astype(jnp.bfloat16)
        grad_ref[start:stop, lanes:HD] = d_query[:, lanes:].astype(jnp.bfloat16)
    back = turn(d_key[:, :lanes], cos_ref[...], -sin_ref[...])
    grad_ref[:, HD : HD + lanes] = back.astype(jnp.bfloat16)
    grad_ref[:, HD + lanes : 2 * HD] = d_key[:, lanes:].astype(jnp.bfloat16)
    grad_ref[:, 2 * HD :] = d_value[...].astype(jnp.bfloat16)


def attend_back(qkv, d_attended, segments, cosines, sines, heads):
    packs, length = segments.shape
    lanes = cosines.shape[1]
    part = lambda which: pl.BlockSpec((length, HD), lambda p, h: (p, h * 3 + which))
    table = pl.BlockSpec((length, lanes), lambda p, h: (0, 0))
    return pl.pallas_call(
        attend_back_kernel,
        grid=(packs, heads),
        in_specs=[
            part(0),
            part(1),
            part(2),
            pl.BlockSpec((length, HD), lambda p, h: (p, h)),
            pl.BlockSpec((1, 1, length), lambda p, h: (p, 0, 0)),
            pl.BlockSpec((1, length, 1), lambda p, h: (p, 0, 0)),
            table,
            table,
        ],
        out_specs=pl.BlockSpec((length, 3 * HD), lambda p, h: (p, h)),
        out_shape=jax.ShapeDtypeStruct((packs * length, 3 * heads * HD), jnp.bfloat16),
        scratch_shapes=[pltpu.VMEM((length, HD), jnp.float32)] * 2,
        compiler_params=kernel_params(),
        cost_estimate=pl.CostEstimate(
            flops=packs * heads * length * length * HD * 7, bytes_accessed=packs * length * heads * HD * 16, transcendentals=0
        ),
        name="attend_back",
    )(qkv, qkv, qkv, d_attended, segments[:, None, :], segments[:, :, None], cosines, sines)


def feed_kernel(
    offsets, owned, x_ref, attended_ref, blocks_ref, bias_ref, turned_ref, slope_ref, out_ref, act_ref, w_in, w_down, sems_in, sems_down
):
    size = blocks_ref.shape[-1]
    width, hidden_units = w_in.shape
    inner = hidden_units // size
    first_out, first_in, first_down = offsets
    head_rows = attended_ref.shape[1] // size
    outer = width // size
    copies_in = block_copies(blocks_ref, owned, first_in, outer, inner, w_in, sems_in)
    copies_down = block_copies(blocks_ref, owned, first_down, inner, outer, w_down.at[pl.ds(0, hidden_units)], sems_down)
    copies_down += block_copies(
        blocks_ref,
        owned,
        first_out,
        head_rows,
        outer,
        w_down.at[pl.ds(hidden_units, head_rows * size)],
        sems_down.at[pl.ds(inner * outer, head_rows * outer)],
    )
    begin_copies(copies_in + copies_down)
    end_copies(copies_in)
    values = x_ref[...]
    for col in range(inner):
        cols = pl.ds(col * size, size)
        hidden = contract(values, w_in[:, cols], NN) + bias_ref[:, cols]
        cdf = 0.5 + 0.5 * lax.erf(hidden * HALF_ROOT)
        density = jnp.exp(-0.5 * hidden * hidden) * DENSITY_SCALE
        activated = (hidden * cdf).astype(jnp.bfloat16)
        act_ref[:, cols] = activated
        turned_ref[cols, :] = activated.T
        slope_ref[:, cols] = (cdf + hidden * density).astype(jnp.bfloat16)
    end_copies(copies_down)
    for col in range(outer):
        cols = pl.ds(col * size, size)
        out_ref[:, cols] = (
            contract(act_ref[...], w_down[:hidden_units, cols], NN)
            + contract(attended_ref[...], w_down[hidden_units:, cols], NN)
        ).astype(jnp.bfloat16)


def feed_forward(normed, attended, blocks, owned, bias, offsets):
    tokens, width = normed.shape
    size = blocks.shape[-1]
    hidden_units = bias.shape[1]
    head_cols = attended.shape[1]
    tile = 512
    row = lambda cols: pl.BlockSpec((tile, cols), lambda i: (i, 0))
    inner, outer = hidden_units // size, width // size
    return pl.pallas_call(
        functools.partial(feed_kernel, offsets, owned),
        grid=(tokens // tile,),
        in_specs=[
            row(width),
            row(head_cols),
            pl.BlockSpec(memory_space=pl.ANY),
            pl.BlockSpec((1, hidden_units), lambda i: (0, 0)),
        ],
        out_specs=[
            pl.BlockSpec((hidden_units, tile), lambda i: (0, i)), row(hidden_units), row(width),
        ],
        out_shape=[
            jax.ShapeDtypeStruct((hidden_units, tokens), jnp.bfloat16),
            jax.ShapeDtypeStruct((tokens, hidden_units), jnp.bfloat16),
            jax.ShapeDtypeStruct((tokens, width), jnp.bfloat16),
        ],
        scratch_shapes=[
            pltpu.VMEM((tile, hidden_units), jnp.bfloat16),
            pltpu.VMEM((width, hidden_units), jnp.bfloat16),
            pltpu.VMEM((hidden_units + head_cols, width), jnp.bfloat16),
            pltpu.SemaphoreType.DMA((inner * outer,)),
            pltpu.SemaphoreType.DMA((inner * outer + head_cols // size * outer,)),
        ],
        compiler_params=kernel_params(),
        cost_estimate=pl.CostEstimate(
            flops=2 * tokens * width * (2 * hidden_units + head_cols), bytes_accessed=tokens * width * 10 + width * hidden_units * 4, transcendentals=0
        ),
        name="feed",
    )(normed, attended, blocks, bias)


def column_sum(values):
    rows, cols = values.shape
    return jnp.sum(values.reshape(rows // 8, 8, cols), axis=0)


def feed_back_kernel(offsets, owned, first_part, parts, held_count, rank_ref, *refs):
    part_refs = refs[:parts]
    factor_ref, slope_ref, tokens_ref, mean_ref, inverse_ref, blocks_ref, norm_ref = refs[parts : parts + 7]
    (
        seed_ref, d_attended_ref, d_hidden_ref, dz_ref, norm_sums, hidden_sums,
        w_in, w_down, w_out, held, sems_in, sems_down, sems_out, part_sems,
    ) = refs[parts + 7 + held_count :]
    size = blocks_ref.shape[-1]
    width, hidden_units = w_in.shape
    inner, outer = hidden_units // size, width // size
    first_out, first_in, first_down = offsets
    tile = seed_ref.shape[0]
    per_part = held.shape[1] // tile
    moves = part_copies(part_refs, held, part_sems)
    copies_out = block_copies(blocks_ref, owned, first_out, w_out.shape[0] // size, outer, w_out, sems_out)
    copies_down = block_copies(blocks_ref, owned, first_down, inner, outer, w_down, sems_down)
    copies_in = block_copies(blocks_ref, owned, first_in, outer, inner, w_in, sems_in)
    begin_copies(moves + copies_out + copies_down + copies_in)

    @pl.when(pl.program_id(0) == 0)
    def _():
        norm_sums[...] = jnp.zeros_like(norm_sums)
        hidden_sums[...] = jnp.zeros_like(hidden_sums)

    await_part(moves, per_part)
    step = pl.program_id(0)
    cotangent = held[step // per_part, pl.ds(pl.multiple_of(step % per_part * tile, tile), tile), :]
    seed_ref[...] = (cotangent.astype(jnp.float32) * factor_ref[...]).astype(jnp.bfloat16)
    seed = seed_ref[...]
    if first_part == 0:

        @pl.when(step < per_part)
        def _():
            norm_sums[16:24, :] += column_sum(seed_ref[...].astype(jnp.float32))

    end_copies(copies_out)
    d_attended_ref[...] = contract(seed, w_out[...], NT).astype(jnp.bfloat16)
    end_copies(copies_down)
    for col in range(inner):
        cols = pl.ds(col * size, size)
        d_act = contract(seed_ref[...], w_down[cols, :], NT)
        d_hidden = (d_act * slope_ref[:, cols].astype(jnp.float32)).astype(jnp.bfloat16)
        d_hidden_ref[:, cols] = d_hidden
        hidden_sums[:, cols] += column_sum(d_hidden.astype(jnp.float32))
    end_copies(copies_in)
    mean, inverse = mean_ref[...], inverse_ref[...]
    for col in range(outer):
        cols = pl.ds(col * size, size)
        scaled = (tokens_ref[:, cols].astype(jnp.float32) - mean) * inverse
        second = contract(d_hidden_ref[...], w_in[cols, :], NT)
        dz_ref[:, cols] = (second * norm_ref[2:3, cols]).astype(jnp.bfloat16)
        norm_sums[0:8, cols] += column_sum(second * scaled)
        norm_sums[8:16, cols] += column_sum(second)


def feed_back(parts, first_part, ways, rank, factor, slope, group_tokens, mean, inverse, blocks, owned, norm_params, offsets, head_cols, priors):
    chunk, width = parts[0].shape
    tokens = ways * chunk
    size = blocks.shape[-1]
    hidden_units = slope.shape[1]
    tile = min(FEED_BACK_TILE, chunk)
    per_part = chunk // tile
    inner, outer = hidden_units // size, width // size
    place = lambda i, rank: (rank[0] - first_part - i // per_part + ways) % ways * per_part + i % per_part
    row = lambda n: pl.BlockSpec((tile, n), lambda i, rank: (place(i, rank), 0))
    whole = lambda rows, cols: pl.BlockSpec((rows, cols), lambda i, rank: (0, 0))
    anywhere = pl.BlockSpec(memory_space=pl.ANY)
    count = len(parts)
    rows = count * chunk
    return pl.pallas_call(
        functools.partial(feed_back_kernel, offsets, owned, first_part, count, len(priors)),
        grid_spec=pltpu.PrefetchScalarGridSpec(
            num_scalar_prefetch=1,
            grid=(count * per_part,),
            in_specs=[anywhere] * count
            + [row(1), row(hidden_units), row(width), row(1), row(1), anywhere]
            + [whole(norm_params.shape[0], width)]
            + [anywhere] * len(priors),
            out_specs=[
                row(width), row(head_cols), row(hidden_units), row(width), whole(24, width), whole(8, hidden_units),
            ],
            scratch_shapes=[
                pltpu.VMEM((width, hidden_units), jnp.bfloat16),
                pltpu.VMEM((hidden_units, width), jnp.bfloat16),
                pltpu.VMEM((head_cols, width), jnp.bfloat16),
                pltpu.VMEM((count, chunk, width), jnp.bfloat16),
                pltpu.SemaphoreType.DMA((inner * outer,)),
                pltpu.SemaphoreType.DMA((inner * outer,)),
                pltpu.SemaphoreType.DMA((head_cols // size * outer,)),
                pltpu.SemaphoreType.DMA((count,)),
            ],
        ),
        out_shape=[
            jax.ShapeDtypeStruct((tokens, width), jnp.bfloat16),
            jax.ShapeDtypeStruct((tokens, head_cols), jnp.bfloat16),
            jax.ShapeDtypeStruct((tokens, hidden_units), jnp.bfloat16),
            jax.ShapeDtypeStruct((tokens, width), jnp.bfloat16),
            jax.ShapeDtypeStruct((24, width), jnp.float32),
            jax.ShapeDtypeStruct((8, hidden_units), jnp.float32),
        ],
        input_output_aliases={1 + count + 7 + index: index for index in range(len(priors))},
        compiler_params=kernel_params(),
        cost_estimate=pl.CostEstimate(
            flops=2 * rows * width * (2 * hidden_units + head_cols), bytes_accessed=rows * width * 14 + width * hidden_units * 4, transcendentals=0
        ),
        name="feed_back",
    )(rank, *parts, factor, slope, group_tokens, mean, inverse, blocks, norm_params, *priors)


def qkv_back_kernel(
    owned, waits, d_qkv_ref, part_ref, tokens_ref, mean_ref, inverse_ref, blocks_ref, norm_ref, *refs
):
    dz_ref, norm_sums, qkv_sums, w_qkv, sems = refs[waits:]
    size = blocks_ref.shape[-1]
    outer = w_qkv.shape[0] // size
    copies = block_copies(blocks_ref, owned, 0, outer, w_qkv.shape[1] // size, w_qkv, sems)
    begin_copies(copies)

    @pl.when(pl.program_id(0) == 0)
    def _():
        norm_sums[...] = jnp.zeros_like(norm_sums)
        qkv_sums[...] = jnp.zeros_like(qkv_sums)

    qkv_sums[...] += column_sum(d_qkv_ref[...].astype(jnp.float32))
    mean, inverse = mean_ref[...], inverse_ref[...]
    end_copies(copies)
    for col in range(outer):
        cols = pl.ds(col * size, size)
        scaled = (tokens_ref[:, cols].astype(jnp.float32) - mean) * inverse
        first = contract(d_qkv_ref[...], w_qkv[cols, :], NT)
        dz_ref[:, cols] = (part_ref[:, cols].astype(jnp.float32) + first * norm_ref[0:1, cols]).astype(jnp.bfloat16)
        norm_sums[0:8, cols] += column_sum(first * scaled)
        norm_sums[8:16, cols] += column_sum(first)


def qkv_back(d_qkv, dz_part, group_tokens, mean, inverse, blocks, owned, norm_params, waits):
    tokens, qkv_cols = d_qkv.shape
    width = dz_part.shape[1]
    size = blocks.shape[-1]
    tile = 512
    row = lambda cols: pl.BlockSpec((tile, cols), lambda i: (i, 0))
    whole = lambda rows, cols: pl.BlockSpec((rows, cols), lambda i: (0, 0))
    outer = width // size
    return pl.pallas_call(
        functools.partial(qkv_back_kernel, owned, len(waits)),
        grid=(tokens // tile,),
        in_specs=[
            row(qkv_cols), row(width), row(width), row(1), row(1), pl.BlockSpec(memory_space=pl.ANY), whole(norm_params.shape[0], width),
        ]
        + [pl.BlockSpec(memory_space=pl.ANY)] * len(waits),
        out_specs=[row(width), whole(16, width), whole(8, qkv_cols)],
        out_shape=[
            jax.ShapeDtypeStruct((tokens, width), jnp.bfloat16),
            jax.ShapeDtypeStruct((16, width), jnp.float32),
            jax.ShapeDtypeStruct((8, qkv_cols), jnp.float32),
        ],
        scratch_shapes=[
            pltpu.VMEM((width, qkv_cols), jnp.bfloat16),
            pltpu.SemaphoreType.DMA((outer * (qkv_cols // size),)),
        ],
        compiler_params=kernel_params(),
        cost_estimate=pl.CostEstimate(
            flops=2 * tokens * width * qkv_cols, bytes_accessed=tokens * width * 11, transcendentals=0
        ),
        name="qkv_back",
    )(d_qkv, dz_part, group_tokens, mean, inverse, blocks, norm_params, *waits)


def weight_grad_kernel(steps, waits, core_ref, *refs):
    lefts, rights, refs = refs[:4], refs[4:7], refs[7 + waits :]
    outs, rows_held, rights_held = refs[:2], refs[2], refs[3:6]
    results, left_sems, right_sems, sems = refs[6:]
    size = results.shape[-1]
    core = core_ref[0]
    depth = rows_held.shape[0]

    def left_copy(index):
        left, first, rows, _, _, _ = steps[index]
        return pltpu.make_async_copy(
            lefts[left].at[pl.ds(first, rows), :],
            rows_held.at[index % depth, pl.ds(0, rows), :],
            left_sems.at[index % depth],
        )

    def right_copy(right, first):
        held = rights_held[right]
        return pltpu.make_async_copy(
            rights[right].at[:, pl.ds(first, held.shape[1])], held, right_sems.at[right]
        )

    def finish(index):
        for place in range(len(steps[index][5])):
            pltpu.make_async_copy(
                results.at[index % 2, place], outs[0].at[0], sems.at[index % 2, place]
            ).wait()

    order = []
    for step in steps:
        if step[3:5] not in order:
            order.append(step[3:5])
    right_copy(*order[0]).start()
    for index in range(min(depth - 1, len(steps))):
        left_copy(index).start()
    for right in order[1:]:
        right_copy(*right).start()
    for index, (left, first, rows, right, right_first, places) in enumerate(steps):
        left_copy(index).wait()
        if index + depth - 1 < len(steps):
            left_copy(index + depth - 1).start()
        if all(step[3:5] != (right, right_first) for step in steps[:index]):
            right_copy(right, right_first).wait()
        if index >= 2:
            finish(index - 2)
        held = rights_held[right]
        cols = held.shape[1] // size
        for col in range(cols):
            result = contract(rows_held[index % depth, :rows, :], held[:, col * size : (col + 1) * size], NN)
            for row in range(rows // size):
                results[index % 2, row * cols + col] = result[row * size : (row + 1) * size].astype(jnp.bfloat16)
        for number, (owner, place) in enumerate(places):
            for away in range(2):

                @pl.when((core == owner % 2) == (away == 0))
                def _():
                    pltpu.make_async_copy(
                        results.at[index % 2, number], outs[away].at[place], sems.at[index % 2, number]
                    ).start()

    for index in range(max(0, len(steps) - 2), len(steps)):
        finish(index)


def weight_grads(part, parts, lefts, rights, firsts, core, owned, dp_ways, size, waits):
    first_normed, second_normed, activated, attended = lefts
    d_hidden, seed, d_qkv = rights
    tokens = d_qkv.shape[0]
    width = seed.shape[1]
    part_size = owned // parts
    qkv_blocks = d_qkv.shape[1] // size
    per_row = width // size
    span = per_row // parts
    steps = []
    for left, right, first, rows_all in (
        (1, 0, firsts[2], second_normed.shape[0]),
        (2, 1, firsts[3], activated.shape[0]),
        (3, 1, firsts[1], attended.shape[0]),
    ):
        rows = min(512, rows_all)
        for begin in range(0, rows_all, rows):
            places = []
            for row in range(begin // size, (begin + rows) // size):
                for col in range(span):
                    block = first + row * per_row + part * span + col
                    owner, within = block // owned, block % owned
                    places.append((owner, owner // 2 * part_size + within // per_row * span + col))
            steps.append((left, begin, rows, right, part * span * size, tuple(places)))
    for owner in range(per_row // parts):
        row = owner * parts + part
        places = [(owner, owner // 2 * part_size + col) for col in range(qkv_blocks)]
        steps.append((0, row * size, size, 2, 0, tuple(places)))
    most = max(len(step[5]) for step in steps)
    anywhere = pl.BlockSpec(memory_space=pl.ANY)
    half = jax.ShapeDtypeStruct((dp_ways // 2 * part_size, size, size), jnp.bfloat16)
    flops = 2 * tokens * size * size * dp_ways * part_size
    return pl.pallas_call(
        functools.partial(weight_grad_kernel, tuple(steps), len(waits)),
        in_specs=[pl.BlockSpec(memory_space=pltpu.SMEM)] + [anywhere] * (7 + len(waits)),
        out_specs=[anywhere] * 2,
        out_shape=[half] * 2,
        scratch_shapes=[
            pltpu.VMEM((4, max(step[2] for step in steps), tokens), jnp.bfloat16),
            pltpu.VMEM((tokens, span * size), jnp.bfloat16),
            pltpu.VMEM((tokens, span * size), jnp.bfloat16),
            pltpu.VMEM((tokens, d_qkv.shape[1]), jnp.bfloat16),
            pltpu.VMEM((2, most, size, size), jnp.bfloat16),
            pltpu.SemaphoreType.DMA((4,)),
            pltpu.SemaphoreType.DMA((3,)),
            pltpu.SemaphoreType.DMA((2, most)),
        ],
        compiler_params=kernel_params(),
        cost_estimate=pl.CostEstimate(flops=flops, bytes_accessed=flops // 500, transcendentals=0),
        name="weight_grads",
    )(core, *lefts, *rights, *waits)


def pair_sum_kernel(chip_ref, *refs):
    chips = len(refs) // 3
    for index in range(chips):
        total = refs[index][...].astype(jnp.float32) + refs[chips + index][...].astype(jnp.float32)
        refs[2 * chips + index][...] = total.astype(refs[2 * chips + index].dtype)


def pair_sum(kept, received, chip, chips):
    rows, size, _ = kept.shape
    part = rows // chips
    tile = next(each for each in (3, 2, 1) if part % each == 0)
    pieces = part // tile
    spec = lambda away: pl.BlockSpec(
        (tile, size, size), lambda i, chip: (jnp.bitwise_xor(chip[0], away) * pieces + i, 0, 0)
    )
    plain = pl.BlockSpec((tile, size, size), lambda i, chip: (i, 0, 0))
    dtypes = [jnp.float32] + [jnp.bfloat16] * (chips - 1)
    return pl.pallas_call(
        pair_sum_kernel,
        grid_spec=pltpu.PrefetchScalarGridSpec(
            num_scalar_prefetch=1,
            grid=(pieces,),
            in_specs=[spec(away) for away in range(chips)] * 2,
            out_specs=[plain] * chips,
        ),
        out_shape=[jax.ShapeDtypeStruct((part, size, size), dtype) for dtype in dtypes],
        compiler_params=kernel_params(),
        cost_estimate=pl.CostEstimate(flops=rows * size * size, bytes_accessed=rows * size * size * 6, transcendentals=0),
        name="pair_sum",
    )(chip, *([kept] * chips), *([received] * chips))


def input_grad_kernel(moved_ref, last_ref, tokens_ref, seed_ref, mean_ref, inverse_ref, out_ref):
    d_scaled = moved_ref[...].astype(jnp.float32) + last_ref[...].astype(jnp.float32)
    inverse = inverse_ref[...]
    scaled = (tokens_ref[...].astype(jnp.float32) - mean_ref[...]) * inverse
    average = jnp.mean(d_scaled, axis=1, keepdims=True)
    projection = jnp.mean(d_scaled * scaled, axis=1, keepdims=True)
    out_ref[...] = seed_ref[...].astype(jnp.float32) + inverse * (d_scaled - average - scaled * projection)


def input_gradient(moved, dz, tokens, seed, mean, inverse, rank, waits):
    rows, width = moved.shape
    tile = min(128, rows)
    per = rows // tile
    own = lambda n: pl.BlockSpec((tile, n), lambda i, rank: (i, 0))
    ranked = lambda n: pl.BlockSpec((tile, n), lambda i, rank: (rank[0] * per + i, 0))

    def kernel(rank_ref, *refs):
        input_grad_kernel(*refs[:6], refs[-1])

    return pl.pallas_call(
        kernel,
        grid_spec=pltpu.PrefetchScalarGridSpec(
            num_scalar_prefetch=1,
            grid=(per,),
            in_specs=[own(width), ranked(width), own(width), ranked(width), ranked(1), ranked(1)]
            + [pl.BlockSpec(memory_space=pl.ANY)] * len(waits),
            out_specs=own(width),
        ),
        out_shape=jax.ShapeDtypeStruct((rows, width), jnp.float32),
        compiler_params=kernel_params(),
        cost_estimate=pl.CostEstimate(flops=rows * width * 12, bytes_accessed=rows * width * 12, transcendentals=0),
        name="input_gradient",
    )(rank, moved, dz, tokens, seed, mean, inverse, *waits)


def dot32(left_arg, right_arg):
    return jnp.dot(left_arg, right_arg, preferred_element_type=jnp.float32)


def two_terms(values):
    high = values.astype(jnp.bfloat16)
    return high, (values - high.astype(jnp.float32)).astype(jnp.bfloat16)


def shampoo_kernel(count, terms, held, places_ref, *refs):
    grads, refs = refs[:terms], refs[terms:]
    left_refs, right_refs, master_refs = (refs[side * count : (side + 1) * count] for side in range(3))
    outs, refs = refs[3 * count + held : 3 * count + held + 4], refs[3 * count + held + 4 :]
    results, scaled, roots, pairs, powers, high, low, sems = refs
    size = results.shape[-1]
    step, steps = pl.program_id(0), pl.num_programs(0)
    slot = lax.rem(step, 2)
    chains = range(2 * count)
    stat_refs = (left_refs, right_refs)
    identity = (
        lax.broadcasted_iota(jnp.int32, (size, size), 0)
        == lax.broadcasted_iota(jnp.int32, (size, size), 1)
    ).astype(jnp.float32)

    def copies(of_step, of_slot):
        return [
            pltpu.make_async_copy(
                results.at[of_slot, kind, block],
                outs[kind].at[places_ref[of_step * count + block]],
                sems.at[of_slot, kind, block],
            )
            for kind in range(4)
            for block in range(count)
        ]

    @pl.when(step >= 2)
    def _():
        for copy in copies(step - 2, slot):
            copy.wait()

    grad16 = []
    for block in range(count):
        total = grads[0][block].astype(jnp.float32)
        for grad in grads[1:]:
            total = total + grad[block].astype(jnp.float32)
        results[slot, 0, block] = total
        grad16.append(total.astype(jnp.bfloat16))
    for item in chains:
        block, side = item // 2, item % 2
        dims = (((1 - side,), (1 - side,)), ((), ()))
        results[slot, 1 + side, block] = DECAY * stat_refs[side][block][0] + lax.dot_general(
            grad16[block], grad16[block], dims, preferred_element_type=jnp.float32
        )
    sums = []
    for item in chains:
        stat = results[slot, 1 + item % 2, item // 2]
        sums.append(jnp.sum(stat * stat, axis=0, keepdims=True))
    norms = [jnp.sqrt(jnp.sum(each, axis=1, keepdims=True)) for each in sums]
    for item in chains:
        scaled[item] = results[slot, 1 + item % 2, item // 2] * (1.0 / norms[item])
    factors = [lax.rsqrt(jnp.sqrt(norm)) for norm in norms]

    for repeat in range(ROOT_ITERS - 1):
        for item in chains:
            quarter = (identity - scaled[item]) * 0.25
            pairs[item, size:] = quarter.astype(jnp.bfloat16)
            if repeat == 0:
                roots[item] = identity + quarter
            else:
                pairs[item, :size] = roots[item].astype(jnp.bfloat16)
        if repeat == 0:
            squares = [dot32(pairs[item, size:], pairs[item, size:]) for item in chains]
        else:
            both = [dot32(pairs[item], pairs[item, size:]) for item in chains]
            for item in chains:
                roots[item] = roots[item] + both[item][:size]
            squares = [each[size:] for each in both]
        seconds = [(identity - scaled[item]) * 0.5 + squares[item] for item in chains]
        seconds16 = [second.astype(jnp.bfloat16) for second in seconds]
        fourths = [2.0 * seconds[item] + dot32(seconds16[item], seconds16[item]) for item in chains]
        for item in chains:
            high[item], low[item] = two_terms(scaled[item])
            powers[item, :size], powers[item, size:] = two_terms(fourths[item])
        for item in chains:
            both_terms = dot32(powers[item], high[item])
            scaled[item] = scaled[item] + (
                both_terms[:size] + both_terms[size:] + dot32(powers[item, :size], low[item])
            )
    for item in chains:
        pairs[item, size:] = ((identity - scaled[item]) * 0.25).astype(jnp.bfloat16)
        pairs[item, :size] = roots[item].astype(jnp.bfloat16)
    for item in chains:
        ends = two_terms(roots[item] + dot32(pairs[item, :size], pairs[item, size:]))
        if item % 2 == 0:
            powers[item, :size], powers[item, size:] = ends
        else:
            high[item], low[item] = ends
    halves = []
    for block in range(count):
        both_terms = dot32(powers[2 * block], grad16[block])
        halves.append(both_terms[:size] + both_terms[size:])
    for block in range(count):
        pairs[block, :size], pairs[block, size:] = two_terms(halves[block])
    for block in range(count):
        item = 2 * block + 1
        both_terms = dot32(pairs[block], high[item])
        product = both_terms[:size] + both_terms[size:] + dot32(pairs[block, :size], low[item])
        rate = RATE_BLOCK * factors[2 * block] * factors[item]
        results[slot, 3, block] = master_refs[block][0] - rate * product
    for copy in copies(step, slot):
        copy.start()

    @pl.when(step == steps - 1)
    def _():
        @pl.when(steps >= 2)
        def _():
            for copy in copies(step - 1, 1 - slot):
                copy.wait()

        for copy in copies(step, slot):
            copy.wait()


def shampoo(grads, left_stats, right_stats, master_blocks, places, priors, waits=()):
    part, size, _ = grads[0].shape
    count = next(each for each in (3, 2, 1) if part % each == 0)
    own = pl.BlockSpec((count, size, size), lambda step, places: (step, 0, 0))
    anywhere = pl.BlockSpec(memory_space=pl.ANY)

    def single(block):
        return pl.BlockSpec((1, size, size), lambda step, places: (places[step * count + block], 0, 0))

    result = jax.ShapeDtypeStruct(left_stats.shape, jnp.float32)
    held = len(priors)
    first_prior = 1 + len(grads) + 3 * count
    wide = pltpu.VMEM((2 * count, 2 * size, size), jnp.bfloat16)
    plain = pltpu.VMEM((2 * count, size, size), jnp.bfloat16)
    return pl.pallas_call(
        functools.partial(shampoo_kernel, count, len(grads), held + len(waits)),
        grid_spec=pltpu.PrefetchScalarGridSpec(
            num_scalar_prefetch=1,
            grid=(part // count,),
            in_specs=[own] * len(grads)
            + [single(block) for block in range(count)] * 3
            + [anywhere] * (held + len(waits)),
            out_specs=[anywhere] * 4,
            scratch_shapes=[
                pltpu.VMEM((2, 4, count, size, size), jnp.float32),
                pltpu.VMEM((2 * count, size, size), jnp.float32),
                pltpu.VMEM((2 * count, size, size), jnp.float32),
                wide,
                wide,
                plain,
                plain,
                pltpu.SemaphoreType.DMA((2, 4, count)),
            ],
        ),
        out_shape=[result] * 4,
        input_output_aliases={first_prior + index: index for index in range(held)},
        compiler_params=kernel_params(),
        cost_estimate=pl.CostEstimate(
            flops=part * 130 * 2 * size**3, bytes_accessed=part * size * size * 30, transcendentals=0
        ),
        name="shampoo",
    )(
        places,
        *grads,
        *([left_stats] * count),
        *([right_stats] * count),
        *([master_blocks] * count),
        *priors,
        *waits,
    )


def after(value, *earlier):
    return lax.optimization_barrier((value,) + earlier)[0]


def onward(part, axis):
    ways = lax.axis_size(axis)
    return lax.ppermute(part, axis, [(each, (each + 1) % ways) for each in range(ways)])


def swap(part, bits):
    ways = lax.axis_size("dp")
    return lax.ppermute(part, "dp", [(each, each ^ bits) for each in range(ways)])


def small_rows(values, ways):
    return jnp.pad(values, ((0, 0), (0, -values.shape[1] % 2048))).reshape(-1, 128)


def shards(
    tokens,
    cotangent,
    segments,
    subsets,
    packs,
    master_blocks,
    left_stats,
    right_stats,
    local_vecs,
    local_vec_stats,
    shared_vecs,
    shared_vec_stats,
):
    tp_ways = lax.axis_size("tp")
    dp_ways = lax.axis_size("dp")
    tp_rank = lax.axis_index("tp")
    tok_dev, model_width = tokens.shape
    group_tok = tok_dev * tp_ways
    pack_count, pack_len = segments.shape
    seg_width = subsets.shape[1]
    heads_dev = HEADS // tp_ways
    ff_dev = FF // tp_ways
    head_cols = heads_dev * HD
    owned, block_size, _ = master_blocks.shape
    block_rows = model_width // block_size
    first_out = block_rows * (3 * head_cols // block_size)
    first_in = first_out + head_cols // block_size * block_rows
    first_down = first_in + block_rows * (ff_dev // block_size)
    all_count = owned * dp_ways
    vec_rows = 3 * heads_dev + ff_dev // HD

    vec_used = local_vecs.size
    shared_used = shared_vecs.size
    vec_flat = jnp.concatenate([local_vecs.reshape(-1), shared_vecs.reshape(-1)])
    extra = jnp.pad(vec_flat, (0, EXTRA_ROWS * block_size - vec_flat.size)).reshape(EXTRA_ROWS, block_size)
    rows16 = jnp.concatenate([master_blocks.reshape(-1, block_size), extra], 0).astype(jnp.bfloat16)
    blocks = lax.all_gather(rows16, "dp", axis=0, tiled=True)

    token_parts = [tokens]
    for step in range(1, tp_ways):
        token_parts.append(onward(token_parts[-1], "tp"))

    gathered = blocks.reshape(dp_ways, -1, block_size)[:, owned * block_size :].reshape(dp_ways, -1)
    vec_values = (
        gathered[:, :vec_used].reshape(dp_ways, vec_rows, -1).transpose(1, 0, 2).reshape(vec_rows, HD)
    ).astype(jnp.float32)
    shared_mine = gathered[:, vec_used : vec_used + shared_used]
    shared_all = jnp.zeros((tp_ways,) + shared_mine.shape, jnp.bfloat16)
    for step in range(tp_ways):
        part = shared_mine
        if step:
            part = lax.ppermute(
                part, "tp", [(each, (each + step) % tp_ways) for each in range(tp_ways)]
            )
        shared_all = lax.dynamic_update_slice(
            shared_all, part[None], ((tp_rank - step) % tp_ways, 0, 0)
        )
    norm_params = (
        shared_all.reshape(tp_ways, dp_ways, 6, -1).transpose(2, 1, 0, 3).reshape(6, model_width)
    ).astype(jnp.float32)
    bias_qkv = vec_values[: 3 * heads_dev].reshape(1, -1)
    bias_in = vec_values[3 * heads_dev :].reshape(1, -1)

    own_pos = tp_rank * tok_dev + jnp.arange(tok_dev)
    own_pack = own_pos // pack_len
    valid_own = (own_pack < packs[0]).astype(jnp.float32)
    owned_input_rows = tokens.astype(jnp.float32)

    group_pack = jnp.arange(group_tok) // pack_len
    lookup_key = group_pack * seg_width + segments.reshape(-1)
    onehot = lookup_key[:, None] == jnp.arange(pack_count * seg_width)[None, :]
    subset_tok = jnp.sum(jnp.where(onehot, subsets.reshape(-1)[None, :], 0), axis=1)
    weight = 0.5 + subset_tok.astype(jnp.float32) / (SUBSETS - 1)
    factor = (weight * (group_pack < packs[0]).astype(jnp.float32))[:, None]

    rank = tp_rank.astype(jnp.int32)[None]
    cosines, sines = turn_tables(pack_len, 128)
    cotangent_parts = [cotangent, onward(after(cotangent, token_parts[-1], shared_all), "tp")]
    qkv16, first_turned, second_normed, second_turned, group_tokens, mean, inverse = project_qkv(
        token_parts, rank, blocks, owned, norm_params, bias_qkv, cosines, sines, heads_dev
    )
    attended, attended_turned = attend(qkv16, segments, heads_dev)
    cotangent_parts.append(onward(after(cotangent_parts[-1], attended), "tp"))
    active_turned, slope, partial_value = feed_forward(
        second_normed, attended, blocks, owned, bias_in, (first_out, first_in, first_down)
    )
    while len(cotangent_parts) < tp_ways:
        cotangent_parts.append(onward(after(cotangent_parts[-1], slope), "tp"))

    back_args = (
        tp_ways, rank, factor, slope, group_tokens, mean, inverse, blocks, owned, norm_params,
        (first_out, first_in, first_down), head_cols,
    )
    early = feed_back(cotangent_parts[:-1], 0, *back_args, ())
    late = feed_back(cotangent_parts[-1:], tp_ways - 1, *back_args, early[:4])
    seed_all, d_attended, d_hidden16, dz_part = late[:4]
    branch = lax.psum_scatter(
        after(partial_value, cotangent_parts[-1], early[5]), "tp", scatter_dimension=0, tiled=True
    )
    d_qkv16 = attend_back(qkv16, d_attended, segments, cosines, sines, heads_dev)
    dp_rank = lax.axis_index("dp").astype(jnp.int32)
    lefts = (first_turned, second_turned, active_turned, attended_turned)
    rights = (d_hidden16, seed_all, d_qkv16)
    firsts = (0, first_out, first_in, first_down)
    qkv_blocks = 3 * head_cols // block_size
    parts = 4
    by_part = (
        dp_ways == 8
        and owned == parts * qkv_blocks
        and block_rows == 2 * parts
        and ff_dev == model_width
        and owned % block_rows == 0
        and first_out % block_rows == 0
        and first_in % block_rows == 0
    )
    sums = []

    def quarter(part, waits):
        kept, away = weight_grads(
            part, parts, lefts, rights, firsts, (dp_rank % 2)[None], owned, dp_ways, block_size, waits
        )
        sums.append(pair_sum(kept, swap(away, 1), (dp_rank // 2)[None], dp_ways // 2))
        return kept

    first_waits = ()
    if by_part:
        quarter(0, ())
        quarter(1, ())
        first_waits = (sums[0][0],)
    dz16, first_sums, qkv_sums = qkv_back(
        d_qkv16, dz_part, group_tokens, mean, inverse, blocks, owned, norm_params, first_waits
    )
    dz_rows = lambda back: lax.dynamic_slice_in_dim(dz16, (tp_rank - back) % tp_ways * tok_dev, tok_dev, 0)
    back = 2

    def pass_on(moving, back):
        total = moving.astype(jnp.float32) + dz_rows(back).astype(jnp.float32)
        return total.astype(jnp.bfloat16)

    moving = onward(dz_rows(1), "tp")
    shared_local = jnp.concatenate(
        [
            jnp.sum(first_sums.reshape(2, 8, model_width), axis=1),
            jnp.sum((early[4][:16] + late[4][:16]).reshape(2, 8, model_width), axis=1),
            jnp.sum(early[4][16:], axis=0)[None],
        ],
        0,
    )
    vecs_local = jnp.concatenate(
        [
            jnp.sum(qkv_sums, axis=0).reshape(3 * heads_dev, HD),
            jnp.sum(early[5] + late[5], axis=0).reshape(ff_dev // HD, HD),
        ],
        0,
    )
    small = jnp.concatenate(
        [
            shared_local.reshape(5, dp_ways, -1).transpose(1, 0, 2).reshape(dp_ways, -1),
            vecs_local.reshape(vec_rows, dp_ways, -1).transpose(1, 0, 2).reshape(dp_ways, -1),
        ],
        1,
    )
    small_in = after(small_rows(small, dp_ways), branch)
    small_own = lax.psum_scatter(small_in, "dp", scatter_dimension=0, tiled=True).reshape(-1)
    output = (
        valid_own[:, None]
        * (owned_input_rows + branch.astype(jnp.float32) + norm_params[4] + norm_params[5])
    ).astype(jnp.bfloat16)

    shared_size = 5 * model_width // dp_ways
    own_vec_grads = small_own[shared_size : small.shape[1]].reshape(vec_rows, HD // dp_ways)
    shared_part = small_own[:shared_size].reshape(5, tp_ways, -1).transpose(1, 0, 2)
    shared_in = small_rows(shared_part.reshape(tp_ways, -1), tp_ways)
    shared_own = lax.psum_scatter(shared_in, "tp", scatter_dimension=0, tiled=True).reshape(-1)
    shared_own = shared_own[: shared_size // tp_ways].reshape(5, -1)
    shared_grads = jnp.concatenate([shared_own, shared_own[4:]], 0)
    results = ()
    if by_part:
        part_size = owned // parts
        span = block_rows // parts
        terms = []
        ready = []

        def send_on(part):
            if part:
                sums[part] = [sums[part][0]] + [after(each, terms[-1][3]) for each in sums[part][1:]]
                ready.append(sums[part][3])
            terms.append([sums[part][0]] + [swap(sums[part][bits], 2 * bits) for bits in range(1, 4)])

        send_on(0)
        quarter(2, (dz16, sums[1][0]) + tuple(terms[0][1:]))
        quarter(3, tuple(terms[0][1:]))
        for part in range(1, parts):
            send_on(part)
        count = jnp.arange(part_size, dtype=jnp.int32)
        in_qkv = dp_rank * owned < first_out
        for part in range(parts):
            places = jnp.where(
                in_qkv,
                part * part_size + count,
                count // span * block_rows + part * span + count % span,
            )
            waits = []
            if part < parts - 1:
                waits.append(ready[part])
            if part == 0:
                waits += terms[1][1:]
            if part % 2 == 0 and back < tp_ways:
                if part:
                    moving, first_result = lax.optimization_barrier((moving, results[0]))
                    results = [first_result] + list(results[1:])
                total = pass_on(moving, back)
                waits.append(total)
                moving = onward(total, "tp")
                back += 1
            if part == 1:
                waits.append(small_in)
            if part == 2:
                waits += [small_own, shared_in]
            if part == 3:
                waits += [output, shared_own]
            results = shampoo(
                terms[part], left_stats, right_stats, master_blocks, places, results, waits
            )
    else:
        local = [
            to_blocks(jnp.dot(left, right, preferred_element_type=jnp.float32).astype(jnp.bfloat16), block_size)
            for left, right in (
                (first_turned, d_qkv16),
                (attended_turned, seed_all),
                (second_turned, d_hidden16),
                (active_turned, seed_all),
            )
        ]
        grads16 = lax.psum_scatter(jnp.concatenate(local, 0), "dp", scatter_dimension=0, tiled=True)
        results = shampoo(
            [grads16], left_stats, right_stats, master_blocks, jnp.arange(owned, dtype=jnp.int32), results
        )
    while back < tp_ways:
        moving = onward(pass_on(moving, back), "tp")
        back += 1
    input_grad = input_gradient(moving, dz16, tokens, seed_all, mean, inverse, rank, results[:1])
    own_grads, left_new, right_new, new_blocks = results
    local_stat_new = DECAY * local_vec_stats + own_vec_grads * own_vec_grads
    local_new = local_vecs - RATE_VEC * own_vec_grads * lax.rsqrt(local_stat_new)
    shared_stat_new = DECAY * shared_vec_stats + shared_grads * shared_grads
    shared_new = shared_vecs - RATE_VEC * shared_grads * lax.rsqrt(shared_stat_new)
    return (
        output,
        input_grad,
        own_grads,
        left_new,
        right_new,
        new_blocks,
        own_vec_grads,
        local_stat_new,
        local_new,
        shared_grads,
        shared_stat_new,
        shared_new,
    )


def solution(mesh):
    placed = (
        P(("dp", "tp"), None),
        P(("dp", "tp"), None),
        P("dp", None),
        P("dp", None),
        P("dp"),
        P(("dp", "tp"), None, None),
        P(("dp", "tp"), None, None),
        P(("dp", "tp"), None, None),
        P("tp", "dp"),
        P("tp", "dp"),
        P(None, ("dp", "tp")),
        P(None, ("dp", "tp")),
    )
    return jax.shard_map(
        shards,
        mesh=mesh,
        in_specs=placed,
        out_specs=(
            P(("dp", "tp"), None),
            P(("dp", "tp"), None),
            P(("dp", "tp"), None, None),
            P(("dp", "tp"), None, None),
            P(("dp", "tp"), None, None),
            P(("dp", "tp"), None, None),
            P("tp", "dp"),
            P("tp", "dp"),
            P("tp", "dp"),
            P(None, ("dp", "tp")),
            P(None, ("dp", "tp")),
            P(None, ("dp", "tp")),
        ),
        check_vma=False,
    )
```
